128 devices in a mesh: slab: 16 (over y, x_lo, core), brick: 8 (over x_hi, z).
Axes of the slice: x: 4 (x_hi: 2, x_lo: 2; x = x_hi * 2 + x_lo), y: 4, z: 4, core: 2. Of those that a mesh axis runs over, the one named last changes fastest.
Arguments:
- fluid_velocity: float32 [3, 128, 256, 512], P(None, ('slab', 'brick')), may hold values from -6 to 6
- porosity: float32 [128, 256, 512], P(('slab', 'brick')), may hold values from 0.4 to 0.95
- particle_velocity: float32 [3, 2097152], P(None, ('slab', 'brick')), may hold values from -6 to 6
- drag_coef: float32 [2097152], P(('slab', 'brick')), may hold values from 0.2 to 2
- send_rows: int32 [4194304], P(('slab', 'brick')), may hold values from 0 to 16383, as said below
- counts: int32 [16384], P(('slab', 'brick')), may hold values from 0 to 256, as said below
- recv_cell: int32 [4194304], P(('slab', 'brick')), may hold values from 0 to 131071
Outputs:
- new_velocity: float32 [3, 128, 256, 512], P(None, ('slab', 'brick'))
- slot_force: float32 [3, 4194304], P(None, ('slab', 'brick'))
The draws below stay inside these ranges and needn't reach their ends.
Inputs may be any that keep to these rules, and one draw needn't show every extreme that they name: One entry equals 256 in every draw; loads differ strongly between destinations; each source's counts sum to at most 16384. `send_rows`: over all destinations of one source, the live slots name distinct particles: each particle is sent to at most one brick owner.
All inputs are finite; a program needn't handle non-finite values.
Results may differ from the reference program's by a relative error of at most 0.00002.
Values sent between devices are 32-bit elements; how exact they have to be, the bound alone decides.
A program may use at most 192 MiB of HBM per device.

```python
import math
import jax
import jax.numpy as jnp

NX = 256
NY = 512
P_DEV = 16384
CAP = 256
NDEV = 128
NZ = 128
ZB = 8
XB = 32
BCELLS = 131072
PARTS_ALL = 2097152
SLOTS = 4194304
N_BRICK = 8


def shared_counts(key):
    inner = jax.random.fold_in(key, 101)
    first, second, third = jax.random.split(inner, 3)
    heat = jax.random.randint(first, (NDEV,), 0, 4)
    upper = CAP * jnp.left_shift(jnp.int32(1), heat) // 4 + 1
    raw = jax.random.randint(second, (NDEV, NDEV), 0, 1 << 30) % upper[None, :]
    raw = jnp.minimum(raw, CAP)
    target = P_DEV - CAP
    row_total = jnp.sum(raw, axis=1, keepdims=True)
    scaled = raw * target // jnp.maximum(row_total, target)
    chosen = jax.random.randint(third, (), 0, NDEV * NDEV)
    return scaled.reshape(-1).at[chosen].set(CAP).reshape(NDEV, NDEV).astype(jnp.int32)


def draw_counts(key, part):
    return shared_counts(key).reshape(-1)


def draw_send_rows(key, part):
    filled = shared_counts(key)
    key = jax.random.fold_in(key, 13)
    keys = jax.random.split(key, NDEV)
    orders = jax.vmap(lambda k: jax.random.permutation(k, P_DEV))(keys).astype(jnp.int32)
    offsets = jnp.cumsum(filled, axis=1) - filled
    position = (offsets[:, :, None] + jnp.arange(CAP, dtype=jnp.int32)[None, None, :]) % P_DEV
    source = jnp.arange(NDEV, dtype=jnp.int32)[:, None, None]
    return orders[source, position].reshape(-1).astype(jnp.int32)


def set_ends(entries, rng, low, top_value):
    longest = entries.shape.index(max(entries.shape))
    spots = []
    for shift in (0, 1):
        where = [jax.random.randint(jax.random.fold_in(rng, axis), (), 0, length) for axis, length in enumerate(entries.shape)]
        where[longest] = (where[longest] + shift) % entries.shape[longest]
        spots.append(tuple(where))
    return entries.at[spots[0]].set(low).at[spots[1]].set(top_value)


def block_scale(rng, dims, cuts, low, largest):
    gain, own = 1.0, jax.random.fold_in(rng, 6)
    for dim, parts in cuts:
        steps = jnp.exp(jax.random.uniform(jax.random.fold_in(own, dim), (parts,), jnp.float32, low / len(cuts), largest / len(cuts)))
        gain = gain * jnp.repeat(steps, dims[dim] // parts).reshape([-1 if axis == dim else 1 for axis in range(len(dims))])
    return gain


def centred(rng, shape, width, limit, cuts=(), kind=jnp.bfloat16):
    factor_of = block_scale(rng, shape, cuts, -0.22, 0.18) if cuts else 1.0
    array = jax.random.normal(rng, shape, jnp.float32) * width * factor_of
    return jnp.minimum(jnp.maximum(array, -limit), limit).astype(kind)


def setup_inputs(seed: int = 0) -> dict:
    splits = jax.random.split(jax.random.key(seed), 8)
    return {
        "fluid_velocity": centred(splits[0], (3, NZ, NX, NY), 1.0, 6.0, ((1, 128),), jnp.float32),
        "porosity": jnp.clip(0.4 + 0.54999998 * jax.random.uniform(splits[1], (NZ, NX, NY), jnp.float32) ** block_scale(splits[1], (NZ, NX, NY), ((0, 128),), -0.2, 0.2), 0.4, 0.95),
        "particle_velocity": centred(splits[2], (3, PARTS_ALL), 1.0, 6.0, ((1, 128),), jnp.float32),
        "drag_coef": jnp.clip(jnp.exp(math.log(2.0) - 2.3025851 * jax.random.uniform(splits[3], (PARTS_ALL,), jnp.float32) ** block_scale(splits[3], (PARTS_ALL,), ((0, 128),), -0.2, 0.2)), 0.2, 2.0),
        "send_rows": draw_send_rows(jax.random.fold_in(splits[7], 71), 0),
        "counts": draw_counts(jax.random.fold_in(splits[7], 71), 0),
        "recv_cell": set_ends(jax.random.randint(splits[6], (SLOTS,), 0, BCELLS), jax.random.fold_in(splits[6], 1), 0, BCELLS - 1).astype(jnp.int32),
    }


time_step = 0.05


def neighbours(padded):
    return [padded[:, 2:, 1:-1, 1:-1], padded[:, :-2, 1:-1, 1:-1],
            padded[:, 1:-1, 2:, 1:-1], padded[:, 1:-1, :-2, 1:-1],
            padded[:, 1:-1, 1:-1, 2:], padded[:, 1:-1, 1:-1, :-2]]


def viscous_sum(padded):
    centre = padded[:, 1:-1, 1:-1, 1:-1]
    total = jnp.zeros_like(centre[:3])
    for beside in neighbours(padded):
        weight = 0.5 * (centre[3] + beside[3])
        total = total + weight * (beside[:3] - centre[:3])
    return total


def reference(fluid_velocity, porosity, particle_velocity, drag_coef, send_rows, counts, recv_cell):
    stacked = jnp.concatenate([fluid_velocity, porosity[None]], 0)
    padded = jnp.pad(stacked, ((0, 0), (1, 1), (1, 1), (1, 1)))
    viscous = viscous_sum(padded)
    devices = jnp.arange(NDEV, dtype=jnp.int32)
    sender_rows = send_rows.reshape(NDEV, NDEV, CAP) + devices[:, None, None] * P_DEV
    global_rows = jnp.transpose(sender_rows, (1, 0, 2))
    slot_index = jnp.arange(CAP, dtype=jnp.int32)
    slot_live = slot_index[None, None, :] < counts.reshape(NDEV, NDEV)[:, :, None]
    slot_live = jnp.transpose(slot_live, (1, 0, 2))
    part_moving = particle_velocity[:, global_rows]
    coefficient = jnp.where(slot_live, drag_coef[global_rows], jnp.zeros((), drag_coef.dtype))
    cells = recv_cell.reshape(NDEV, NDEV, CAP)
    destination = devices[:, None, None]
    slab_index = destination // N_BRICK
    brick_index = destination % N_BRICK
    plane = cells // (XB * NY)
    across = (cells // NY) % XB
    along = cells % NY
    flat_cell = ((slab_index * ZB + plane) * NX + brick_index * XB + across) * NY + along
    fields = stacked.reshape(4, -1)[:, flat_cell]
    fluid_frac = fields[3]
    beta = coefficient * (1.0 - fluid_frac) / (fluid_frac * fluid_frac)
    force = beta * (fields[:3] - part_moving)
    deposit = jnp.zeros((3, NZ * NX * NY), jnp.float32).astype(force.dtype)
    deposit = deposit.at[:, flat_cell.reshape(-1)].add(force.reshape(3, -1)).reshape(3, NZ, NX, NY)
    new_velocity = fluid_velocity + time_step * (viscous - deposit) / porosity
    return new_velocity, force.reshape(3, -1)
```

```python
import functools

import jax
import jax.numpy as jnp
from jax import lax
from jax.experimental import pallas as pl
from jax.experimental.pallas import tpu as pltpu
from jax.sharding import PartitionSpec as P

time_step = 0.05
F32, BF16, I32 = jnp.float32, jnp.bfloat16, jnp.int32
LAST = 2**31 - 1


def split3(x):
    high = x.astype(BF16)
    rest = x - high.astype(F32)
    mid = rest.astype(BF16)
    low = (rest - mid.astype(F32)).astype(BF16)
    return high, mid, low


def pick_kernel(counts_ref, pv_ref, coef_ref, rows_ref, out_ref, table, *, cap):
    me = lax.axis_index("slab") * lax.axis_size("brick") + lax.axis_index("brick")
    for c in range(4):
        whole = coef_ref[...] if c == 3 else pv_ref[c]
        halves = jnp.concatenate([whole[:64], whole[64:]], axis=1)
        for p, piece in enumerate(split3(halves)):
            table[p * 256 + c * 64 : p * 256 + (c + 1) * 64, :] = piece
    r_iota = lax.broadcasted_iota(I32, (256, cap), 0)
    l_iota = lax.broadcasted_iota(I32, (64, cap), 0)
    k_iota = lax.broadcasted_iota(I32, (1, cap), 1)

    def one(t, carry):
        row = jnp.concatenate([rows_ref[pl.ds(2 * t, 1), :], rows_ref[pl.ds(2 * t + 1, 1), :]], axis=1)
        r = (row & 127) + ((row >> 13) << 7)
        l = (row >> 7) & 63
        onehot = jnp.where(r_iota == r, 1.0, 0.0).astype(BF16)
        got = jnp.dot(table[...], onehot, preferred_element_type=F32)
        got = got[:256] + (got[256:512] + got[512:])
        mask = l_iota == l
        live = k_iota < counts_ref[t]
        slot = (me * cap + k_iota).astype(F32)
        for c in range(4):
            value = jnp.sum(jnp.where(mask, got[c * 64 : (c + 1) * 64], 0.0), axis=0, keepdims=True)
            if c == 0:
                value = jnp.where(live, value, slot)
            if c == 3:
                value = jnp.where(live, value, 0.0)
            out_ref[t, 2 * c : 2 * c + 1, :] = value[:, :128]
            out_ref[t, 2 * c + 1 : 2 * c + 2, :] = value[:, 128:]
        return carry

    lax.fori_loop(0, out_ref.shape[0], one, 0, unroll=2)


def key_kernel(arrived_ref, cell_ref, key_ref, data_ref, starts_ref):
    tiles = cell_ref.shape[0] // 8
    place = lax.broadcasted_iota(I32, (8, 128), 0) * 128 + lax.broadcasted_iota(I32, (8, 128), 1)

    def one(j, sums):
        parts = [arrived_ref[4 * j + i] for i in range(4)]
        rows = pl.ds(pl.multiple_of(8 * j, 8), 8)
        for c in range(4):
            value = jnp.concatenate([part[2 * c : 2 * c + 2] for part in parts], axis=0)
            data_ref[c, rows, :] = value
        live = value != 0.0
        cell = cell_ref[rows, :]
        block = cell >> 12
        slot = j * 1024 + place
        key = ((block - 16) << 27) + (slot << 12) + (cell & 4095)
        key_ref[rows, :] = jnp.where(live, key, LAST)
        block = jnp.where(live, block, 32)
        return tuple(s + jnp.where(block < b + 1, 1, 0) for b, s in enumerate(sums))

    sums = lax.fori_loop(0, tiles, one, tuple(jnp.zeros((8, 128), I32) for _ in range(32)))
    tail = (cell_ref[tiles * 8 - 8 :, :] == 131071) & (data_ref[3, tiles * 8 - 8 :, :] != 0.0) & (place == 1023)
    starts_ref[0] = 0
    for b in range(32):
        starts_ref[b + 1] = jnp.sum(sums[b])
    starts_ref[32] = jnp.where(jnp.sum(jnp.where(tail, 1, 0)) > 0, tiles * 1024, starts_ref[32])


def brick_kernel(
    starts_ref, key_ref, coef_ref, p0_ref, p1_ref, p2_ref, fluid_ref, zlo_ref, zhi_ref, xlo_ref, xhi_ref,
    force_ref, slot_ref, net_ref, padded, table, deposit, *, width,
):
    rows = key_ref.shape[0]
    n = width // 128
    force_ref[...] = jnp.zeros_like(force_ref)
    slot_ref[...] = jnp.where(coef_ref[...] != 0.0, (key_ref[...] >> 12) & 32767, p0_ref[...].astype(I32))
    for z in range(8):
        padded[z + 1, :, 8:40, :] = fluid_ref[z]
        for c in range(4):
            padded[z + 1, c, 7:8, :] = xlo_ref[z, c : c + 1, :]
            padded[z + 1, c, 40:41, :] = xhi_ref[z, c : c + 1, :]
    padded[0, :, 8:40, :] = zlo_ref[...]
    padded[9, :, 8:40, :] = zhi_ref[...]

    r_iota = lax.broadcasted_iota(I32, (256, width), 0)
    l_iota = lax.broadcasted_iota(I32, (16, width), 0)
    p_iota = lax.broadcasted_iota(I32, (1, width), 1)
    y_iota = lax.broadcasted_iota(I32, (8, 512), 1)

    def block(b, carry):
        z, q = b // 4, b % 4
        x8 = pl.multiple_of(q * 8, 8)
        for c in range(4):
            centre = fluid_ref[z, c, pl.ds(x8, 8), :]
            for h in range(2):
                for p, piece in enumerate(split3(centre[:, h * 256 : (h + 1) * 256])):
                    at = p * 64 + c * 16 + h * 8
                    table[at : at + 8, :] = piece.astype(F32)
        pieces = table[...].astype(BF16)
        deposit[...] = jnp.zeros_like(deposit)
        first, end = starts_ref[b], starts_ref[b + 1]
        row0 = first // 128

        def window(w, inner):
            row = row0 + w * n
            at = jnp.minimum(row, rows - n)

            def line(ref):
                return jnp.concatenate([ref[pl.ds(at + i, 1), :] for i in range(n)], axis=1)

            key = line(key_ref)
            valid = ((key >> 27) + 16 == b) & (p_iota >= (row - at) * 128)
            r = jnp.where(valid, key & 255, -1)
            l = ((key >> 9) & 7) + ((key >> 8) & 1) * 8
            onehot = jnp.where(r_iota == r, 1.0, 0.0).astype(BF16)
            got = jnp.dot(pieces, onehot, preferred_element_type=F32)
            got = got[:64] + (got[64:128] + got[128:])
            mask = l_iota == l
            u = [
                jnp.sum(jnp.where(mask, got[c * 16 : (c + 1) * 16], 0.0), axis=0, keepdims=True) for c in range(4)
            ]
            frac = jnp.where(valid, u[3], 1.0)
            beta = line(coef_ref) * (1.0 - frac) / (frac * frac)
            split = []
            for c, ref in enumerate((p0_ref, p1_ref, p2_ref)):
                force = jnp.where(valid, beta * (u[c] - line(ref)), 0.0)
                for i in range(n):
                    force_ref[c, pl.ds(at + i, 1), :] += force[:, i * 128 : (i + 1) * 128]
                split.append(split3(force))
            spread = jnp.concatenate(
                [jnp.where(mask, split[c][p].astype(F32), 0.0) for p in range(3) for c in range(3)], axis=0
            ).astype(BF16)
            deposit[...] += lax.dot_general(
                spread, onehot, (((1,), (1,)), ((), ())), preferred_element_type=F32
            )
            return inner

        windows = jnp.where(end > first, (end - row0 * 128 + width - 1) // width, 0)
        lax.fori_loop(0, windows, window, 0)

        tall = [padded[z + 1, c, pl.ds(x8, 24), :] for c in range(4)]
        below = [padded[z, c, pl.ds(x8 + 8, 8), :] for c in range(4)]
        above = [padded[z + 2, c, pl.ds(x8 + 8, 8), :] for c in range(4)]
        centre = [t[8:16] for t in tall]
        sides = [above, below, [t[9:17] for t in tall], [t[7:15] for t in tall]]
        sides.append([jnp.where(y_iota == 511, 0.0, pltpu.roll(t, 511, 1)) for t in centre])
        sides.append([jnp.where(y_iota == 0, 0.0, pltpu.roll(t, 1, 1)) for t in centre])
        total = [jnp.zeros((8, 512), F32) for _ in range(3)]
        for side in sides:
            weight = 0.5 * (centre[3] + side[3])
            for c in range(3):
                total[c] = total[c] + weight * (side[c] - centre[c])
        summed = deposit[0:48, :] + (deposit[48:96, :] + deposit[96:144, :])
        for c in range(3):
            left, right = summed[c * 16 : c * 16 + 8], summed[c * 16 + 8 : c * 16 + 16]
            net_ref[z, c, pl.ds(x8, 8), :] = total[c] - jnp.concatenate([left, right], axis=1)
        return carry

    lax.fori_loop(0, 32, block, 0)


def shift(block, axis, step):
    count = lax.axis_size(axis)
    pairs = [(i, i + step) for i in range(count) if 0 <= i + step < count]
    return lax.ppermute(block, axis, pairs)


def per_device(
    fluid_velocity, porosity, particle_velocity, drag_coef, send_rows, counts, recv_cell
):
    n_slab = lax.axis_size("slab")
    n_brick = lax.axis_size("brick")
    devices = n_slab * n_brick
    cap = send_rows.shape[0] // devices
    vmem = pl.BlockSpec(memory_space=pltpu.VMEM)
    smem = pl.BlockSpec(memory_space=pltpu.SMEM)
    params = pltpu.CompilerParams(vmem_limit_bytes=40 << 20)

    stacked = jnp.concatenate([fluid_velocity[:, 0], porosity], 0).reshape(4, 8, 32, 512)
    bricks = lax.all_to_all(jnp.swapaxes(stacked, 0, 1), "brick", split_axis=0, concat_axis=0, tiled=True)

    packed = pl.pallas_call(
        functools.partial(pick_kernel, cap=cap),
        out_shape=jax.ShapeDtypeStruct((devices, 8, 128), F32),
        in_specs=[smem, vmem, vmem, vmem],
        out_specs=vmem,
        scratch_shapes=[pltpu.VMEM((768, 256), BF16)],
        compiler_params=params,
        name="pick_particles",
    )(counts, particle_velocity.reshape(3, 128, 128), drag_coef.reshape(128, 128), send_rows.reshape(256, 128))
    arrived = lax.all_to_all(packed, ("slab", "brick"), split_axis=0, concat_axis=0, tiled=True)

    zlo = shift(bricks[7], "slab", 1)
    zhi = shift(bricks[0], "slab", -1)
    xlo = shift(bricks[:, :, 31, :], "brick", 1)
    xhi = shift(bricks[:, :, 0, :], "brick", -1)

    key, data, starts = pl.pallas_call(
        key_kernel,
        out_shape=(
            jax.ShapeDtypeStruct((256, 128), I32),
            jax.ShapeDtypeStruct((4, 256, 128), F32),
            jax.ShapeDtypeStruct((33,), I32),
        ),
        in_specs=[vmem, vmem],
        out_specs=(vmem, vmem, smem),
        compiler_params=params,
        name="block_keys",
    )(arrived, recv_cell.reshape(256, 128))
    flat = data.reshape(4, -1)
    ordered = lax.sort(
        (key.reshape(-1), flat[3], flat[0], flat[1], flat[2]), num_keys=1, is_stable=False
    )
    force, slot, net = pl.pallas_call(
        functools.partial(brick_kernel, width=256),
        out_shape=(
            jax.ShapeDtypeStruct((3, 256, 128), F32),
            jax.ShapeDtypeStruct((256, 128), I32),
            jax.ShapeDtypeStruct((8, 3, 32, 512), F32),
        ),
        in_specs=[smem] + [vmem] * 10,
        out_specs=(vmem, vmem, vmem),
        scratch_shapes=[
            pltpu.VMEM((10, 4, 48, 512), F32),
            pltpu.VMEM((192, 256), F32),
            pltpu.VMEM((144, 256), F32),
        ],
        compiler_params=params,
        name="brick_forces",
    )(starts, *[part.reshape(256, 128) for part in ordered], bricks, zlo, zhi, xlo, xhi)

    returned = lax.all_to_all(net, "brick", split_axis=0, concat_axis=0, tiled=True)
    flat = force.reshape(3, -1)
    back = lax.sort((slot.reshape(-1), flat[0], flat[1], flat[2]), num_keys=1, is_stable=False)
    slot_force = jnp.stack(back[1:])
    returned = jnp.swapaxes(returned, 0, 1).reshape(fluid_velocity.shape)
    new_velocity = fluid_velocity + time_step * returned / porosity
    return (new_velocity, slot_force)


def solution(mesh):
    placed = (
        P(None, ("slab", "brick"), None, None),
        P(("slab", "brick"), None, None),
        P(None, ("slab", "brick")),
        P(("slab", "brick")),
        P(("slab", "brick")),
        P(("slab", "brick")),
        P(("slab", "brick")),
    )
    return jax.shard_map(
        per_device,
        mesh=mesh,
        in_specs=placed,
        out_specs=(P(None, ("slab", "brick"), None, None), P(None, ("slab", "brick"))),
        check_vma=False,
    )
```

```python
import functools

import jax
import jax.numpy as jnp
from jax import lax
from jax.experimental import pallas as pl
from jax.experimental.pallas import tpu as pltpu
from jax.sharding import PartitionSpec as P

time_step = 0.05
F32, BF16, I32 = jnp.float32, jnp.bfloat16, jnp.int32
LAST = 2**31 - 1


def split3(x):
    high = x.astype(BF16)
    rest = x - high.astype(F32)
    mid = rest.astype(BF16)
    low = (rest - mid.astype(F32)).astype(BF16)
    return high, mid, low


def exchange_kernel(
    counts_ref, pv_ref, coef_ref, rows_ref, u_ref, frac_ref, arrived_ref, bricks_ref, zhalo_ref,
    table, packed, stage, fluid_send, fluid_recv, part_send, part_recv, halo_send, halo_recv, *, cap, group,
):
    n_slab, n_brick = lax.axis_size("slab"), lax.axis_size("brick")
    devices = n_slab * n_brick
    slab, brick = lax.axis_index("slab"), lax.axis_index("brick")
    me = slab * n_brick + brick
    mesh_id = pl.DeviceIdType.MESH

    def coords(d):
        return (d // n_brick, d % n_brick)

    barrier = pltpu.get_barrier_semaphore()

    def greet(j, carry):
        pl.semaphore_signal(barrier, inc=1, device_id=coords((me + j) % devices), device_id_type=mesh_id)
        return carry

    lax.fori_loop(1, devices, greet, 0)

    for c in range(4):
        for b in range(8):
            field = frac_ref[b * 32 : (b + 1) * 32, :] if c == 3 else u_ref[c, b * 32 : (b + 1) * 32, :]
            stage[b, c * 32 : (c + 1) * 32, :] = field
            if b < 7:
                stage[b + 1, 128 + c : 129 + c, :] = field[31:32]
            if b > 0:
                stage[b - 1, 132 + c : 133 + c, :] = field[0:1]
        stage[0, 128 + c : 129 + c, :] = jnp.zeros((1, 512), F32)
        stage[7, 132 + c : 133 + c, :] = jnp.zeros((1, 512), F32)
        whole = coef_ref[...] if c == 3 else pv_ref[c]
        halves = jnp.concatenate([whole[:64], whole[64:]], axis=1)
        for p, piece in enumerate(split3(halves)):
            table[p * 256 + c * 64 : p * 256 + (c + 1) * 64, :] = piece

    pl.semaphore_wait(barrier, devices - 1)

    def chunk(j):
        to = (brick + j) % n_brick
        return pltpu.make_async_remote_copy(
            src_ref=stage.at[to], dst_ref=bricks_ref.at[brick], send_sem=fluid_send.at[to],
            recv_sem=fluid_recv.at[brick], device_id=(slab, to), device_id_type=mesh_id,
        )

    for j in range(1, 8):
        chunk(j).start()
    bricks_ref[brick] = stage[brick]

    r_iota = lax.broadcasted_iota(I32, (256, cap), 0)
    l_iota = lax.broadcasted_iota(I32, (64, cap), 0)
    k_iota = lax.broadcasted_iota(I32, (1, cap), 1)

    def pick(t):
        row = jnp.concatenate([rows_ref[pl.ds(2 * t, 1), :], rows_ref[pl.ds(2 * t + 1, 1), :]], axis=1)
        r = (row & 127) + ((row >> 13) << 7)
        l = (row >> 7) & 63
        onehot = jnp.where(r_iota == r, 1.0, 0.0).astype(BF16)
        got = jnp.dot(table[...], onehot, preferred_element_type=F32)
        got = got[:256] + (got[256:512] + got[512:])
        mask = l_iota == l
        live = k_iota < counts_ref[t]
        slot = (me * cap + k_iota).astype(F32)
        values = []
        for c in range(4):
            value = jnp.sum(jnp.where(mask, got[c * 64 : (c + 1) * 64], 0.0), axis=0, keepdims=True)
            if c == 0:
                value = jnp.where(live, value, slot)
            if c == 3:
                value = jnp.where(live, value, 0.0)
            values += [value[:, :128], value[:, 128:]]
        return jnp.concatenate(values, axis=0)

    def parcel(t):
        return pltpu.make_async_remote_copy(
            src_ref=packed.at[t], dst_ref=arrived_ref.at[me], send_sem=part_send, recv_sem=part_recv,
            device_id=coords(t), device_id_type=mesh_id,
        )

    def some(i, carry):
        to = [(me + 1 + i * group + j) % devices for j in range(group)]
        picked = [pick(t) for t in to]
        for t, value in zip(to, picked):
            packed[t] = value
        for t in to:
            parcel(t).start()
        return carry

    lax.fori_loop(0, devices // group - 1, some, 0)
    to = [(me + 1 + devices - group + j) % devices for j in range(group)]
    picked = [pick(t) for t in to]
    for t, value in zip(to[:-1], picked):
        packed[t] = value
    arrived_ref[me] = picked[-1]
    for t in to[:-1]:
        parcel(t).start()

    for j in range(1, 8):
        source = (brick + j) % n_brick
        pltpu.make_async_remote_copy(
            src_ref=stage.at[source], dst_ref=bricks_ref.at[source], send_sem=fluid_send.at[source],
            recv_sem=fluid_recv.at[source], device_id=(slab, source), device_id_type=mesh_id,
        ).wait_recv()

    def halo(i, to):
        return pltpu.make_async_remote_copy(
            src_ref=bricks_ref.at[7 - 7 * i, pl.ds(0, 128)], dst_ref=zhalo_ref.at[i], send_sem=halo_send.at[i],
            recv_sem=halo_recv.at[i], device_id=(to, brick), device_id_type=mesh_id,
        )

    up, down = slab < n_slab - 1, slab > 0

    @pl.when(up)
    def _():
        halo(0, slab + 1).start()

    @pl.when(down)
    def _():
        halo(1, slab - 1).start()

    @pl.when(jnp.logical_not(up))
    def _():
        zhalo_ref[1] = jnp.zeros((128, 512), F32)

    @pl.when(jnp.logical_not(down))
    def _():
        zhalo_ref[0] = jnp.zeros((128, 512), F32)

    for j in range(1, 8):
        chunk(j).wait_send()
    rest = pltpu.make_async_remote_copy(
        src_ref=packed.at[pl.ds(0, devices - 1)], dst_ref=arrived_ref.at[pl.ds(0, devices - 1)],
        send_sem=part_send, recv_sem=part_recv, device_id=coords((me + 1) % devices), device_id_type=mesh_id,
    )
    rest.wait_send()
    rest.wait_recv()

    @pl.when(up)
    def _():
        halo(0, slab + 1).wait_send()
        halo(1, slab + 1).wait_recv()

    @pl.when(down)
    def _():
        halo(1, slab - 1).wait_send()
        halo(0, slab - 1).wait_recv()


def key_kernel(arrived_ref, cell_ref, key_ref, data_ref, starts_ref):
    tiles = cell_ref.shape[0] // 8
    place = lax.broadcasted_iota(I32, (8, 128), 0) * 128 + lax.broadcasted_iota(I32, (8, 128), 1)

    def one(j, sums):
        parts = [arrived_ref[4 * j + i] for i in range(4)]
        rows = pl.ds(pl.multiple_of(8 * j, 8), 8)
        for c in range(4):
            value = jnp.concatenate([part[2 * c : 2 * c + 2] for part in parts], axis=0)
            data_ref[c, rows, :] = value
        live = value != 0.0
        cell = cell_ref[rows, :]
        block = cell >> 12
        slot = j * 1024 + place
        key = ((block - 16) << 27) + (slot << 12) + (cell & 4095)
        key_ref[rows, :] = jnp.where(live, key, LAST)
        block = jnp.where(live, block, 32)
        return tuple(s + jnp.where(block < b + 1, 1, 0) for b, s in enumerate(sums))

    sums = lax.fori_loop(0, tiles, one, tuple(jnp.zeros((8, 128), I32) for _ in range(32)))
    tail = (cell_ref[tiles * 8 - 8 :, :] == 131071) & (data_ref[3, tiles * 8 - 8 :, :] != 0.0) & (place == 1023)
    starts_ref[0] = 0
    for b in range(32):
        starts_ref[b + 1] = jnp.sum(sums[b])
    starts_ref[32] = jnp.where(jnp.sum(jnp.where(tail, 1, 0)) > 0, tiles * 1024, starts_ref[32])


def brick_kernel(
    starts_ref, key_ref, coef_ref, p0_ref, p1_ref, p2_ref, bricks_ref, zhalo_ref,
    force_ref, slot_ref, net_ref, padded, table, deposit, *, width,
):
    rows = key_ref.shape[0]
    n = width // 128
    force_ref[...] = jnp.zeros_like(force_ref)
    slot_ref[...] = jnp.where(coef_ref[...] != 0.0, (key_ref[...] >> 12) & 32767, p0_ref[...].astype(I32))
    for c in range(4):
        own = slice(c * 32, (c + 1) * 32)
        for z in range(8):
            padded[z + 1, c, 8:40, :] = bricks_ref[z, own, :]
            padded[z + 1, c, 7:8, :] = bricks_ref[z, 128 + c : 129 + c, :]
            padded[z + 1, c, 40:41, :] = bricks_ref[z, 132 + c : 133 + c, :]
        padded[0, c, 8:40, :] = zhalo_ref[0, own, :]
        padded[9, c, 8:40, :] = zhalo_ref[1, own, :]

    r_iota = lax.broadcasted_iota(I32, (256, width), 0)
    l_iota = lax.broadcasted_iota(I32, (16, width), 0)
    p_iota = lax.broadcasted_iota(I32, (1, width), 1)
    y_iota = lax.broadcasted_iota(I32, (8, 512), 1)

    def block(b, carry):
        z, q = b // 4, b % 4
        x8 = pl.multiple_of(q * 8, 8)
        for c in range(4):
            centre = padded[z + 1, c, pl.ds(x8 + 8, 8), :]
            for h in range(2):
                for p, piece in enumerate(split3(centre[:, h * 256 : (h + 1) * 256])):
                    at = p * 64 + c * 16 + h * 8
                    table[at : at + 8, :] = piece.astype(F32)
        pieces = table[...].astype(BF16)
        deposit[...] = jnp.zeros_like(deposit)
        first, end = starts_ref[b], starts_ref[b + 1]
        row0 = first // 128

        def window(w, inner):
            row = row0 + w * n
            at = jnp.minimum(row, rows - n)

            def line(ref):
                return jnp.concatenate([ref[pl.ds(at + i, 1), :] for i in range(n)], axis=1)

            key = line(key_ref)
            valid = ((key >> 27) + 16 == b) & (p_iota >= (row - at) * 128)
            r = jnp.where(valid, key & 255, -1)
            l = ((key >> 9) & 7) + ((key >> 8) & 1) * 8
            onehot = jnp.where(r_iota == r, 1.0, 0.0).astype(BF16)
            got = jnp.dot(pieces, onehot, preferred_element_type=F32)
            got = got[:64] + (got[64:128] + got[128:])
            mask = l_iota == l
            u = [
                jnp.sum(jnp.where(mask, got[c * 16 : (c + 1) * 16], 0.0), axis=0, keepdims=True) for c in range(4)
            ]
            frac = jnp.where(valid, u[3], 1.0)
            beta = line(coef_ref) * (1.0 - frac) / (frac * frac)
            split = []
            for c, ref in enumerate((p0_ref, p1_ref, p2_ref)):
                force = jnp.where(valid, beta * (u[c] - line(ref)), 0.0)
                for i in range(n):
                    force_ref[c, pl.ds(at + i, 1), :] += force[:, i * 128 : (i + 1) * 128]
                split.append(split3(force))
            spread = jnp.concatenate(
                [jnp.where(mask, split[c][p].astype(F32), 0.0) for p in range(3) for c in range(3)], axis=0
            ).astype(BF16)
            deposit[...] += lax.dot_general(
                spread, onehot, (((1,), (1,)), ((), ())), preferred_element_type=F32
            )
            return inner

        windows = jnp.where(end > first, (end - row0 * 128 + width - 1) // width, 0)
        lax.fori_loop(0, windows, window, 0)

        tall = [padded[z + 1, c, pl.ds(x8, 24), :] for c in range(4)]
        below = [padded[z, c, pl.ds(x8 + 8, 8), :] for c in range(4)]
        above = [padded[z + 2, c, pl.ds(x8 + 8, 8), :] for c in range(4)]
        centre = [t[8:16] for t in tall]
        sides = [above, below, [t[9:17] for t in tall], [t[7:15] for t in tall]]
        sides.append([jnp.where(y_iota == 511, 0.0, pltpu.roll(t, 511, 1)) for t in centre])
        sides.append([jnp.where(y_iota == 0, 0.0, pltpu.roll(t, 1, 1)) for t in centre])
        total = [jnp.zeros((8, 512), F32) for _ in range(3)]
        for side in sides:
            weight = 0.5 * (centre[3] + side[3])
            for c in range(3):
                total[c] = total[c] + weight * (side[c] - centre[c])
        summed = deposit[0:48, :] + (deposit[48:96, :] + deposit[96:144, :])
        for c in range(3):
            left, right = summed[c * 16 : c * 16 + 8], summed[c * 16 + 8 : c * 16 + 16]
            net_ref[z, c, pl.ds(x8, 8), :] = total[c] - jnp.concatenate([left, right], axis=1)
        return carry

    lax.fori_loop(0, 32, block, 0)


def per_device(
    fluid_velocity, porosity, particle_velocity, drag_coef, send_rows, counts, recv_cell
):
    n_slab = lax.axis_size("slab")
    n_brick = lax.axis_size("brick")
    devices = n_slab * n_brick
    cap = send_rows.shape[0] // devices
    vmem = pl.BlockSpec(memory_space=pltpu.VMEM)
    smem = pl.BlockSpec(memory_space=pltpu.SMEM)
    params = pltpu.CompilerParams(vmem_limit_bytes=40 << 20)

    arrived, bricks, zhalo = pl.pallas_call(
        functools.partial(exchange_kernel, cap=cap, group=4),
        out_shape=(
            jax.ShapeDtypeStruct((devices, 8, 128), F32),
            jax.ShapeDtypeStruct((8, 136, 512), F32),
            jax.ShapeDtypeStruct((2, 128, 512), F32),
        ),
        in_specs=[smem] + [vmem] * 5,
        out_specs=(vmem, vmem, vmem),
        scratch_shapes=[
            pltpu.VMEM((768, 256), BF16),
            pltpu.VMEM((devices, 8, 128), F32),
            pltpu.VMEM((8, 136, 512), F32),
            pltpu.SemaphoreType.DMA((8,)),
            pltpu.SemaphoreType.DMA((8,)),
            pltpu.SemaphoreType.DMA,
            pltpu.SemaphoreType.DMA,
            pltpu.SemaphoreType.DMA((2,)),
            pltpu.SemaphoreType.DMA((2,)),
        ],
        compiler_params=pltpu.CompilerParams(
            vmem_limit_bytes=40 << 20, collective_id=0, has_side_effects=True
        ),
        name="exchange",
    )(
        counts,
        particle_velocity.reshape(3, 128, 128),
        drag_coef.reshape(128, 128),
        send_rows.reshape(256, 128),
        fluid_velocity.reshape(3, 256, 512),
        porosity.reshape(256, 512),
    )

    key, data, starts = pl.pallas_call(
        key_kernel,
        out_shape=(
            jax.ShapeDtypeStruct((256, 128), I32),
            jax.ShapeDtypeStruct((4, 256, 128), F32),
            jax.ShapeDtypeStruct((33,), I32),
        ),
        in_specs=[vmem, vmem],
        out_specs=(vmem, vmem, smem),
        compiler_params=params,
        name="block_keys",
    )(arrived, recv_cell.reshape(256, 128))
    flat = data.reshape(4, -1)
    ordered = lax.sort(
        (key.reshape(-1), flat[3], flat[0], flat[1], flat[2]), num_keys=1, is_stable=False
    )
    force, slot, net = pl.pallas_call(
        functools.partial(brick_kernel, width=256),
        out_shape=(
            jax.ShapeDtypeStruct((3, 256, 128), F32),
            jax.ShapeDtypeStruct((256, 128), I32),
            jax.ShapeDtypeStruct((8, 3, 32, 512), F32),
        ),
        in_specs=[smem] + [vmem] * 7,
        out_specs=(vmem, vmem, vmem),
        scratch_shapes=[
            pltpu.VMEM((10, 4, 48, 512), F32),
            pltpu.VMEM((192, 256), F32),
            pltpu.VMEM((144, 256), F32),
        ],
        compiler_params=params,
        name="brick_forces",
    )(starts, *[part.reshape(256, 128) for part in ordered], bricks, zhalo)

    returned = lax.all_to_all(net, "brick", split_axis=0, concat_axis=0, tiled=True)
    flat = force.reshape(3, -1)
    back = lax.sort((slot.reshape(-1), flat[0], flat[1], flat[2]), num_keys=1, is_stable=False)
    slot_force = jnp.stack(back[1:])
    returned = jnp.swapaxes(returned, 0, 1).reshape(fluid_velocity.shape)
    new_velocity = fluid_velocity + time_step * returned / porosity
    return (new_velocity, slot_force)


def solution(mesh):
    placed = (
        P(None, ("slab", "brick"), None, None),
        P(("slab", "brick"), None, None),
        P(None, ("slab", "brick")),
        P(("slab", "brick")),
        P(("slab", "brick")),
        P(("slab", "brick")),
        P(("slab", "brick")),
    )
    return jax.shard_map(
        per_device,
        mesh=mesh,
        in_specs=placed,
        out_specs=(P(None, ("slab", "brick"), None, None), P(None, ("slab", "brick"))),
        check_vma=False,
    )
```

```python
import functools

import jax
import jax.numpy as jnp
from jax import lax
from jax.experimental import pallas as pl
from jax.experimental.pallas import tpu as pltpu
from jax.sharding import PartitionSpec as P

time_step = 0.05
F32, BF16, I32 = jnp.float32, jnp.bfloat16, jnp.int32
LAST = 2**31 - 1


def split3(x):
    high = x.astype(BF16)
    rest = x - high.astype(F32)
    mid = rest.astype(BF16)
    low = (rest - mid.astype(F32)).astype(BF16)
    return high, mid, low


def exchange_kernel(
    counts_ref, pv_ref, coef_ref, rows_ref, u_ref, frac_ref, arrived_ref, bricks_ref, zhalo_ref,
    table, packed, stage, fluid_send, fluid_recv, part_send, part_recv, halo_send, halo_recv, *, cap, group,
):
    n_slab, n_brick = lax.axis_size("slab"), lax.axis_size("brick")
    devices = n_slab * n_brick
    slab, brick = lax.axis_index("slab"), lax.axis_index("brick")
    me = slab * n_brick + brick
    mesh_id = pl.DeviceIdType.MESH

    def coords(d):
        return (d // n_brick, d % n_brick)

    barrier = pltpu.get_barrier_semaphore()

    def greet(j, carry):
        pl.semaphore_signal(barrier, inc=1, device_id=coords((me + j) % devices), device_id_type=mesh_id)
        return carry

    lax.fori_loop(1, devices, greet, 0)

    for c in range(4):
        for b in range(8):
            field = frac_ref[b * 32 : (b + 1) * 32, :] if c == 3 else u_ref[c, b * 32 : (b + 1) * 32, :]
            stage[b, c * 32 : (c + 1) * 32, :] = field
            if b < 7:
                stage[b + 1, 128 + c : 129 + c, :] = field[31:32]
            if b > 0:
                stage[b - 1, 132 + c : 133 + c, :] = field[0:1]
        stage[0, 128 + c : 129 + c, :] = jnp.zeros((1, 512), F32)
        stage[7, 132 + c : 133 + c, :] = jnp.zeros((1, 512), F32)
        whole = coef_ref[...] if c == 3 else pv_ref[c]
        halves = jnp.concatenate([whole[:64], whole[64:]], axis=1)
        for p, piece in enumerate(split3(halves)):
            table[p * 256 + c * 64 : p * 256 + (c + 1) * 64, :] = piece

    pl.semaphore_wait(barrier, devices - 1)

    def chunk(j):
        to = (brick + j) % n_brick
        return pltpu.make_async_remote_copy(
            src_ref=stage.at[to], dst_ref=bricks_ref.at[brick], send_sem=fluid_send.at[to],
            recv_sem=fluid_recv.at[brick], device_id=(slab, to), device_id_type=mesh_id,
        )

    for j in range(1, 8):
        chunk(j).start()
    bricks_ref[brick] = stage[brick]

    r_iota = lax.broadcasted_iota(I32, (256, cap), 0).astype(F32).astype(BF16)
    one, zero = jnp.ones((), BF16), jnp.zeros((), BF16)
    l_iota = lax.broadcasted_iota(I32, (64, cap), 0)
    k_iota = lax.broadcasted_iota(I32, (1, cap), 1)

    def pick(to):
        onehots, planes, gots, picked = [], [], [], []
        for t in to:
            row = jnp.concatenate([rows_ref[pl.ds(2 * t, 1), :], rows_ref[pl.ds(2 * t + 1, 1), :]], axis=1)
            r = (row & 127) + ((row >> 13) << 7)
            onehots.append(jnp.where(r_iota == r.astype(F32).astype(BF16), one, zero))
            planes.append((row >> 7) & 63)
        for onehot in onehots:
            gots.append(jnp.dot(table[...], onehot, preferred_element_type=F32))
        slot = (me * cap + k_iota).astype(F32)
        for t, got, l in zip(to, gots, planes):
            got = got[:256] + (got[256:512] + got[512:])
            mask = l_iota == l
            live = k_iota < counts_ref[t]
            values = []
            for c in range(4):
                value = jnp.sum(jnp.where(mask, got[c * 64 : (c + 1) * 64], 0.0), axis=0, keepdims=True)
                if c == 0:
                    value = jnp.where(live, value, slot)
                if c == 3:
                    value = jnp.where(live, value, 0.0)
                values += [value[:, :128], value[:, 128:]]
            picked.append(jnp.concatenate(values, axis=0))
        return picked

    def parcel(t):
        return pltpu.make_async_remote_copy(
            src_ref=packed.at[t], dst_ref=arrived_ref.at[me], send_sem=part_send, recv_sem=part_recv,
            device_id=coords(t), device_id_type=mesh_id,
        )

    def some(i, carry):
        to = [(me + 1 + i * group + j) % devices for j in range(group)]
        picked = pick(to)
        for t, value in zip(to, picked):
            packed[t] = value
        for t in to:
            parcel(t).start()
        return carry

    lax.fori_loop(0, devices // group - 1, some, 0)
    to = [(me + 1 + devices - group + j) % devices for j in range(group)]
    picked = pick(to)
    for t, value in zip(to[:-1], picked):
        packed[t] = value
    arrived_ref[me] = picked[-1]
    for t in to[:-1]:
        parcel(t).start()

    for j in range(1, 8):
        source = (brick + j) % n_brick
        pltpu.make_async_remote_copy(
            src_ref=stage.at[source], dst_ref=bricks_ref.at[source], send_sem=fluid_send.at[source],
            recv_sem=fluid_recv.at[source], device_id=(slab, source), device_id_type=mesh_id,
        ).wait_recv()

    def halo(i, to):
        return pltpu.make_async_remote_copy(
            src_ref=bricks_ref.at[7 - 7 * i, pl.ds(0, 128)], dst_ref=zhalo_ref.at[i], send_sem=halo_send.at[i],
            recv_sem=halo_recv.at[i], device_id=(to, brick), device_id_type=mesh_id,
        )

    up, down = slab < n_slab - 1, slab > 0

    @pl.when(up)
    def _():
        halo(0, slab + 1).start()

    @pl.when(down)
    def _():
        halo(1, slab - 1).start()

    @pl.when(jnp.logical_not(up))
    def _():
        zhalo_ref[1] = jnp.zeros((128, 512), F32)

    @pl.when(jnp.logical_not(down))
    def _():
        zhalo_ref[0] = jnp.zeros((128, 512), F32)

    for j in range(1, 8):
        chunk(j).wait_send()
    rest = pltpu.make_async_remote_copy(
        src_ref=packed.at[pl.ds(0, devices - 1)], dst_ref=arrived_ref.at[pl.ds(0, devices - 1)],
        send_sem=part_send, recv_sem=part_recv, device_id=coords((me + 1) % devices), device_id_type=mesh_id,
    )
    rest.wait_send()
    rest.wait_recv()

    @pl.when(up)
    def _():
        halo(0, slab + 1).wait_send()
        halo(1, slab + 1).wait_recv()

    @pl.when(down)
    def _():
        halo(1, slab - 1).wait_send()
        halo(0, slab - 1).wait_recv()


def key_kernel(arrived_ref, cell_ref, key_ref, data_ref, starts_ref):
    tiles = cell_ref.shape[0] // 8
    place = lax.broadcasted_iota(I32, (8, 128), 0) * 128 + lax.broadcasted_iota(I32, (8, 128), 1)

    def one(j, sums):
        parts = [arrived_ref[4 * j + i] for i in range(4)]
        rows = pl.ds(pl.multiple_of(8 * j, 8), 8)
        for c in range(4):
            value = jnp.concatenate([part[2 * c : 2 * c + 2] for part in parts], axis=0)
            data_ref[c, rows, :] = value
        live = value != 0.0
        cell = cell_ref[rows, :]
        block = cell >> 12
        slot = j * 1024 + place
        key = ((block - 16) << 27) + (slot << 12) + (cell & 4095)
        key_ref[rows, :] = jnp.where(live, key, LAST)
        block = jnp.where(live, block, 32)
        return tuple(s + jnp.where(block < b + 1, 1, 0) for b, s in enumerate(sums))

    sums = lax.fori_loop(0, tiles, one, tuple(jnp.zeros((8, 128), I32) for _ in range(32)))
    tail = (cell_ref[tiles * 8 - 8 :, :] == 131071) & (data_ref[3, tiles * 8 - 8 :, :] != 0.0) & (place == 1023)
    starts_ref[0] = 0
    for b in range(32):
        starts_ref[b + 1] = jnp.sum(sums[b])
    starts_ref[32] = jnp.where(jnp.sum(jnp.where(tail, 1, 0)) > 0, tiles * 1024, starts_ref[32])


def brick_kernel(
    starts_ref, key_ref, coef_ref, p0_ref, p1_ref, p2_ref, bricks_ref, zhalo_ref,
    force_ref, slot_ref, net_ref, padded, table, deposit, *, width, group,
):
    rows = key_ref.shape[0]
    n = width // 128
    force_ref[...] = jnp.zeros_like(force_ref)
    slot_ref[...] = jnp.where(coef_ref[...] != 0.0, (key_ref[...] >> 12) & 32767, p0_ref[...].astype(I32))
    for c in range(4):
        own = slice(c * 32, (c + 1) * 32)
        for z in range(8):
            padded[z + 1, c, 8:40, :] = bricks_ref[z, own, :]
            padded[z + 1, c, 7:8, :] = bricks_ref[z, 128 + c : 129 + c, :]
            padded[z + 1, c, 40:41, :] = bricks_ref[z, 132 + c : 133 + c, :]
        padded[0, c, 8:40, :] = zhalo_ref[0, own, :]
        padded[9, c, 8:40, :] = zhalo_ref[1, own, :]

    r_iota = lax.broadcasted_iota(I32, (256, width), 0)
    l_iota = lax.broadcasted_iota(I32, (16, width), 0)
    r_iota = r_iota.astype(F32).astype(BF16)
    l_bf = l_iota.astype(F32).astype(BF16)
    p_iota = lax.broadcasted_iota(I32, (1, width), 1)
    y_iota = lax.broadcasted_iota(I32, (8, 512), 1)
    one, zero = jnp.ones((), BF16), jnp.zeros((), BF16)

    def blocks(g, carry):
        bs = [g * group + i for i in range(group)]
        row0s, counts = [], []
        for i, b in enumerate(bs):
            z, q = b // 4, b % 4
            x8 = pl.multiple_of(q * 8, 8)
            for c in range(4):
                centre = padded[z + 1, c, pl.ds(x8 + 8, 8), :]
                for p, piece in enumerate(split3(centre)):
                    at = p * 64 + c * 16
                    table[i, at : at + 16, :] = jnp.concatenate([piece[:, :256], piece[:, 256:]], axis=0)
            deposit[i] = jnp.zeros(deposit.shape[1:], F32)
            first, end = starts_ref[b], starts_ref[b + 1]
            row0 = first // 128
            row0s.append(row0)
            counts.append(jnp.where(end > first, (end - row0 * 128 + width - 1) // width, 0))
        windows = counts[0]
        for c in counts[1:]:
            windows = jnp.maximum(windows, c)

        def window(w, inner):
            ats, oh, valids, ls, gots = [], [], [], [], []

            def line(ref, at):
                return jnp.concatenate([ref[pl.ds(at + k, 1), :] for k in range(n)], axis=1)

            for i, b in enumerate(bs):
                row = row0s[i] + w * n
                at = jnp.minimum(row, rows - n)
                key = line(key_ref, at)
                valid = ((key >> 27) + 16 == b) & (p_iota >= (row - at) * 128)
                r = jnp.where(valid, key & 255, -1)
                l = ((key >> 9) & 7) + ((key >> 8) & 1) * 8
                ats.append(at)
                oh.append(jnp.where(r_iota == r.astype(F32).astype(BF16), one, zero))
                valids.append(valid)
                ls.append(l)
            for i in range(group):
                gots.append(jnp.dot(table[i], oh[i], preferred_element_type=F32))
            spreads = []
            forces = []
            for i in range(group):
                got = gots[i]
                got = got[:64] + (got[64:128] + got[128:])
                mask = l_iota == ls[i]
                u = [
                    jnp.sum(jnp.where(mask, got[c * 16 : (c + 1) * 16], 0.0), axis=0, keepdims=True) for c in range(4)
                ]
                frac = jnp.where(valids[i], u[3], 1.0)
                beta = line(coef_ref, ats[i]) * (1.0 - frac) / (frac * frac)
                fs = [
                    jnp.where(valids[i], beta * (u[c] - line(ref, ats[i])), 0.0)
                    for c, ref in enumerate((p0_ref, p1_ref, p2_ref))
                ]
                forces.append(fs)
                split = [split3(f) for f in fs]
                low_mask = l_bf == ls[i].astype(F32).astype(BF16)
                spreads.append(
                    jnp.concatenate(
                        [jnp.where(low_mask, split[c][p], zero) for p in range(3) for c in range(3)], axis=0
                    )
                )
            for i in range(group):
                deposit[i] += lax.dot_general(
                    spreads[i], oh[i], (((1,), (1,)), ((), ())), preferred_element_type=F32
                )
            for i in range(group):
                for c in range(3):
                    for k in range(n):
                        force_ref[c, pl.ds(ats[i] + k, 1), :] += forces[i][c][:, k * 128 : (k + 1) * 128]
            return inner

        lax.fori_loop(0, windows, window, 0)

        for i, b in enumerate(bs):
            z, q = b // 4, b % 4
            x8 = pl.multiple_of(q * 8, 8)
            tall = [padded[z + 1, c, pl.ds(x8, 24), :] for c in range(4)]
            below = [padded[z, c, pl.ds(x8 + 8, 8), :] for c in range(4)]
            above = [padded[z + 2, c, pl.ds(x8 + 8, 8), :] for c in range(4)]
            centre = [t[8:16] for t in tall]
            sides = [above, below, [t[9:17] for t in tall], [t[7:15] for t in tall]]
            sides.append([jnp.where(y_iota == 511, 0.0, pltpu.roll(t, 511, 1)) for t in centre])
            sides.append([jnp.where(y_iota == 0, 0.0, pltpu.roll(t, 1, 1)) for t in centre])
            total = [jnp.zeros((8, 512), F32) for _ in range(3)]
            for side in sides:
                weight = 0.5 * (centre[3] + side[3])
                for c in range(3):
                    total[c] = total[c] + weight * (side[c] - centre[c])
            summed = deposit[i, 0:48, :] + (deposit[i, 48:96, :] + deposit[i, 96:144, :])
            for c in range(3):
                left, right = summed[c * 16 : c * 16 + 8], summed[c * 16 + 8 : c * 16 + 16]
                net_ref[z, c, pl.ds(x8, 8), :] = total[c] - jnp.concatenate([left, right], axis=1)
        return carry

    lax.fori_loop(0, 32 // group, blocks, 0)


def per_device(
    fluid_velocity, porosity, particle_velocity, drag_coef, send_rows, counts, recv_cell
):
    n_slab = lax.axis_size("slab")
    n_brick = lax.axis_size("brick")
    devices = n_slab * n_brick
    cap = send_rows.shape[0] // devices
    vmem = pl.BlockSpec(memory_space=pltpu.VMEM)
    smem = pl.BlockSpec(memory_space=pltpu.SMEM)
    params = pltpu.CompilerParams(vmem_limit_bytes=40 << 20)

    arrived, bricks, zhalo = pl.pallas_call(
        functools.partial(exchange_kernel, cap=cap, group=8),
        out_shape=(
            jax.ShapeDtypeStruct((devices, 8, 128), F32),
            jax.ShapeDtypeStruct((8, 136, 512), F32),
            jax.ShapeDtypeStruct((2, 128, 512), F32),
        ),
        in_specs=[smem] + [vmem] * 5,
        out_specs=(vmem, vmem, vmem),
        scratch_shapes=[
            pltpu.VMEM((768, 256), BF16),
            pltpu.VMEM((devices, 8, 128), F32),
            pltpu.VMEM((8, 136, 512), F32),
            pltpu.SemaphoreType.DMA((8,)),
            pltpu.SemaphoreType.DMA((8,)),
            pltpu.SemaphoreType.DMA,
            pltpu.SemaphoreType.DMA,
            pltpu.SemaphoreType.DMA((2,)),
            pltpu.SemaphoreType.DMA((2,)),
        ],
        compiler_params=pltpu.CompilerParams(
            vmem_limit_bytes=40 << 20, collective_id=0, has_side_effects=True
        ),
        name="exchange",
    )(
        counts,
        particle_velocity.reshape(3, 128, 128),
        drag_coef.reshape(128, 128),
        send_rows.reshape(256, 128),
        fluid_velocity.reshape(3, 256, 512),
        porosity.reshape(256, 512),
    )

    key, data, starts = pl.pallas_call(
        key_kernel,
        out_shape=(
            jax.ShapeDtypeStruct((256, 128), I32),
            jax.ShapeDtypeStruct((4, 256, 128), F32),
            jax.ShapeDtypeStruct((33,), I32),
        ),
        in_specs=[vmem, vmem],
        out_specs=(vmem, vmem, smem),
        compiler_params=params,
        name="block_keys",
    )(arrived, recv_cell.reshape(256, 128))
    flat = data.reshape(4, -1)
    ordered = lax.sort(
        (key.reshape(-1), flat[3], flat[0], flat[1], flat[2]), num_keys=1, is_stable=False
    )
    force, slot, net = pl.pallas_call(
        functools.partial(brick_kernel, width=256, group=8),
        out_shape=(
            jax.ShapeDtypeStruct((3, 256, 128), F32),
            jax.ShapeDtypeStruct((256, 128), I32),
            jax.ShapeDtypeStruct((8, 3, 32, 512), F32),
        ),
        in_specs=[smem] + [vmem] * 7,
        out_specs=(vmem, vmem, vmem),
        scratch_shapes=[
            pltpu.VMEM((10, 4, 48, 512), F32),
            pltpu.VMEM((8, 192, 256), BF16),
            pltpu.VMEM((8, 144, 256), F32),
        ],
        compiler_params=params,
        name="brick_forces",
    )(starts, *[part.reshape(256, 128) for part in ordered], bricks, zhalo)

    returned = lax.all_to_all(net, "brick", split_axis=0, concat_axis=0, tiled=True)
    flat = force.reshape(3, -1)
    back = lax.sort((slot.reshape(-1), flat[0], flat[1], flat[2]), num_keys=1, is_stable=False)
    slot_force = jnp.stack(back[1:])
    returned = jnp.swapaxes(returned, 0, 1).reshape(fluid_velocity.shape)
    new_velocity = fluid_velocity + time_step * returned / porosity
    return (new_velocity, slot_force)


def solution(mesh):
    placed = (
        P(None, ("slab", "brick"), None, None),
        P(("slab", "brick"), None, None),
        P(None, ("slab", "brick")),
        P(("slab", "brick")),
        P(("slab", "brick")),
        P(("slab", "brick")),
        P(("slab", "brick")),
    )
    return jax.shard_map(
        per_device,
        mesh=mesh,
        in_specs=placed,
        out_specs=(P(None, ("slab", "brick"), None, None), P(None, ("slab", "brick"))),
        check_vma=False,
    )
```

```python
import functools

import jax
import jax.numpy as jnp
from jax import lax
from jax.experimental import pallas as pl
from jax.experimental.pallas import tpu as pltpu
from jax.sharding import PartitionSpec as P

time_step = 0.05
F32, BF16, I32 = jnp.float32, jnp.bfloat16, jnp.int32
LAST = 2**31 - 1


def split3(x):
    high = x.astype(BF16)
    rest = x - high.astype(F32)
    mid = rest.astype(BF16)
    low = (rest - mid.astype(F32)).astype(BF16)
    return high, mid, low


def exchange_kernel(
    counts_ref, pv_ref, coef_ref, rows_ref, u_ref, frac_ref, arrived_ref, stage,
    table, packed, part_send, part_recv, *, cap, group,
):
    n_slab, n_brick = lax.axis_size("slab"), lax.axis_size("brick")
    devices = n_slab * n_brick
    slab, brick = lax.axis_index("slab"), lax.axis_index("brick")
    me = slab * n_brick + brick
    mesh_id = pl.DeviceIdType.MESH

    def coords(d):
        return (d // n_brick, d % n_brick)

    barrier = pltpu.get_barrier_semaphore()

    def greet(j, carry):
        pl.semaphore_signal(barrier, inc=1, device_id=coords((me + j) % devices), device_id_type=mesh_id)
        return carry

    lax.fori_loop(1, devices, greet, 0)

    for c in range(4):
        for b in range(8):
            field = frac_ref[b * 32 : (b + 1) * 32, :] if c == 3 else u_ref[c, b * 32 : (b + 1) * 32, :]
            stage[b, c * 32 : (c + 1) * 32, :] = field
            if b < 7:
                stage[b + 1, 128 + c : 129 + c, :] = field[31:32]
            if b > 0:
                stage[b - 1, 132 + c : 133 + c, :] = field[0:1]
        stage[0, 128 + c : 129 + c, :] = jnp.zeros((1, 512), F32)
        stage[7, 132 + c : 133 + c, :] = jnp.zeros((1, 512), F32)
        whole = coef_ref[...] if c == 3 else pv_ref[c]
        halves = jnp.concatenate([whole[:64], whole[64:]], axis=1)
        for p, piece in enumerate(split3(halves)):
            table[p * 256 + c * 64 : p * 256 + (c + 1) * 64, :] = piece

    pl.semaphore_wait(barrier, devices - 1)

    r_iota = lax.broadcasted_iota(I32, (256, cap), 0).astype(F32).astype(BF16)
    one, zero = jnp.ones((), BF16), jnp.zeros((), BF16)
    l_iota = lax.broadcasted_iota(I32, (64, cap), 0)
    k_iota = lax.broadcasted_iota(I32, (1, cap), 1)

    def pick(to):
        onehots, planes, gots, picked = [], [], [], []
        for t in to:
            row = jnp.concatenate([rows_ref[pl.ds(2 * t, 1), :], rows_ref[pl.ds(2 * t + 1, 1), :]], axis=1)
            r = (row & 127) + ((row >> 13) << 7)
            onehots.append(jnp.where(r_iota == r.astype(F32).astype(BF16), one, zero))
            planes.append((row >> 7) & 63)
        for onehot in onehots:
            gots.append(jnp.dot(table[...], onehot, preferred_element_type=F32))
        slot = (me * cap + k_iota).astype(F32)
        for t, got, l in zip(to, gots, planes):
            got = got[:256] + (got[256:512] + got[512:])
            mask = l_iota == l
            live = k_iota < counts_ref[t]
            values = []
            for c in range(4):
                value = jnp.sum(jnp.where(mask, got[c * 64 : (c + 1) * 64], 0.0), axis=0, keepdims=True)
                if c == 0:
                    value = jnp.where(live, value, slot)
                if c == 3:
                    value = jnp.where(live, value, 0.0)
                values += [value[:, :128], value[:, 128:]]
            picked.append(jnp.concatenate(values, axis=0))
        return picked

    def parcel(t):
        return pltpu.make_async_remote_copy(
            src_ref=packed.at[t], dst_ref=arrived_ref.at[me], send_sem=part_send, recv_sem=part_recv,
            device_id=coords(t), device_id_type=mesh_id,
        )

    def some(i, carry):
        to = [(me + 1 + i * group + j) % devices for j in range(group)]
        picked = pick(to)
        for t, value in zip(to, picked):
            packed[t] = value
        for t in to:
            parcel(t).start()
        return carry

    lax.fori_loop(0, devices // group - 1, some, 0)
    to = [(me + 1 + devices - group + j) % devices for j in range(group)]
    picked = pick(to)
    for t, value in zip(to[:-1], picked):
        packed[t] = value
    arrived_ref[me] = picked[-1]
    for t in to[:-1]:
        parcel(t).start()

    rest = pltpu.make_async_remote_copy(
        src_ref=packed.at[pl.ds(0, devices - 1)], dst_ref=arrived_ref.at[pl.ds(0, devices - 1)],
        send_sem=part_send, recv_sem=part_recv, device_id=coords((me + 1) % devices), device_id_type=mesh_id,
    )
    rest.wait_send()
    rest.wait_recv()


def key_kernel(arrived_ref, cell_ref, key_ref, data_ref, starts_ref):
    tiles = cell_ref.shape[0] // 8
    place = lax.broadcasted_iota(I32, (8, 128), 0) * 128 + lax.broadcasted_iota(I32, (8, 128), 1)

    def one(j, sums):
        parts = [arrived_ref[4 * j + i] for i in range(4)]
        rows = pl.ds(pl.multiple_of(8 * j, 8), 8)
        for c in range(4):
            value = jnp.concatenate([part[2 * c : 2 * c + 2] for part in parts], axis=0)
            data_ref[c, rows, :] = value
        live = value != 0.0
        cell = cell_ref[rows, :]
        block = cell >> 12
        slot = j * 1024 + place
        key = ((block - 16) << 27) + (slot << 12) + (cell & 4095)
        key_ref[rows, :] = jnp.where(live, key, LAST)
        block = jnp.where(live, block, 32)
        return tuple(s + jnp.where(block < b + 1, 1, 0) for b, s in enumerate(sums))

    sums = lax.fori_loop(0, tiles, one, tuple(jnp.zeros((8, 128), I32) for _ in range(32)))
    tail = (cell_ref[tiles * 8 - 8 :, :] == 131071) & (data_ref[3, tiles * 8 - 8 :, :] != 0.0) & (place == 1023)
    starts_ref[0] = 0
    for b in range(32):
        starts_ref[b + 1] = jnp.sum(sums[b])
    starts_ref[32] = jnp.where(jnp.sum(jnp.where(tail, 1, 0)) > 0, tiles * 1024, starts_ref[32])


def brick_kernel(
    starts_ref, key_ref, coef_ref, p0_ref, p1_ref, p2_ref, bricks_ref,
    force_ref, slot_ref, net_ref, padded, table, deposit, *, width, group,
):
    rows = key_ref.shape[0]
    n = width // 128
    force_ref[...] = jnp.zeros_like(force_ref)
    slot_ref[...] = jnp.where(coef_ref[...] != 0.0, (key_ref[...] >> 12) & 32767, p0_ref[...].astype(I32))
    for c in range(4):
        own = slice(c * 32, (c + 1) * 32)
        for z in range(8):
            padded[z + 1, c, 8:40, :] = bricks_ref[z, own, :]
            padded[z + 1, c, 7:8, :] = bricks_ref[z, 128 + c : 129 + c, :]
            padded[z + 1, c, 40:41, :] = bricks_ref[z, 132 + c : 133 + c, :]
        padded[0, c, 8:40, :] = bricks_ref[0, own, :]
        padded[9, c, 8:40, :] = bricks_ref[7, own, :]

    r_iota = lax.broadcasted_iota(I32, (256, width), 0)
    l_iota = lax.broadcasted_iota(I32, (16, width), 0)
    r_iota = r_iota.astype(F32).astype(BF16)
    l_bf = l_iota.astype(F32).astype(BF16)
    p_iota = lax.broadcasted_iota(I32, (1, width), 1)
    y_iota = lax.broadcasted_iota(I32, (8, 512), 1)
    one, zero = jnp.ones((), BF16), jnp.zeros((), BF16)

    def blocks(g, carry):
        bs = [g * group + i for i in range(group)]
        row0s, counts = [], []
        for i, b in enumerate(bs):
            z, q = b // 4, b % 4
            x8 = pl.multiple_of(q * 8, 8)
            for c in range(4):
                centre = padded[z + 1, c, pl.ds(x8 + 8, 8), :]
                for p, piece in enumerate(split3(centre)):
                    at = p * 64 + c * 16
                    table[i, at : at + 16, :] = jnp.concatenate([piece[:, :256], piece[:, 256:]], axis=0)
            deposit[i] = jnp.zeros(deposit.shape[1:], F32)
            first, end = starts_ref[b], starts_ref[b + 1]
            row0 = first // 128
            row0s.append(row0)
            counts.append(jnp.where(end > first, (end - row0 * 128 + width - 1) // width, 0))
        windows = counts[0]
        for c in counts[1:]:
            windows = jnp.maximum(windows, c)

        def window(w, inner):
            ats, oh, valids, ls, gots = [], [], [], [], []

            def line(ref, at):
                return jnp.concatenate([ref[pl.ds(at + k, 1), :] for k in range(n)], axis=1)

            for i, b in enumerate(bs):
                row = row0s[i] + w * n
                at = jnp.minimum(row, rows - n)
                key = line(key_ref, at)
                valid = ((key >> 27) + 16 == b) & (p_iota >= (row - at) * 128)
                r = jnp.where(valid, key & 255, -1)
                l = ((key >> 9) & 7) + ((key >> 8) & 1) * 8
                ats.append(at)
                oh.append(jnp.where(r_iota == r.astype(F32).astype(BF16), one, zero))
                valids.append(valid)
                ls.append(l)
            for i in range(group):
                gots.append(jnp.dot(table[i], oh[i], preferred_element_type=F32))
            spreads = []
            forces = []
            for i in range(group):
                got = gots[i]
                got = got[:64] + (got[64:128] + got[128:])
                mask = l_iota == ls[i]
                u = [
                    jnp.sum(jnp.where(mask, got[c * 16 : (c + 1) * 16], 0.0), axis=0, keepdims=True) for c in range(4)
                ]
                frac = jnp.where(valids[i], u[3], 1.0)
                beta = line(coef_ref, ats[i]) * (1.0 - frac) / (frac * frac)
                fs = [
                    jnp.where(valids[i], beta * (u[c] - line(ref, ats[i])), 0.0)
                    for c, ref in enumerate((p0_ref, p1_ref, p2_ref))
                ]
                forces.append(fs)
                split = [split3(f) for f in fs]
                low_mask = l_bf == ls[i].astype(F32).astype(BF16)
                spreads.append(
                    jnp.concatenate(
                        [jnp.where(low_mask, split[c][p], zero) for p in range(3) for c in range(3)], axis=0
                    )
                )
            for i in range(group):
                deposit[i] += lax.dot_general(
                    spreads[i], oh[i], (((1,), (1,)), ((), ())), preferred_element_type=F32
                )
            for i in range(group):
                for c in range(3):
                    for k in range(n):
                        force_ref[c, pl.ds(ats[i] + k, 1), :] += forces[i][c][:, k * 128 : (k + 1) * 128]
            return inner

        lax.fori_loop(0, windows, window, 0)

        for i, b in enumerate(bs):
            z, q = b // 4, b % 4
            x8 = pl.multiple_of(q * 8, 8)
            tall = [padded[z + 1, c, pl.ds(x8, 24), :] for c in range(4)]
            below = [padded[z, c, pl.ds(x8 + 8, 8), :] for c in range(4)]
            above = [padded[z + 2, c, pl.ds(x8 + 8, 8), :] for c in range(4)]
            centre = [t[8:16] for t in tall]
            sides = [above, below, [t[9:17] for t in tall], [t[7:15] for t in tall]]
            sides.append([jnp.where(y_iota == 511, 0.0, pltpu.roll(t, 511, 1)) for t in centre])
            sides.append([jnp.where(y_iota == 0, 0.0, pltpu.roll(t, 1, 1)) for t in centre])
            total = [jnp.zeros((8, 512), F32) for _ in range(3)]
            for side in sides:
                weight = 0.5 * (centre[3] + side[3])
                for c in range(3):
                    total[c] = total[c] + weight * (side[c] - centre[c])
            summed = deposit[i, 0:48, :] + (deposit[i, 48:96, :] + deposit[i, 96:144, :])
            for c in range(3):
                left, right = summed[c * 16 : c * 16 + 8], summed[c * 16 + 8 : c * 16 + 16]
                net_ref[z, c, pl.ds(x8, 8), :] = total[c] - jnp.concatenate([left, right], axis=1)
        return carry

    lax.fori_loop(0, 32 // group, blocks, 0)


def per_device(
    fluid_velocity, porosity, particle_velocity, drag_coef, send_rows, counts, recv_cell
):
    n_slab = lax.axis_size("slab")
    n_brick = lax.axis_size("brick")
    devices = n_slab * n_brick
    cap = send_rows.shape[0] // devices
    vmem = pl.BlockSpec(memory_space=pltpu.VMEM)
    smem = pl.BlockSpec(memory_space=pltpu.SMEM)
    params = pltpu.CompilerParams(vmem_limit_bytes=40 << 20)

    ends = [(d, d + 1) for d in range(n_brick - 1, devices - 1, n_brick)]
    ends += [(target, source) for source, target in ends]
    next_velocity = lax.ppermute(fluid_velocity, ("slab", "brick"), ends)
    next_porosity = lax.ppermute(porosity, ("slab", "brick"), ends)

    arrived, staged = pl.pallas_call(
        functools.partial(exchange_kernel, cap=cap, group=8),
        out_shape=(
            jax.ShapeDtypeStruct((devices, 8, 128), F32),
            jax.ShapeDtypeStruct((8, 136, 512), F32),
        ),
        in_specs=[smem] + [vmem] * 5,
        out_specs=(vmem, vmem),
        scratch_shapes=[
            pltpu.VMEM((768, 256), BF16),
            pltpu.VMEM((devices, 8, 128), F32),
            pltpu.SemaphoreType.DMA,
            pltpu.SemaphoreType.DMA,
        ],
        compiler_params=pltpu.CompilerParams(
            vmem_limit_bytes=40 << 20, collective_id=0, has_side_effects=True
        ),
        name="exchange",
    )(
        counts,
        particle_velocity.reshape(3, 128, 128),
        drag_coef.reshape(128, 128),
        send_rows.reshape(256, 128),
        fluid_velocity.reshape(3, 256, 512),
        porosity.reshape(256, 512),
    )

    bricks = lax.all_to_all(staged, "brick", split_axis=0, concat_axis=0, tiled=True)

    key, data, starts = pl.pallas_call(
        key_kernel,
        out_shape=(
            jax.ShapeDtypeStruct((256, 128), I32),
            jax.ShapeDtypeStruct((4, 256, 128), F32),
            jax.ShapeDtypeStruct((33,), I32),
        ),
        in_specs=[vmem, vmem],
        out_specs=(vmem, vmem, smem),
        compiler_params=params,
        name="block_keys",
    )(arrived, recv_cell.reshape(256, 128))
    flat = data.reshape(4, -1)
    ordered = lax.sort(
        (key.reshape(-1), flat[3], flat[0], flat[1], flat[2]), num_keys=1, is_stable=False
    )
    force, slot, net = pl.pallas_call(
        functools.partial(brick_kernel, width=256, group=8),
        out_shape=(
            jax.ShapeDtypeStruct((3, 256, 128), F32),
            jax.ShapeDtypeStruct((256, 128), I32),
            jax.ShapeDtypeStruct((8, 3, 32, 512), F32),
        ),
        in_specs=[smem] + [vmem] * 6,
        out_specs=(vmem, vmem, vmem),
        scratch_shapes=[
            pltpu.VMEM((10, 4, 48, 512), F32),
            pltpu.VMEM((8, 192, 256), BF16),
            pltpu.VMEM((8, 144, 256), F32),
        ],
        compiler_params=params,
        name="brick_forces",
    )(starts, *[part.reshape(256, 128) for part in ordered], bricks)

    returned = lax.all_to_all(net, "brick", split_axis=0, concat_axis=0, tiled=True)
    flat = force.reshape(3, -1)
    back = lax.sort((slot.reshape(-1), flat[0], flat[1], flat[2]), num_keys=1, is_stable=False)
    slot_force = jnp.stack(back[1:])
    returned = jnp.swapaxes(returned, 0, 1).reshape(fluid_velocity.shape)
    brick = lax.axis_index("brick")
    face = 0.5 * (porosity + next_porosity) * (next_velocity - fluid_velocity)
    face = jnp.where((brick == 0) | (brick == n_brick - 1), face, 0.0)
    new_velocity = fluid_velocity + time_step * (returned + face) / porosity
    return (new_velocity, slot_force)


def solution(mesh):
    placed = (
        P(None, ("slab", "brick"), None, None),
        P(("slab", "brick"), None, None),
        P(None, ("slab", "brick")),
        P(("slab", "brick")),
        P(("slab", "brick")),
        P(("slab", "brick")),
        P(("slab", "brick")),
    )
    return jax.shard_map(
        per_device,
        mesh=mesh,
        in_specs=placed,
        out_specs=(P(None, ("slab", "brick"), None, None), P(None, ("slab", "brick"))),
        check_vma=False,
    )
```

```python
import functools

import jax
import jax.numpy as jnp
from jax import lax
from jax.experimental import pallas as pl
from jax.experimental.pallas import tpu as pltpu
from jax.sharding import PartitionSpec as P

time_step = 0.05
F32, BF16, I32 = jnp.float32, jnp.bfloat16, jnp.int32
LAST = 2**31 - 1


def split3(x):
    high = x.astype(BF16)
    rest = x - high.astype(F32)
    mid = rest.astype(BF16)
    low = (rest - mid.astype(F32)).astype(BF16)
    return high, mid, low


def exchange_kernel(
    counts_ref, pv_hbm, coef_hbm, rows_hbm, u_hbm, frac_hbm, cell_hbm,
    stage_hbm, starts_ref, key_ref, p0_ref, p1_ref, p2_ref, drag_ref,
    pv_ref, coef_ref, rows_ref, u_ref, frac_ref, cell_ref, particles,
    stage, table, packed, arrived_ref, load_sem, stage_sem, part_send, part_recv, *, cap, group,
):
    pairs = (
        (u_hbm, u_ref), (frac_hbm, frac_ref), (pv_hbm, pv_ref), (coef_hbm, coef_ref), (rows_hbm, rows_ref),
        (cell_hbm, cell_ref),
    )
    loads = [pltpu.make_async_copy(source, target, load_sem.at[i]) for i, (source, target) in enumerate(pairs)]
    for load in loads:
        load.start()
    n_slab, n_brick = lax.axis_size("slab"), lax.axis_size("brick")
    devices = n_slab * n_brick
    slab, brick = lax.axis_index("slab"), lax.axis_index("brick")
    me = slab * n_brick + brick
    mesh_id = pl.DeviceIdType.MESH

    def coords(d):
        return (d // n_brick, d % n_brick)

    barrier = pltpu.get_barrier_semaphore()

    def greet(j, carry):
        pl.semaphore_signal(barrier, inc=1, device_id=coords((me + j) % devices), device_id_type=mesh_id)
        return carry

    lax.fori_loop(1, devices, greet, 0)

    loads[0].wait()
    loads[1].wait()
    for c in range(4):
        for b in range(8):
            field = frac_ref[b * 32 : (b + 1) * 32, :] if c == 3 else u_ref[c, b * 32 : (b + 1) * 32, :]
            stage[b, c * 32 : (c + 1) * 32, :] = field
            if b < 7:
                stage[b + 1, 128 + c : 129 + c, :] = field[31:32]
            if b > 0:
                stage[b - 1, 132 + c : 133 + c, :] = field[0:1]
        stage[0, 128 + c : 129 + c, :] = jnp.zeros((1, 512), F32)
        stage[7, 132 + c : 133 + c, :] = jnp.zeros((1, 512), F32)
    saved = pltpu.make_async_copy(stage, stage_hbm, stage_sem)
    saved.start()
    for load in loads[2:]:
        load.wait()
    for l in range(128):
        part = pv_ref[:, l * 128 : (l + 1) * 128]
        for c in range(3):
            particles[c, l : l + 1, :] = part[c : c + 1]
    for c in range(4):
        whole = coef_ref[...] if c == 3 else particles[c]
        halves = jnp.concatenate([whole[:64], whole[64:]], axis=1)
        for p, piece in enumerate(split3(halves)):
            table[p * 256 + c * 64 : p * 256 + (c + 1) * 64, :] = piece

    pl.semaphore_wait(barrier, devices - 1)

    r_iota = lax.broadcasted_iota(I32, (256, cap), 0).astype(F32).astype(BF16)
    one, zero = jnp.ones((), BF16), jnp.zeros((), BF16)
    l_iota = lax.broadcasted_iota(I32, (64, cap), 0)
    k_iota = lax.broadcasted_iota(I32, (1, cap), 1)

    def pick(to):
        onehots, planes, gots, picked = [], [], [], []
        for t in to:
            row = jnp.concatenate([rows_ref[pl.ds(2 * t, 1), :], rows_ref[pl.ds(2 * t + 1, 1), :]], axis=1)
            r = (row & 127) + ((row >> 13) << 7)
            onehots.append(jnp.where(r_iota == r.astype(F32).astype(BF16), one, zero))
            planes.append((row >> 7) & 63)
        for onehot in onehots:
            gots.append(jnp.dot(table[...], onehot, preferred_element_type=F32))
        slot = (me * cap + k_iota).astype(F32)
        for t, got, l in zip(to, gots, planes):
            got = got[:256] + (got[256:512] + got[512:])
            mask = l_iota == l
            live = k_iota < counts_ref[t]
            values = []
            for c in range(4):
                value = jnp.sum(jnp.where(mask, got[c * 64 : (c + 1) * 64], 0.0), axis=0, keepdims=True)
                if c == 0:
                    value = jnp.where(live, value, slot)
                if c == 3:
                    value = jnp.where(live, value, 0.0)
                values += [value[:, :128], value[:, 128:]]
            picked.append(jnp.concatenate(values, axis=0))
        return picked

    def parcel(t):
        return pltpu.make_async_remote_copy(
            src_ref=packed.at[t], dst_ref=arrived_ref.at[me], send_sem=part_send, recv_sem=part_recv,
            device_id=coords(t), device_id_type=mesh_id,
        )

    def some(i, carry):
        to = [(me + 1 + i * group + j) % devices for j in range(group)]
        picked = pick(to)
        for t, value in zip(to, picked):
            packed[t] = value
        for t in to:
            parcel(t).start()
        return carry

    lax.fori_loop(0, devices // group - 1, some, 0)
    to = [(me + 1 + devices - group + j) % devices for j in range(group)]
    picked = pick(to)
    for t, value in zip(to[:-1], picked):
        packed[t] = value
    arrived_ref[me] = picked[-1]
    for t in to[:-1]:
        parcel(t).start()

    rest = pltpu.make_async_remote_copy(
        src_ref=packed.at[pl.ds(0, devices - 1)], dst_ref=arrived_ref.at[pl.ds(0, devices - 1)],
        send_sem=part_send, recv_sem=part_recv, device_id=coords((me + 1) % devices), device_id_type=mesh_id,
    )
    rest.wait_send()
    rest.wait_recv()
    saved.wait()

    tiles = cell_ref.shape[0] // 8
    place = lax.broadcasted_iota(I32, (8, 128), 0) * 128 + lax.broadcasted_iota(I32, (8, 128), 1)

    def keys(j, sums):
        parts = [arrived_ref[4 * j + i] for i in range(4)]
        rows = pl.ds(pl.multiple_of(8 * j, 8), 8)
        for c, ref in enumerate((p0_ref, p1_ref, p2_ref, drag_ref)):
            value = jnp.concatenate([part[2 * c : 2 * c + 2] for part in parts], axis=0)
            ref[rows, :] = value
        live = value != 0.0
        cell = cell_ref[rows, :]
        block = cell >> 12
        slot = j * 1024 + place
        key = ((block - 16) << 27) + (slot << 12) + (cell & 4095)
        key_ref[rows, :] = jnp.where(live, key, LAST)
        block = jnp.where(live, block, 32)
        return tuple(s + jnp.where(block < b + 1, 1, 0) for b, s in enumerate(sums))

    sums = lax.fori_loop(0, tiles, keys, tuple(jnp.zeros((8, 128), I32) for _ in range(32)))
    tail = (cell_ref[tiles * 8 - 8 :, :] == 131071) & (drag_ref[tiles * 8 - 8 :, :] != 0.0) & (place == 1023)
    starts_ref[0] = 0
    for b in range(32):
        starts_ref[b + 1] = jnp.sum(sums[b])
    starts_ref[32] = jnp.where(jnp.sum(jnp.where(tail, 1, 0)) > 0, tiles * 1024, starts_ref[32])


def brick_kernel(
    starts_ref, key_hbm, coef_hbm, p0_hbm, p1_hbm, p2_hbm, bricks_hbm,
    f0_ref, f1_ref, f2_ref, slot_ref, net_hbm,
    key_ref, coef_ref, p0_ref, p1_ref, p2_ref, bricks_ref, net_ref, padded, table, deposit, load_sem, net_sem,
    *, width, group,
):
    rows = key_ref.shape[0]
    n = width // 128
    pairs = (
        (bricks_hbm, bricks_ref), (key_hbm, key_ref), (coef_hbm, coef_ref), (p0_hbm, p0_ref), (p1_hbm, p1_ref),
        (p2_hbm, p2_ref),
    )
    loads = [pltpu.make_async_copy(source, target, load_sem.at[i]) for i, (source, target) in enumerate(pairs)]
    for load in loads:
        load.start()
    force_refs = (f0_ref, f1_ref, f2_ref)
    for ref in force_refs:
        ref[...] = jnp.zeros_like(ref)
    for load in loads:
        load.wait()
    slot_ref[...] = jnp.where(coef_ref[...] != 0.0, (key_ref[...] >> 12) & 32767, p0_ref[...].astype(I32))
    for c in range(4):
        own = slice(c * 32, (c + 1) * 32)
        for z in range(8):
            padded[z + 1, c, 8:40, :] = bricks_ref[z, own, :]
            padded[z + 1, c, 7:8, :] = bricks_ref[z, 128 + c : 129 + c, :]
            padded[z + 1, c, 40:41, :] = bricks_ref[z, 132 + c : 133 + c, :]
        padded[0, c, 8:40, :] = bricks_ref[0, own, :]
        padded[9, c, 8:40, :] = bricks_ref[7, own, :]

    r_iota = lax.broadcasted_iota(I32, (256, width), 0)
    l_iota = lax.broadcasted_iota(I32, (16, width), 0)
    r_iota = r_iota.astype(F32).astype(BF16)
    l_bf = l_iota.astype(F32).astype(BF16)
    p_iota = lax.broadcasted_iota(I32, (1, width), 1)
    y_iota = lax.broadcasted_iota(I32, (8, 512), 1)
    one, zero = jnp.ones((), BF16), jnp.zeros((), BF16)

    def blocks(g, carry):
        bs = [g * group + i for i in range(group)]
        row0s, counts = [], []
        for i, b in enumerate(bs):
            z, q = b // 4, b % 4
            x8 = pl.multiple_of(q * 8, 8)
            for c in range(4):
                centre = padded[z + 1, c, pl.ds(x8 + 8, 8), :]
                for p, piece in enumerate(split3(centre)):
                    at = p * 64 + c * 16
                    table[i, at : at + 16, :] = jnp.concatenate([piece[:, :256], piece[:, 256:]], axis=0)
            deposit[i] = jnp.zeros(deposit.shape[1:], F32)
            first, end = starts_ref[b], starts_ref[b + 1]
            row0 = first // 128
            row0s.append(row0)
            counts.append(jnp.where(end > first, (end - row0 * 128 + width - 1) // width, 0))
        windows = counts[0]
        for c in counts[1:]:
            windows = jnp.maximum(windows, c)

        def window(w, inner):
            ats, oh, valids, ls, gots = [], [], [], [], []

            def line(ref, at):
                return jnp.concatenate([ref[pl.ds(at + k, 1), :] for k in range(n)], axis=1)

            for i, b in enumerate(bs):
                row = row0s[i] + w * n
                at = jnp.minimum(row, rows - n)
                key = line(key_ref, at)
                valid = ((key >> 27) + 16 == b) & (p_iota >= (row - at) * 128)
                r = jnp.where(valid, key & 255, -1)
                l = ((key >> 9) & 7) + ((key >> 8) & 1) * 8
                ats.append(at)
                oh.append(jnp.where(r_iota == r.astype(F32).astype(BF16), one, zero))
                valids.append(valid)
                ls.append(l)
            for i in range(group):
                gots.append(jnp.dot(table[i], oh[i], preferred_element_type=F32))
            spreads = []
            forces = []
            for i in range(group):
                got = gots[i]
                got = got[:64] + (got[64:128] + got[128:])
                mask = l_iota == ls[i]
                u = [
                    jnp.sum(jnp.where(mask, got[c * 16 : (c + 1) * 16], 0.0), axis=0, keepdims=True) for c in range(4)
                ]
                frac = jnp.where(valids[i], u[3], 1.0)
                beta = line(coef_ref, ats[i]) * (1.0 - frac) / (frac * frac)
                fs = [
                    jnp.where(valids[i], beta * (u[c] - line(ref, ats[i])), 0.0)
                    for c, ref in enumerate((p0_ref, p1_ref, p2_ref))
                ]
                forces.append(fs)
                split = [split3(f) for f in fs]
                low_mask = l_bf == ls[i].astype(F32).astype(BF16)
                spreads.append(
                    jnp.concatenate(
                        [jnp.where(low_mask, split[c][p], zero) for p in range(3) for c in range(3)], axis=0
                    )
                )
            for i in range(group):
                deposit[i] += lax.dot_general(
                    spreads[i], oh[i], (((1,), (1,)), ((), ())), preferred_element_type=F32
                )
            for i in range(group):
                for c in range(3):
                    for k in range(n):
                        force_refs[c][pl.ds(ats[i] + k, 1), :] += forces[i][c][:, k * 128 : (k + 1) * 128]
            return inner

        lax.fori_loop(0, windows, window, 0)

        for i, b in enumerate(bs):
            z, q = b // 4, b % 4
            x8 = pl.multiple_of(q * 8, 8)
            tall = [padded[z + 1, c, pl.ds(x8, 24), :] for c in range(4)]
            below = [padded[z, c, pl.ds(x8 + 8, 8), :] for c in range(4)]
            above = [padded[z + 2, c, pl.ds(x8 + 8, 8), :] for c in range(4)]
            centre = [t[8:16] for t in tall]
            sides = [above, below, [t[9:17] for t in tall], [t[7:15] for t in tall]]
            sides.append([jnp.where(y_iota == 511, 0.0, pltpu.roll(t, 511, 1)) for t in centre])
            sides.append([jnp.where(y_iota == 0, 0.0, pltpu.roll(t, 1, 1)) for t in centre])
            total = [jnp.zeros((8, 512), F32) for _ in range(3)]
            for side in sides:
                weight = 0.5 * (centre[3] + side[3])
                for c in range(3):
                    total[c] = total[c] + weight * (side[c] - centre[c])
            summed = deposit[i, 0:48, :] + (deposit[i, 48:96, :] + deposit[i, 96:144, :])
            for c in range(3):
                left, right = summed[c * 16 : c * 16 + 8], summed[c * 16 + 8 : c * 16 + 16]
                net_ref[z, c, pl.ds(x8, 8), :] = total[c] - jnp.concatenate([left, right], axis=1)
        planes = pl.ds(g * (group // 4), group // 4)
        pltpu.make_async_copy(net_ref.at[planes], net_hbm.at[planes], net_sem.at[g]).start()
        return carry

    lax.fori_loop(0, 32 // group, blocks, 0)
    for g in range(32 // group):
        planes = pl.ds(g * (group // 4), group // 4)
        pltpu.make_async_copy(net_ref.at[planes], net_hbm.at[planes], net_sem.at[g]).wait()


def per_device(
    fluid_velocity, porosity, particle_velocity, drag_coef, send_rows, counts, recv_cell
):
    n_slab = lax.axis_size("slab")
    n_brick = lax.axis_size("brick")
    devices = n_slab * n_brick
    cap = send_rows.shape[0] // devices
    vmem = pl.BlockSpec(memory_space=pltpu.VMEM)
    smem = pl.BlockSpec(memory_space=pltpu.SMEM)
    params = pltpu.CompilerParams(vmem_limit_bytes=60 << 20)
    ends = [(d, d + 1) for d in range(n_brick - 1, devices - 1, n_brick)]
    ends += [(target, source) for source, target in ends]
    next_velocity = lax.ppermute(fluid_velocity, ("slab", "brick"), ends)
    next_porosity = lax.ppermute(porosity, ("slab", "brick"), ends)

    square = jax.ShapeDtypeStruct((256, 128), F32)
    hbm = pl.BlockSpec(memory_space=pl.ANY)
    staged, starts, key, p0, p1, p2, drag = pl.pallas_call(
        functools.partial(exchange_kernel, cap=cap, group=8),
        out_shape=(
            jax.ShapeDtypeStruct((8, 136, 512), F32),
            jax.ShapeDtypeStruct((33,), I32),
            jax.ShapeDtypeStruct((256, 128), I32),
            square, square, square, square,
        ),
        in_specs=[smem] + [hbm] * 6,
        out_specs=(hbm, smem) + (vmem,) * 5,
        scratch_shapes=[
            pltpu.VMEM((3, 16384), F32),
            pltpu.VMEM((128, 128), F32),
            pltpu.VMEM((256, 128), I32),
            pltpu.VMEM((3, 256, 512), F32),
            pltpu.VMEM((256, 512), F32),
            pltpu.VMEM((256, 128), I32),
            pltpu.VMEM((3, 128, 128), F32),
            pltpu.VMEM((8, 136, 512), F32),
            pltpu.VMEM((768, 256), BF16),
            pltpu.VMEM((devices, 8, 128), F32),
            pltpu.VMEM((devices, 8, 128), F32),
            pltpu.SemaphoreType.DMA((6,)),
            pltpu.SemaphoreType.DMA,
            pltpu.SemaphoreType.DMA,
            pltpu.SemaphoreType.DMA,
        ],
        compiler_params=pltpu.CompilerParams(
            vmem_limit_bytes=60 << 20, collective_id=0, has_side_effects=True
        ),
        name="exchange",
    )(
        counts,
        particle_velocity,
        drag_coef.reshape(128, 128),
        send_rows.reshape(256, 128),
        fluid_velocity.reshape(3, 256, 512),
        porosity.reshape(256, 512),
        recv_cell.reshape(256, 128),
    )

    bricks = lax.all_to_all(staged, "brick", split_axis=0, concat_axis=0, tiled=True)
    ordered = lax.sort(
        [part.reshape(-1) for part in (key, drag, p0, p1, p2)], num_keys=1, is_stable=False
    )
    f0, f1, f2, slot, net = pl.pallas_call(
        functools.partial(brick_kernel, width=256, group=8),
        out_shape=(
            square, square, square,
            jax.ShapeDtypeStruct((256, 128), I32),
            jax.ShapeDtypeStruct((8, 3, 32, 512), F32),
        ),
        in_specs=[smem] + [hbm] * 6,
        out_specs=(vmem,) * 4 + (hbm,),
        scratch_shapes=[
            pltpu.VMEM((256, 128), I32),
            pltpu.VMEM((256, 128), F32),
            pltpu.VMEM((256, 128), F32),
            pltpu.VMEM((256, 128), F32),
            pltpu.VMEM((256, 128), F32),
            pltpu.VMEM((8, 136, 512), F32),
            pltpu.VMEM((8, 3, 32, 512), F32),
            pltpu.VMEM((10, 4, 48, 512), F32),
            pltpu.VMEM((8, 192, 256), BF16),
            pltpu.VMEM((8, 144, 256), F32),
            pltpu.SemaphoreType.DMA((6,)),
            pltpu.SemaphoreType.DMA((4,)),
        ],
        compiler_params=params,
        name="brick_forces",
    )(starts, *[part.reshape(256, 128) for part in ordered], bricks)

    returned = lax.all_to_all(net, "brick", split_axis=0, concat_axis=0, tiled=True)
    back = lax.sort([part.reshape(-1) for part in (slot, f0, f1, f2)], num_keys=1, is_stable=False)
    slot_force = jnp.stack(back[1:])
    slot_force, next_velocity, next_porosity = lax.optimization_barrier(
        (slot_force, next_velocity, next_porosity)
    )
    brick = lax.axis_index("brick")
    face = 0.5 * (porosity + next_porosity) * (next_velocity - fluid_velocity)
    face = jnp.where((brick == 0) | (brick == n_brick - 1), face, 0.0)
    returned = jnp.swapaxes(returned, 0, 1).reshape(fluid_velocity.shape)
    new_velocity = fluid_velocity + time_step * (returned + face) / porosity
    return (new_velocity, slot_force)


def solution(mesh):
    placed = (
        P(None, ("slab", "brick"), None, None),
        P(("slab", "brick"), None, None),
        P(None, ("slab", "brick")),
        P(("slab", "brick")),
        P(("slab", "brick")),
        P(("slab", "brick")),
        P(("slab", "brick")),
    )
    return jax.shard_map(
        per_device,
        mesh=mesh,
        in_specs=placed,
        out_specs=(P(None, ("slab", "brick"), None, None), P(None, ("slab", "brick"))),
        check_vma=False,
    )
```

```python
import functools

import jax
import jax.numpy as jnp
from jax import lax
from jax.experimental import pallas as pl
from jax.experimental.pallas import tpu as pltpu
from jax.sharding import PartitionSpec as P

time_step = 0.05
F32, BF16, I32 = jnp.float32, jnp.bfloat16, jnp.int32
LAST = 2**31 - 1


def split3(x):
    high = x.astype(BF16)
    rest = x - high.astype(F32)
    mid = rest.astype(BF16)
    low = (rest - mid.astype(F32)).astype(BF16)
    return high, mid, low


def exchange_kernel(
    counts_ref, pv_hbm, coef_hbm, rows_hbm, u_hbm, frac_hbm, cell_hbm,
    stage_hbm, zhalo_ref, starts_ref, key_ref, p0_ref, p1_ref, p2_ref, drag_ref,
    pv_ref, coef_ref, rows_ref, u_ref, frac_ref, cell_ref, particles,
    stage, table, packed, arrived_ref, load_sem, stage_sem, part_send, part_recv, halo_send, halo_recv,
    *, cap, group,
):
    pairs = (
        (u_hbm, u_ref), (frac_hbm, frac_ref), (pv_hbm, pv_ref), (coef_hbm, coef_ref), (rows_hbm, rows_ref),
        (cell_hbm, cell_ref),
    )
    loads = [pltpu.make_async_copy(source, target, load_sem.at[i]) for i, (source, target) in enumerate(pairs)]
    for load in loads:
        load.start()
    n_slab, n_brick = lax.axis_size("slab"), lax.axis_size("brick")
    devices = n_slab * n_brick
    slab, brick = lax.axis_index("slab"), lax.axis_index("brick")
    me = slab * n_brick + brick
    mesh_id = pl.DeviceIdType.MESH

    def coords(d):
        return (d // n_brick, d % n_brick)

    barrier = pltpu.get_barrier_semaphore()

    def greet(j, carry):
        pl.semaphore_signal(barrier, inc=1, device_id=coords((me + j) % devices), device_id_type=mesh_id)
        return carry

    lax.fori_loop(1, devices, greet, 0)

    loads[0].wait()
    loads[1].wait()
    for c in range(4):
        for b in range(8):
            field = frac_ref[b * 32 : (b + 1) * 32, :] if c == 3 else u_ref[c, b * 32 : (b + 1) * 32, :]
            stage[b, c * 32 : (c + 1) * 32, :] = field
            if b < 7:
                stage[b + 1, 128 + c : 129 + c, :] = field[31:32]
            if b > 0:
                stage[b - 1, 132 + c : 133 + c, :] = field[0:1]
        stage[0, 128 + c : 129 + c, :] = jnp.zeros((1, 512), F32)
        stage[7, 132 + c : 133 + c, :] = jnp.zeros((1, 512), F32)
    saved = pltpu.make_async_copy(stage, stage_hbm, stage_sem)
    saved.start()
    for load in loads[2:]:
        load.wait()
    for l in range(128):
        part = pv_ref[:, l * 128 : (l + 1) * 128]
        for c in range(3):
            particles[c, l : l + 1, :] = part[c : c + 1]
    for c in range(4):
        whole = coef_ref[...] if c == 3 else particles[c]
        halves = jnp.concatenate([whole[:64], whole[64:]], axis=1)
        for p, piece in enumerate(split3(halves)):
            table[p * 256 + c * 64 : p * 256 + (c + 1) * 64, :] = piece

    pl.semaphore_wait(barrier, devices - 1)

    def halo(i, b):
        return pltpu.make_async_remote_copy(
            src_ref=stage.at[b, pl.ds(0, 128)], dst_ref=zhalo_ref.at[i], send_sem=halo_send.at[i, b],
            recv_sem=halo_recv.at[i], device_id=((slab + 1, b), (slab - 1, b))[i], device_id_type=mesh_id,
        )

    up, down = slab < n_slab - 1, slab > 0
    gives = (up & (brick == n_brick - 1), down & (brick == 0))
    gets = (down, up)
    for i in range(2):

        @pl.when(gives[i])
        def _():
            for b in range(8):
                halo(i, b).start()

        @pl.when(jnp.logical_not(gets[i]))
        def _():
            zhalo_ref[i] = jnp.zeros((128, 512), F32)

    r_iota = lax.broadcasted_iota(I32, (256, cap), 0).astype(F32).astype(BF16)
    one, zero = jnp.ones((), BF16), jnp.zeros((), BF16)
    l_iota = lax.broadcasted_iota(I32, (64, cap), 0)
    k_iota = lax.broadcasted_iota(I32, (1, cap), 1)

    def pick(to):
        onehots, planes, gots, picked = [], [], [], []
        for t in to:
            row = jnp.concatenate([rows_ref[pl.ds(2 * t, 1), :], rows_ref[pl.ds(2 * t + 1, 1), :]], axis=1)
            r = (row & 127) + ((row >> 13) << 7)
            onehots.append(jnp.where(r_iota == r.astype(F32).astype(BF16), one, zero))
            planes.append((row >> 7) & 63)
        for onehot in onehots:
            gots.append(jnp.dot(table[...], onehot, preferred_element_type=F32))
        slot = (me * cap + k_iota).astype(F32)
        for t, got, l in zip(to, gots, planes):
            got = got[:256] + (got[256:512] + got[512:])
            mask = l_iota == l
            live = k_iota < counts_ref[t]
            values = []
            for c in range(4):
                value = jnp.sum(jnp.where(mask, got[c * 64 : (c + 1) * 64], 0.0), axis=0, keepdims=True)
                if c == 0:
                    value = jnp.where(live, value, slot)
                if c == 3:
                    value = jnp.where(live, value, 0.0)
                values += [value[:, :128], value[:, 128:]]
            picked.append(jnp.concatenate(values, axis=0))
        return picked

    def parcel(t):
        return pltpu.make_async_remote_copy(
            src_ref=packed.at[t], dst_ref=arrived_ref.at[me], send_sem=part_send, recv_sem=part_recv,
            device_id=coords(t), device_id_type=mesh_id,
        )

    def some(i, carry):
        to = [(me + 1 + i * group + j) % devices for j in range(group)]
        picked = pick(to)
        for t, value in zip(to, picked):
            packed[t] = value
        for t in to:
            parcel(t).start()
        return carry

    lax.fori_loop(0, devices // group - 1, some, 0)
    to = [(me + 1 + devices - group + j) % devices for j in range(group)]
    picked = pick(to)
    for t, value in zip(to[:-1], picked):
        packed[t] = value
    arrived_ref[me] = picked[-1]
    for t in to[:-1]:
        parcel(t).start()

    rest = pltpu.make_async_remote_copy(
        src_ref=packed.at[pl.ds(0, devices - 1)], dst_ref=arrived_ref.at[pl.ds(0, devices - 1)],
        send_sem=part_send, recv_sem=part_recv, device_id=coords((me + 1) % devices), device_id_type=mesh_id,
    )
    rest.wait_send()
    rest.wait_recv()
    saved.wait()
    for i in range(2):

        @pl.when(gives[i])
        def _():
            for b in range(8):
                halo(i, b).wait_send()

        @pl.when(gets[i])
        def _():
            halo(i, 0).wait_recv()


    tiles = cell_ref.shape[0] // 8
    place = lax.broadcasted_iota(I32, (8, 128), 0) * 128 + lax.broadcasted_iota(I32, (8, 128), 1)

    def keys(j, sums):
        parts = [arrived_ref[4 * j + i] for i in range(4)]
        rows = pl.ds(pl.multiple_of(8 * j, 8), 8)
        for c, ref in enumerate((p0_ref, p1_ref, p2_ref, drag_ref)):
            value = jnp.concatenate([part[2 * c : 2 * c + 2] for part in parts], axis=0)
            ref[rows, :] = value
        live = value != 0.0
        cell = cell_ref[rows, :]
        block = cell >> 12
        slot = j * 1024 + place
        key = ((block - 16) << 27) + (slot << 12) + (cell & 4095)
        key_ref[rows, :] = jnp.where(live, key, LAST)
        block = jnp.where(live, block, 32)
        return tuple(s + jnp.where(block < b + 1, 1, 0) for b, s in enumerate(sums))

    sums = lax.fori_loop(0, tiles, keys, tuple(jnp.zeros((8, 128), I32) for _ in range(32)))
    tail = (cell_ref[tiles * 8 - 8 :, :] == 131071) & (drag_ref[tiles * 8 - 8 :, :] != 0.0) & (place == 1023)
    starts_ref[0] = 0
    for b in range(32):
        starts_ref[b + 1] = jnp.sum(sums[b])
    starts_ref[32] = jnp.where(jnp.sum(jnp.where(tail, 1, 0)) > 0, tiles * 1024, starts_ref[32])


def brick_kernel(
    starts_ref, key_hbm, coef_hbm, p0_hbm, p1_hbm, p2_hbm, bricks_hbm, zhalo_hbm,
    f0_ref, f1_ref, f2_ref, slot_ref, net_hbm,
    key_ref, coef_ref, p0_ref, p1_ref, p2_ref, bricks_ref, zhalo_ref, net_ref, padded, table, deposit, load_sem, net_sem,
    *, width, group,
):
    rows = key_ref.shape[0]
    n = width // 128
    pairs = (
        (bricks_hbm, bricks_ref), (key_hbm, key_ref), (coef_hbm, coef_ref), (p0_hbm, p0_ref), (p1_hbm, p1_ref),
        (p2_hbm, p2_ref), (zhalo_hbm, zhalo_ref),
    )
    loads = [pltpu.make_async_copy(source, target, load_sem.at[i]) for i, (source, target) in enumerate(pairs)]
    for load in loads:
        load.start()
    force_refs = (f0_ref, f1_ref, f2_ref)
    for ref in force_refs:
        ref[...] = jnp.zeros_like(ref)
    for load in loads:
        load.wait()
    slot_ref[...] = jnp.where(coef_ref[...] != 0.0, (key_ref[...] >> 12) & 32767, p0_ref[...].astype(I32))
    for c in range(4):
        own = slice(c * 32, (c + 1) * 32)
        for z in range(8):
            padded[z + 1, c, 8:40, :] = bricks_ref[z, own, :]
            padded[z + 1, c, 7:8, :] = bricks_ref[z, 128 + c : 129 + c, :]
            padded[z + 1, c, 40:41, :] = bricks_ref[z, 132 + c : 133 + c, :]
        padded[0, c, 8:40, :] = zhalo_ref[0, own, :]
        padded[9, c, 8:40, :] = zhalo_ref[1, own, :]

    r_iota = lax.broadcasted_iota(I32, (256, width), 0)
    l_iota = lax.broadcasted_iota(I32, (16, width), 0)
    r_iota = r_iota.astype(F32).astype(BF16)
    l_bf = l_iota.astype(F32).astype(BF16)
    p_iota = lax.broadcasted_iota(I32, (1, width), 1)
    y_iota = lax.broadcasted_iota(I32, (8, 512), 1)
    one, zero = jnp.ones((), BF16), jnp.zeros((), BF16)

    def blocks(g, carry):
        bs = [g * group + i for i in range(group)]
        row0s, counts = [], []
        for i, b in enumerate(bs):
            z, q = b // 4, b % 4
            x8 = pl.multiple_of(q * 8, 8)
            for c in range(4):
                centre = padded[z + 1, c, pl.ds(x8 + 8, 8), :]
                for p, piece in enumerate(split3(centre)):
                    at = p * 64 + c * 16
                    table[i, at : at + 16, :] = jnp.concatenate([piece[:, :256], piece[:, 256:]], axis=0)
            deposit[i] = jnp.zeros(deposit.shape[1:], F32)
            first, end = starts_ref[b], starts_ref[b + 1]
            row0 = first // 128
            row0s.append(row0)
            counts.append(jnp.where(end > first, (end - row0 * 128 + width - 1) // width, 0))
        windows = counts[0]
        for c in counts[1:]:
            windows = jnp.maximum(windows, c)

        def window(w, inner):
            ats, oh, valids, ls, gots = [], [], [], [], []

            def line(ref, at):
                return jnp.concatenate([ref[pl.ds(at + k, 1), :] for k in range(n)], axis=1)

            for i, b in enumerate(bs):
                row = row0s[i] + w * n
                at = jnp.minimum(row, rows - n)
                key = line(key_ref, at)
                valid = ((key >> 27) + 16 == b) & (p_iota >= (row - at) * 128)
                r = jnp.where(valid, key & 255, -1)
                l = ((key >> 9) & 7) + ((key >> 8) & 1) * 8
                ats.append(at)
                oh.append(jnp.where(r_iota == r.astype(F32).astype(BF16), one, zero))
                valids.append(valid)
                ls.append(l)
            for i in range(group):
                gots.append(jnp.dot(table[i], oh[i], preferred_element_type=F32))
            spreads = []
            forces = []
            for i in range(group):
                got = gots[i]
                got = got[:64] + (got[64:128] + got[128:])
                mask = l_iota == ls[i]
                u = [
                    jnp.sum(jnp.where(mask, got[c * 16 : (c + 1) * 16], 0.0), axis=0, keepdims=True) for c in range(4)
                ]
                frac = jnp.where(valids[i], u[3], 1.0)
                beta = line(coef_ref, ats[i]) * (1.0 - frac) / (frac * frac)
                fs = [
                    jnp.where(valids[i], beta * (u[c] - line(ref, ats[i])), 0.0)
                    for c, ref in enumerate((p0_ref, p1_ref, p2_ref))
                ]
                forces.append(fs)
                split = [split3(f) for f in fs]
                low_mask = l_bf == ls[i].astype(F32).astype(BF16)
                spreads.append(
                    jnp.concatenate(
                        [jnp.where(low_mask, split[c][p], zero) for p in range(3) for c in range(3)], axis=0
                    )
                )
            for i in range(group):
                deposit[i] += lax.dot_general(
                    spreads[i], oh[i], (((1,), (1,)), ((), ())), preferred_element_type=F32
                )
            for i in range(group):
                for c in range(3):
                    for k in range(n):
                        force_refs[c][pl.ds(ats[i] + k, 1), :] += forces[i][c][:, k * 128 : (k + 1) * 128]
            return inner

        lax.fori_loop(0, windows, window, 0)

        for i, b in enumerate(bs):
            z, q = b // 4, b % 4
            x8 = pl.multiple_of(q * 8, 8)
            tall = [padded[z + 1, c, pl.ds(x8, 24), :] for c in range(4)]
            below = [padded[z, c, pl.ds(x8 + 8, 8), :] for c in range(4)]
            above = [padded[z + 2, c, pl.ds(x8 + 8, 8), :] for c in range(4)]
            centre = [t[8:16] for t in tall]
            sides = [above, below, [t[9:17] for t in tall], [t[7:15] for t in tall]]
            sides.append([jnp.where(y_iota == 511, 0.0, pltpu.roll(t, 511, 1)) for t in centre])
            sides.append([jnp.where(y_iota == 0, 0.0, pltpu.roll(t, 1, 1)) for t in centre])
            total = [jnp.zeros((8, 512), F32) for _ in range(3)]
            for side in sides:
                weight = 0.5 * (centre[3] + side[3])
                for c in range(3):
                    total[c] = total[c] + weight * (side[c] - centre[c])
            summed = deposit[i, 0:48, :] + (deposit[i, 48:96, :] + deposit[i, 96:144, :])
            for c in range(3):
                left, right = summed[c * 16 : c * 16 + 8], summed[c * 16 + 8 : c * 16 + 16]
                net_ref[z, c, pl.ds(x8, 8), :] = total[c] - jnp.concatenate([left, right], axis=1)
        planes = pl.ds(g * (group // 4), group // 4)
        pltpu.make_async_copy(net_ref.at[planes], net_hbm.at[planes], net_sem.at[g]).start()
        return carry

    lax.fori_loop(0, 32 // group, blocks, 0)
    for g in range(32 // group):
        planes = pl.ds(g * (group // 4), group // 4)
        pltpu.make_async_copy(net_ref.at[planes], net_hbm.at[planes], net_sem.at[g]).wait()


def per_device(
    fluid_velocity, porosity, particle_velocity, drag_coef, send_rows, counts, recv_cell
):
    n_slab = lax.axis_size("slab")
    n_brick = lax.axis_size("brick")
    devices = n_slab * n_brick
    cap = send_rows.shape[0] // devices
    vmem = pl.BlockSpec(memory_space=pltpu.VMEM)
    smem = pl.BlockSpec(memory_space=pltpu.SMEM)
    params = pltpu.CompilerParams(vmem_limit_bytes=60 << 20)
    square = jax.ShapeDtypeStruct((256, 128), F32)
    hbm = pl.BlockSpec(memory_space=pl.ANY)
    staged, zhalo, starts, key, p0, p1, p2, drag = pl.pallas_call(
        functools.partial(exchange_kernel, cap=cap, group=8),
        out_shape=(
            jax.ShapeDtypeStruct((8, 136, 512), F32),
            jax.ShapeDtypeStruct((2, 128, 512), F32),
            jax.ShapeDtypeStruct((33,), I32),
            jax.ShapeDtypeStruct((256, 128), I32),
            square, square, square, square,
        ),
        in_specs=[smem] + [hbm] * 6,
        out_specs=(hbm, vmem, smem) + (vmem,) * 5,
        scratch_shapes=[
            pltpu.VMEM((3, 16384), F32),
            pltpu.VMEM((128, 128), F32),
            pltpu.VMEM((256, 128), I32),
            pltpu.VMEM((3, 256, 512), F32),
            pltpu.VMEM((256, 512), F32),
            pltpu.VMEM((256, 128), I32),
            pltpu.VMEM((3, 128, 128), F32),
            pltpu.VMEM((8, 136, 512), F32),
            pltpu.VMEM((768, 256), BF16),
            pltpu.VMEM((devices, 8, 128), F32),
            pltpu.VMEM((devices, 8, 128), F32),
            pltpu.SemaphoreType.DMA((6,)),
            pltpu.SemaphoreType.DMA,
            pltpu.SemaphoreType.DMA,
            pltpu.SemaphoreType.DMA,
            pltpu.SemaphoreType.DMA((2, 8)),
            pltpu.SemaphoreType.DMA((2,)),
        ],
        compiler_params=pltpu.CompilerParams(
            vmem_limit_bytes=60 << 20, collective_id=0, has_side_effects=True
        ),
        name="exchange",
    )(
        counts,
        particle_velocity,
        drag_coef.reshape(128, 128),
        send_rows.reshape(256, 128),
        fluid_velocity.reshape(3, 256, 512),
        porosity.reshape(256, 512),
        recv_cell.reshape(256, 128),
    )

    bricks = lax.all_to_all(staged, "brick", split_axis=0, concat_axis=0, tiled=True)
    ordered = lax.sort(
        [part.reshape(-1) for part in (key, drag, p0, p1, p2)], num_keys=1, is_stable=False
    )
    f0, f1, f2, slot, net = pl.pallas_call(
        functools.partial(brick_kernel, width=256, group=8),
        out_shape=(
            square, square, square,
            jax.ShapeDtypeStruct((256, 128), I32),
            jax.ShapeDtypeStruct((8, 3, 32, 512), F32),
        ),
        in_specs=[smem] + [hbm] * 7,
        out_specs=(vmem,) * 4 + (hbm,),
        scratch_shapes=[
            pltpu.VMEM((256, 128), I32),
            pltpu.VMEM((256, 128), F32),
            pltpu.VMEM((256, 128), F32),
            pltpu.VMEM((256, 128), F32),
            pltpu.VMEM((256, 128), F32),
            pltpu.VMEM((8, 136, 512), F32),
            pltpu.VMEM((2, 128, 512), F32),
            pltpu.VMEM((8, 3, 32, 512), F32),
            pltpu.VMEM((10, 4, 48, 512), F32),
            pltpu.VMEM((8, 192, 256), BF16),
            pltpu.VMEM((8, 144, 256), F32),
            pltpu.SemaphoreType.DMA((7,)),
            pltpu.SemaphoreType.DMA((4,)),
        ],
        compiler_params=params,
        name="brick_forces",
    )(starts, *[part.reshape(256, 128) for part in ordered], bricks, zhalo)

    returned = lax.all_to_all(net, "brick", split_axis=0, concat_axis=0, tiled=True)
    back = lax.sort([part.reshape(-1) for part in (slot, f0, f1, f2)], num_keys=1, is_stable=False)
    slot_force = jnp.stack(back[1:])
    returned = jnp.swapaxes(returned, 0, 1).reshape(fluid_velocity.shape)
    new_velocity = fluid_velocity + time_step * returned / porosity
    return (new_velocity, slot_force)


def solution(mesh):
    placed = (
        P(None, ("slab", "brick"), None, None),
        P(("slab", "brick"), None, None),
        P(None, ("slab", "brick")),
        P(("slab", "brick")),
        P(("slab", "brick")),
        P(("slab", "brick")),
        P(("slab", "brick")),
    )
    return jax.shard_map(
        per_device,
        mesh=mesh,
        in_specs=placed,
        out_specs=(P(None, ("slab", "brick"), None, None), P(None, ("slab", "brick"))),
        check_vma=False,
    )
```

```python
import functools

import jax
import jax.numpy as jnp
from jax import lax
from jax.experimental import pallas as pl
from jax.experimental.pallas import tpu as pltpu
from jax.sharding import PartitionSpec as P

time_step = 0.05
F32, BF16, I32 = jnp.float32, jnp.bfloat16, jnp.int32
LAST = 2**31 - 1


def split3(x):
    high = x.astype(BF16)
    rest = x - high.astype(F32)
    mid = rest.astype(BF16)
    low = (rest - mid.astype(F32)).astype(BF16)
    return high, mid, low


def exchange_kernel(
    counts_ref, pv_hbm, coef_hbm, rows_hbm, u_hbm, frac_hbm, cell_hbm,
    stage_hbm, starts_ref, key_ref, p0_ref, p1_ref, p2_ref, drag_ref,
    pv_ref, coef_ref, rows_ref, u_ref, frac_ref, cell_ref, particles,
    stage, table, packed, arrived_ref, load_sem, stage_sem, part_send, part_recv, *, cap, group,
):
    pairs = (
        (u_hbm, u_ref), (frac_hbm, frac_ref), (pv_hbm, pv_ref), (coef_hbm, coef_ref), (rows_hbm, rows_ref),
        (cell_hbm, cell_ref),
    )
    loads = [pltpu.make_async_copy(source, target, load_sem.at[i]) for i, (source, target) in enumerate(pairs)]
    for load in loads:
        load.start()
    n_slab, n_brick = lax.axis_size("slab"), lax.axis_size("brick")
    devices = n_slab * n_brick
    slab, brick = lax.axis_index("slab"), lax.axis_index("brick")
    me = slab * n_brick + brick
    mesh_id = pl.DeviceIdType.MESH

    def coords(d):
        return (d // n_brick, d % n_brick)

    barrier = pltpu.get_barrier_semaphore()

    def greet(j, carry):
        pl.semaphore_signal(barrier, inc=1, device_id=coords((me + j) % devices), device_id_type=mesh_id)
        return carry

    lax.fori_loop(1, devices, greet, 0)

    loads[0].wait()
    loads[1].wait()
    for c in range(4):
        for b in range(8):
            field = frac_ref[b * 32 : (b + 1) * 32, :] if c == 3 else u_ref[c, b * 32 : (b + 1) * 32, :]
            stage[b, c * 32 : (c + 1) * 32, :] = field
            if b < 7:
                stage[b + 1, 128 + c : 129 + c, :] = field[31:32]
            if b > 0:
                stage[b - 1, 132 + c : 133 + c, :] = field[0:1]
        stage[0, 128 + c : 129 + c, :] = jnp.zeros((1, 512), F32)
        stage[7, 132 + c : 133 + c, :] = jnp.zeros((1, 512), F32)
    saved = pltpu.make_async_copy(stage, stage_hbm, stage_sem)
    saved.start()
    for load in loads[2:]:
        load.wait()
    for l in range(128):
        part = pv_ref[:, l * 128 : (l + 1) * 128]
        for c in range(3):
            particles[c, l : l + 1, :] = part[c : c + 1]
    for c in range(4):
        whole = coef_ref[...] if c == 3 else particles[c]
        halves = jnp.concatenate([whole[:64], whole[64:]], axis=1)
        for p, piece in enumerate(split3(halves)):
            table[p * 256 + c * 64 : p * 256 + (c + 1) * 64, :] = piece

    pl.semaphore_wait(barrier, devices - 1)

    r_iota = lax.broadcasted_iota(I32, (256, cap), 0).astype(F32).astype(BF16)
    one, zero = jnp.ones((), BF16), jnp.zeros((), BF16)
    l_iota = lax.broadcasted_iota(I32, (64, cap), 0)
    k_iota = lax.broadcasted_iota(I32, (1, cap), 1)

    def pick(to):
        onehots, planes, gots, picked = [], [], [], []
        for t in to:
            row = jnp.concatenate([rows_ref[pl.ds(2 * t, 1), :], rows_ref[pl.ds(2 * t + 1, 1), :]], axis=1)
            r = (row & 127) + ((row >> 13) << 7)
            onehots.append(jnp.where(r_iota == r.astype(F32).astype(BF16), one, zero))
            planes.append((row >> 7) & 63)
        for onehot in onehots:
            gots.append(jnp.dot(table[...], onehot, preferred_element_type=F32))
        slot = (me * cap + k_iota).astype(F32)
        for t, got, l in zip(to, gots, planes):
            got = got[:256] + (got[256:512] + got[512:])
            mask = l_iota == l
            live = k_iota < counts_ref[t]
            values = []
            for c in range(4):
                value = jnp.sum(jnp.where(mask, got[c * 64 : (c + 1) * 64], 0.0), axis=0, keepdims=True)
                if c == 0:
                    value = jnp.where(live, value, slot)
                if c == 3:
                    value = jnp.where(live, value, 0.0)
                values += [value[:, :128], value[:, 128:]]
            picked.append(jnp.concatenate(values, axis=0))
        return picked

    def parcel(t):
        return pltpu.make_async_remote_copy(
            src_ref=packed.at[t], dst_ref=arrived_ref.at[me], send_sem=part_send, recv_sem=part_recv,
            device_id=coords(t), device_id_type=mesh_id,
        )

    def some(i, carry):
        to = [(me + 1 + i * group + j) % devices for j in range(group)]
        picked = pick(to)
        for t, value in zip(to, picked):
            packed[t] = value
        for t in to:
            parcel(t).start()
        return carry

    lax.fori_loop(0, devices // group - 1, some, 0)
    to = [(me + 1 + devices - group + j) % devices for j in range(group)]
    picked = pick(to)
    for t, value in zip(to[:-1], picked):
        packed[t] = value
    arrived_ref[me] = picked[-1]
    for t in to[:-1]:
        parcel(t).start()

    rest = pltpu.make_async_remote_copy(
        src_ref=packed.at[pl.ds(0, devices - 1)], dst_ref=arrived_ref.at[pl.ds(0, devices - 1)],
        send_sem=part_send, recv_sem=part_recv, device_id=coords((me + 1) % devices), device_id_type=mesh_id,
    )
    rest.wait_send()
    rest.wait_recv()
    saved.wait()

    tiles = cell_ref.shape[0] // 8
    place = lax.broadcasted_iota(I32, (8, 128), 0) * 128 + lax.broadcasted_iota(I32, (8, 128), 1)

    def keys(j, sums):
        parts = [arrived_ref[4 * j + i] for i in range(4)]
        rows = pl.ds(pl.multiple_of(8 * j, 8), 8)
        for c, ref in enumerate((p0_ref, p1_ref, p2_ref, drag_ref)):
            value = jnp.concatenate([part[2 * c : 2 * c + 2] for part in parts], axis=0)
            ref[rows, :] = value
        live = value != 0.0
        cell = cell_ref[rows, :]
        block = cell >> 12
        slot = j * 1024 + place
        key = ((block - 16) << 27) + (slot << 12) + (cell & 4095)
        key_ref[rows, :] = jnp.where(live, key, LAST)
        block = jnp.where(live, block, 32)
        return tuple(s + jnp.where(block < b + 1, 1, 0) for b, s in enumerate(sums))

    sums = lax.fori_loop(0, tiles, keys, tuple(jnp.zeros((8, 128), I32) for _ in range(32)))
    tail = (cell_ref[tiles * 8 - 8 :, :] == 131071) & (drag_ref[tiles * 8 - 8 :, :] != 0.0) & (place == 1023)
    starts_ref[0] = 0
    for b in range(32):
        starts_ref[b + 1] = jnp.sum(sums[b])
    starts_ref[32] = jnp.where(jnp.sum(jnp.where(tail, 1, 0)) > 0, tiles * 1024, starts_ref[32])


def brick_kernel(
    starts_ref, key_ref, coef_ref, p0_ref, p1_ref, p2_ref, bricks_ref,
    f0_ref, f1_ref, f2_ref, slot_ref, sum_ref, table, deposit, *, width, group,
):
    rows = key_ref.shape[0]
    n = width // 128
    force_refs = (f0_ref, f1_ref, f2_ref)
    for ref in force_refs:
        ref[...] = jnp.zeros_like(ref)
    slot_ref[...] = jnp.where(coef_ref[...] != 0.0, (key_ref[...] >> 12) & 32767, p0_ref[...].astype(I32))

    r_iota = lax.broadcasted_iota(I32, (256, width), 0)
    l_iota = lax.broadcasted_iota(I32, (16, width), 0)
    r_iota = r_iota.astype(F32).astype(BF16)
    l_bf = l_iota.astype(F32).astype(BF16)
    p_iota = lax.broadcasted_iota(I32, (1, width), 1)
    one, zero = jnp.ones((), BF16), jnp.zeros((), BF16)

    def blocks(g, carry):
        bs = [g * group + i for i in range(group)]
        row0s, counts = [], []
        for i, b in enumerate(bs):
            z, q = b // 4, b % 4
            x8 = pl.multiple_of(q * 8, 8)
            for c in range(4):
                centre = bricks_ref[z, pl.ds(pl.multiple_of(c * 32 + x8, 8), 8), :]
                for p, piece in enumerate(split3(centre)):
                    at = p * 64 + c * 16
                    table[i, at : at + 16, :] = jnp.concatenate([piece[:, :256], piece[:, 256:]], axis=0)
            deposit[i] = jnp.zeros(deposit.shape[1:], F32)
            first, end = starts_ref[b], starts_ref[b + 1]
            row0 = first // 128
            row0s.append(row0)
            counts.append(jnp.where(end > first, (end - row0 * 128 + width - 1) // width, 0))
        windows = counts[0]
        for c in counts[1:]:
            windows = jnp.maximum(windows, c)

        def window(w, inner):
            ats, oh, valids, ls, gots = [], [], [], [], []

            def line(ref, at):
                return jnp.concatenate([ref[pl.ds(at + k, 1), :] for k in range(n)], axis=1)

            for i, b in enumerate(bs):
                row = row0s[i] + w * n
                at = jnp.minimum(row, rows - n)
                key = line(key_ref, at)
                valid = ((key >> 27) + 16 == b) & (p_iota >= (row - at) * 128)
                r = jnp.where(valid, key & 255, -1)
                l = ((key >> 9) & 7) + ((key >> 8) & 1) * 8
                ats.append(at)
                oh.append(jnp.where(r_iota == r.astype(F32).astype(BF16), one, zero))
                valids.append(valid)
                ls.append(l)
            for i in range(group):
                gots.append(jnp.dot(table[i], oh[i], preferred_element_type=F32))
            spreads = []
            forces = []
            for i in range(group):
                got = gots[i]
                got = got[:64] + (got[64:128] + got[128:])
                mask = l_iota == ls[i]
                u = [
                    jnp.sum(jnp.where(mask, got[c * 16 : (c + 1) * 16], 0.0), axis=0, keepdims=True) for c in range(4)
                ]
                frac = jnp.where(valids[i], u[3], 1.0)
                beta = line(coef_ref, ats[i]) * (1.0 - frac) / (frac * frac)
                fs = [
                    jnp.where(valids[i], beta * (u[c] - line(ref, ats[i])), 0.0)
                    for c, ref in enumerate((p0_ref, p1_ref, p2_ref))
                ]
                forces.append(fs)
                split = [split3(f) for f in fs]
                low_mask = l_bf == ls[i].astype(F32).astype(BF16)
                spreads.append(
                    jnp.concatenate(
                        [jnp.where(low_mask, split[c][p], zero) for p in range(3) for c in range(3)], axis=0
                    )
                )
            for i in range(group):
                deposit[i] += lax.dot_general(
                    spreads[i], oh[i], (((1,), (1,)), ((), ())), preferred_element_type=F32
                )
            for i in range(group):
                for c in range(3):
                    for k in range(n):
                        force_refs[c][pl.ds(ats[i] + k, 1), :] += forces[i][c][:, k * 128 : (k + 1) * 128]
            return inner

        lax.fori_loop(0, windows, window, 0)

        for i, b in enumerate(bs):
            z, q = b // 4, b % 4
            x8 = pl.multiple_of(q * 8, 8)
            summed = deposit[i, 0:48, :] + (deposit[i, 48:96, :] + deposit[i, 96:144, :])
            for c in range(3):
                left, right = summed[c * 16 : c * 16 + 8], summed[c * 16 + 8 : c * 16 + 16]
                sum_ref[z, c, pl.ds(x8, 8), :] = jnp.concatenate([left, right], axis=1)
        return carry

    lax.fori_loop(0, 32 // group, blocks, 0)


def viscous_kernel(bricks_ref, below_ref, above_ref, sum_ref, net_ref, padded):
    for c in range(4):
        own = slice(c * 32, (c + 1) * 32)
        for z in range(8):
            padded[z + 1, c, 8:40, :] = bricks_ref[z, own, :]
            padded[z + 1, c, 7:8, :] = bricks_ref[z, 128 + c : 129 + c, :]
            padded[z + 1, c, 40:41, :] = bricks_ref[z, 132 + c : 133 + c, :]
        padded[0, c, 8:40, :] = below_ref[own, :]
        padded[9, c, 8:40, :] = above_ref[own, :]
    y_iota = lax.broadcasted_iota(I32, (8, 512), 1)

    def plane(z, carry):
        for x8 in range(0, 32, 8):
            tall = [padded[z + 1, c, x8 : x8 + 24, :] for c in range(4)]
            below = [padded[z, c, x8 + 8 : x8 + 16, :] for c in range(4)]
            above = [padded[z + 2, c, x8 + 8 : x8 + 16, :] for c in range(4)]
            centre = [t[8:16] for t in tall]
            sides = [above, below, [t[9:17] for t in tall], [t[7:15] for t in tall]]
            sides.append([jnp.where(y_iota == 511, 0.0, pltpu.roll(t, 511, 1)) for t in centre])
            sides.append([jnp.where(y_iota == 0, 0.0, pltpu.roll(t, 1, 1)) for t in centre])
            total = [jnp.zeros((8, 512), F32) for _ in range(3)]
            for side in sides:
                weight = 0.5 * (centre[3] + side[3])
                for c in range(3):
                    total[c] = total[c] + weight * (side[c] - centre[c])
            for c in range(3):
                net_ref[z, c, x8 : x8 + 8, :] = total[c] - sum_ref[z, c, x8 : x8 + 8, :]
        return carry

    lax.fori_loop(0, 8, plane, 0)


def per_device(
    fluid_velocity, porosity, particle_velocity, drag_coef, send_rows, counts, recv_cell
):
    n_slab = lax.axis_size("slab")
    n_brick = lax.axis_size("brick")
    devices = n_slab * n_brick
    cap = send_rows.shape[0] // devices
    vmem = pl.BlockSpec(memory_space=pltpu.VMEM)
    smem = pl.BlockSpec(memory_space=pltpu.SMEM)
    params = pltpu.CompilerParams(vmem_limit_bytes=32 << 20)
    square = jax.ShapeDtypeStruct((256, 128), F32)
    hbm = pl.BlockSpec(memory_space=pl.ANY)
    staged, starts, key, p0, p1, p2, drag = pl.pallas_call(
        functools.partial(exchange_kernel, cap=cap, group=8),
        out_shape=(
            jax.ShapeDtypeStruct((8, 136, 512), F32),
            jax.ShapeDtypeStruct((33,), I32),
            jax.ShapeDtypeStruct((256, 128), I32),
            square, square, square, square,
        ),
        in_specs=[smem] + [hbm] * 6,
        out_specs=(hbm, smem) + (vmem,) * 5,
        scratch_shapes=[
            pltpu.VMEM((3, 16384), F32),
            pltpu.VMEM((128, 128), F32),
            pltpu.VMEM((256, 128), I32),
            pltpu.VMEM((3, 256, 512), F32),
            pltpu.VMEM((256, 512), F32),
            pltpu.VMEM((256, 128), I32),
            pltpu.VMEM((3, 128, 128), F32),
            pltpu.VMEM((8, 136, 512), F32),
            pltpu.VMEM((768, 256), BF16),
            pltpu.VMEM((devices, 8, 128), F32),
            pltpu.VMEM((devices, 8, 128), F32),
            pltpu.SemaphoreType.DMA((6,)),
            pltpu.SemaphoreType.DMA,
            pltpu.SemaphoreType.DMA,
            pltpu.SemaphoreType.DMA,
        ],
        compiler_params=pltpu.CompilerParams(
            vmem_limit_bytes=60 << 20, collective_id=0, has_side_effects=True
        ),
        name="exchange",
    )(
        counts,
        particle_velocity,
        drag_coef.reshape(128, 128),
        send_rows.reshape(256, 128),
        fluid_velocity.reshape(3, 256, 512),
        porosity.reshape(256, 512),
        recv_cell.reshape(256, 128),
    )

    bricks = lax.all_to_all(staged, "brick", split_axis=0, concat_axis=0, tiled=True)
    ordered = lax.sort(
        [part.reshape(-1) for part in (key, drag, p0, p1, p2)], num_keys=1, is_stable=False
    )
    below = lax.ppermute(bricks[7, :128], "slab", [(i, i + 1) for i in range(n_slab - 1)])
    above = lax.ppermute(bricks[0, :128], "slab", [(i + 1, i) for i in range(n_slab - 1)])
    f0, f1, f2, slot, summed = pl.pallas_call(
        functools.partial(brick_kernel, width=256, group=8),
        out_shape=(
            square, square, square,
            jax.ShapeDtypeStruct((256, 128), I32),
            jax.ShapeDtypeStruct((8, 3, 32, 512), F32),
        ),
        in_specs=[smem] + [vmem] * 6,
        out_specs=(vmem,) * 5,
        scratch_shapes=[pltpu.VMEM((8, 192, 256), BF16), pltpu.VMEM((8, 144, 256), F32)],
        compiler_params=params,
        cost_estimate=pl.CostEstimate(flops=30_000_000_000, bytes_accessed=6_000_000, transcendentals=0),
        name="brick_forces",
    )(starts, *[part.reshape(256, 128) for part in ordered], bricks)
    net = pl.pallas_call(
        viscous_kernel,
        out_shape=jax.ShapeDtypeStruct((8, 3, 32, 512), F32),
        in_specs=[vmem] * 4,
        out_specs=vmem,
        scratch_shapes=[pltpu.VMEM((10, 4, 48, 512), F32)],
        compiler_params=params,
        name="viscous",
    )(bricks, below, above, summed)

    slot, f0, f1, f2, net = lax.optimization_barrier((slot, f0, f1, f2, net))
    returned = lax.all_to_all(net, "brick", split_axis=0, concat_axis=0, tiled=True)
    back = lax.sort([part.reshape(-1) for part in (slot, f0, f1, f2)], num_keys=1, is_stable=False)
    slot_force = jnp.stack(back[1:])
    returned = jnp.swapaxes(returned, 0, 1).reshape(fluid_velocity.shape)
    new_velocity = fluid_velocity + time_step * returned / porosity
    return (new_velocity, slot_force)


def solution(mesh):
    placed = (
        P(None, ("slab", "brick"), None, None),
        P(("slab", "brick"), None, None),
        P(None, ("slab", "brick")),
        P(("slab", "brick")),
        P(("slab", "brick")),
        P(("slab", "brick")),
        P(("slab", "brick")),
    )
    return jax.shard_map(
        per_device,
        mesh=mesh,
        in_specs=placed,
        out_specs=(P(None, ("slab", "brick"), None, None), P(None, ("slab", "brick"))),
        check_vma=False,
    )
```

```python
import functools

import jax
import jax.numpy as jnp
from jax import lax
from jax.experimental import pallas as pl
from jax.experimental.pallas import tpu as pltpu
from jax.sharding import PartitionSpec as P

time_step = 0.05
F32, BF16, I32 = jnp.float32, jnp.bfloat16, jnp.int32
LAST = 2**31 - 1


def split3(x):
    high = x.astype(BF16)
    rest = x - high.astype(F32)
    mid = rest.astype(BF16)
    low = (rest - mid.astype(F32)).astype(BF16)
    return high, mid, low


def exchange_kernel(
    counts_ref, pv_hbm, coef_hbm, rows_hbm, u_hbm, frac_hbm, cell_hbm,
    stage_hbm, rest_ref, starts_ref, key_ref, p0_ref, p1_ref, p2_ref, drag_ref,
    pv_ref, coef_ref, rows_ref, u_ref, frac_ref, cell_ref, particles,
    stage, table, packed, arrived_ref, load_sem, stage_sem, part_send, part_recv, rest_send, rest_recv,
    *, cap, group,
):
    pairs = (
        (u_hbm, u_ref), (frac_hbm, frac_ref), (pv_hbm, pv_ref), (coef_hbm, coef_ref), (rows_hbm, rows_ref),
        (cell_hbm, cell_ref),
    )
    loads = [pltpu.make_async_copy(source, target, load_sem.at[i]) for i, (source, target) in enumerate(pairs)]
    for load in loads:
        load.start()
    n_slab, n_brick = lax.axis_size("slab"), lax.axis_size("brick")
    devices = n_slab * n_brick
    slab, brick = lax.axis_index("slab"), lax.axis_index("brick")
    me = slab * n_brick + brick
    mesh_id = pl.DeviceIdType.MESH

    def coords(d):
        return (d // n_brick, d % n_brick)

    barrier = pltpu.get_barrier_semaphore()

    def greet(j, carry):
        pl.semaphore_signal(barrier, inc=1, device_id=coords((me + j) % devices), device_id_type=mesh_id)
        return carry

    lax.fori_loop(1, devices, greet, 0)

    loads[0].wait()
    loads[1].wait()
    for c in range(4):
        for b in range(8):
            field = frac_ref[b * 32 : (b + 1) * 32, :] if c == 3 else u_ref[c, b * 32 : (b + 1) * 32, :]
            stage[b, c * 32 : (c + 1) * 32, :] = field
            if b < 7:
                stage[b + 1, 128 + c : 129 + c, :] = field[31:32]
            if b > 0:
                stage[b - 1, 132 + c : 133 + c, :] = field[0:1]
        stage[0, 128 + c : 129 + c, :] = jnp.zeros((1, 512), F32)
        stage[7, 132 + c : 133 + c, :] = jnp.zeros((1, 512), F32)
    saved = pltpu.make_async_copy(stage.at[:, pl.ds(0, 96)], stage_hbm, stage_sem)
    saved.start()
    for load in loads[2:]:
        load.wait()
    for l in range(128):
        part = pv_ref[:, l * 128 : (l + 1) * 128]
        for c in range(3):
            particles[c, l : l + 1, :] = part[c : c + 1]
    for c in range(4):
        whole = coef_ref[...] if c == 3 else particles[c]
        halves = jnp.concatenate([whole[:64], whole[64:]], axis=1)
        for p, piece in enumerate(split3(halves)):
            table[p * 256 + c * 64 : p * 256 + (c + 1) * 64, :] = piece

    r_iota = lax.broadcasted_iota(I32, (256, cap), 0).astype(F32).astype(BF16)
    one, zero = jnp.ones((), BF16), jnp.zeros((), BF16)
    l_iota = lax.broadcasted_iota(I32, (64, cap), 0)
    k_iota = lax.broadcasted_iota(I32, (1, cap), 1)

    def pick(to):
        onehots, planes, gots, picked = [], [], [], []
        for t in to:
            row = jnp.concatenate([rows_ref[pl.ds(2 * t, 1), :], rows_ref[pl.ds(2 * t + 1, 1), :]], axis=1)
            r = (row & 127) + ((row >> 13) << 7)
            onehots.append(jnp.where(r_iota == r.astype(F32).astype(BF16), one, zero))
            planes.append((row >> 7) & 63)
        for onehot in onehots:
            gots.append(jnp.dot(table[...], onehot, preferred_element_type=F32))
        slot = (me * cap + k_iota).astype(F32)
        for t, got, l in zip(to, gots, planes):
            got = got[:256] + (got[256:512] + got[512:])
            mask = l_iota == l
            live = k_iota < counts_ref[t]
            values = []
            for c in range(4):
                value = jnp.sum(jnp.where(mask, got[c * 64 : (c + 1) * 64], 0.0), axis=0, keepdims=True)
                if c == 0:
                    value = jnp.where(live, value, slot)
                if c == 3:
                    value = jnp.where(live, value, 0.0)
                values += [value[:, :128], value[:, 128:]]
            picked.append(jnp.concatenate(values, axis=0))
        return picked

    def parcel(t):
        return pltpu.make_async_remote_copy(
            src_ref=packed.at[t], dst_ref=arrived_ref.at[me], send_sem=part_send, recv_sem=part_recv,
            device_id=coords(t), device_id_type=mesh_id,
        )

    def other(j):
        to = (brick + j) % n_brick
        return pltpu.make_async_remote_copy(
            src_ref=stage.at[to, pl.ds(96, 40)], dst_ref=rest_ref.at[brick], send_sem=rest_send.at[to],
            recv_sem=rest_recv.at[brick], device_id=(slab, to), device_id_type=mesh_id,
        )

    def fill(i, carry):
        to = [(me + 1 + i * group + j) % devices for j in range(group)]
        for t, value in zip(to, pick(to)):
            packed[t] = value
        return carry

    def send(i, carry):
        for j in range(group):
            parcel((me + 1 + i * group + j) % devices).start()
        return carry

    def some(i, carry):
        return send(i, fill(i, carry))

    rest_ref[brick] = stage[brick, 96:136]
    lax.fori_loop(0, 2, fill, 0)
    pl.semaphore_wait(barrier, devices - 1)
    for j in range(1, 8):
        other(j).start()
    lax.fori_loop(0, 2, send, 0)
    lax.fori_loop(2, devices // group - 1, some, 0)
    to = [(me + 1 + devices - group + j) % devices for j in range(group)]
    picked = pick(to)
    for t, value in zip(to[:-1], picked):
        packed[t] = value
    arrived_ref[me] = picked[-1]
    for t in to[:-1]:
        parcel(t).start()

    rest = pltpu.make_async_remote_copy(
        src_ref=packed.at[pl.ds(0, devices - 1)], dst_ref=arrived_ref.at[pl.ds(0, devices - 1)],
        send_sem=part_send, recv_sem=part_recv, device_id=coords((me + 1) % devices), device_id_type=mesh_id,
    )
    rest.wait_send()
    rest.wait_recv()
    saved.wait()
    for j in range(1, 8):
        other(j).wait_send()
        source = (brick + j) % n_brick
        pltpu.make_async_remote_copy(
            src_ref=stage.at[source, pl.ds(96, 40)], dst_ref=rest_ref.at[source], send_sem=rest_send.at[source],
            recv_sem=rest_recv.at[source], device_id=(slab, source), device_id_type=mesh_id,
        ).wait_recv()

    tiles = cell_ref.shape[0] // 8
    place = lax.broadcasted_iota(I32, (8, 128), 0) * 128 + lax.broadcasted_iota(I32, (8, 128), 1)

    def keys(j, sums):
        parts = [arrived_ref[4 * j + i] for i in range(4)]
        rows = pl.ds(pl.multiple_of(8 * j, 8), 8)
        for c, ref in enumerate((p0_ref, p1_ref, p2_ref, drag_ref)):
            value = jnp.concatenate([part[2 * c : 2 * c + 2] for part in parts], axis=0)
            ref[rows, :] = value
        live = value != 0.0
        cell = cell_ref[rows, :]
        block = cell >> 12
        slot = j * 1024 + place
        key = ((block - 16) << 27) + (slot << 12) + (cell & 4095)
        key_ref[rows, :] = jnp.where(live, key, LAST)
        block = jnp.where(live, block, 32)
        return tuple(s + jnp.where(block < b + 1, 1, 0) for b, s in enumerate(sums))

    sums = lax.fori_loop(0, tiles, keys, tuple(jnp.zeros((8, 128), I32) for _ in range(32)))
    tail = (cell_ref[tiles * 8 - 8 :, :] == 131071) & (drag_ref[tiles * 8 - 8 :, :] != 0.0) & (place == 1023)
    starts_ref[0] = 0
    for b in range(32):
        starts_ref[b + 1] = jnp.sum(sums[b])
    starts_ref[32] = jnp.where(jnp.sum(jnp.where(tail, 1, 0)) > 0, tiles * 1024, starts_ref[32])


def brick_kernel(
    starts_ref, key_ref, coef_ref, p0_ref, p1_ref, p2_ref, bricks_ref, rest_ref,
    f0_ref, f1_ref, f2_ref, slot_ref, sum_ref, table, deposit, *, width, group,
):
    rows = key_ref.shape[0]
    n = width // 128
    force_refs = (f0_ref, f1_ref, f2_ref)
    for ref in force_refs:
        ref[...] = jnp.zeros_like(ref)
    slot_ref[...] = jnp.where(coef_ref[...] != 0.0, (key_ref[...] >> 12) & 32767, p0_ref[...].astype(I32))

    r_iota = lax.broadcasted_iota(I32, (256, width), 0)
    l_iota = lax.broadcasted_iota(I32, (16, width), 0)
    r_iota = r_iota.astype(F32).astype(BF16)
    l_bf = l_iota.astype(F32).astype(BF16)
    p_iota = lax.broadcasted_iota(I32, (1, width), 1)
    one, zero = jnp.ones((), BF16), jnp.zeros((), BF16)

    def blocks(g, carry):
        bs = [g * group + i for i in range(group)]
        row0s, counts = [], []
        for i, b in enumerate(bs):
            z, q = b // 4, b % 4
            x8 = pl.multiple_of(q * 8, 8)
            for c in range(4):
                ref, at = (rest_ref, x8) if c == 3 else (bricks_ref, pl.multiple_of(c * 32 + x8, 8))
                centre = ref[z, pl.ds(at, 8), :]
                for p, piece in enumerate(split3(centre)):
                    at = p * 64 + c * 16
                    table[i, at : at + 16, :] = jnp.concatenate([piece[:, :256], piece[:, 256:]], axis=0)
            deposit[i] = jnp.zeros(deposit.shape[1:], F32)
            first, end = starts_ref[b], starts_ref[b + 1]
            row0 = first // 128
            row0s.append(row0)
            counts.append(jnp.where(end > first, (end - row0 * 128 + width - 1) // width, 0))
        windows = counts[0]
        for c in counts[1:]:
            windows = jnp.maximum(windows, c)

        def window(w, inner):
            ats, oh, valids, ls, gots = [], [], [], [], []

            def line(ref, at):
                return jnp.concatenate([ref[pl.ds(at + k, 1), :] for k in range(n)], axis=1)

            for i, b in enumerate(bs):
                row = row0s[i] + w * n
                at = jnp.minimum(row, rows - n)
                key = line(key_ref, at)
                valid = ((key >> 27) + 16 == b) & (p_iota >= (row - at) * 128)
                r = jnp.where(valid, key & 255, -1)
                l = ((key >> 9) & 7) + ((key >> 8) & 1) * 8
                ats.append(at)
                oh.append(jnp.where(r_iota == r.astype(F32).astype(BF16), one, zero))
                valids.append(valid)
                ls.append(l)
            for i in range(group):
                gots.append(jnp.dot(table[i], oh[i], preferred_element_type=F32))
            spreads = []
            forces = []
            for i in range(group):
                got = gots[i]
                got = got[:64] + (got[64:128] + got[128:])
                mask = l_iota == ls[i]
                u = [
                    jnp.sum(jnp.where(mask, got[c * 16 : (c + 1) * 16], 0.0), axis=0, keepdims=True) for c in range(4)
                ]
                frac = jnp.where(valids[i], u[3], 1.0)
                beta = line(coef_ref, ats[i]) * (1.0 - frac) / (frac * frac)
                fs = [
                    jnp.where(valids[i], beta * (u[c] - line(ref, ats[i])), 0.0)
                    for c, ref in enumerate((p0_ref, p1_ref, p2_ref))
                ]
                forces.append(fs)
                split = [split3(f) for f in fs]
                low_mask = l_bf == ls[i].astype(F32).astype(BF16)
                spreads.append(
                    jnp.concatenate(
                        [jnp.where(low_mask, split[c][p], zero) for p in range(3) for c in range(3)], axis=0
                    )
                )
            for i in range(group):
                deposit[i] += lax.dot_general(
                    spreads[i], oh[i], (((1,), (1,)), ((), ())), preferred_element_type=F32
                )
            for i in range(group):
                for c in range(3):
                    for k in range(n):
                        force_refs[c][pl.ds(ats[i] + k, 1), :] += forces[i][c][:, k * 128 : (k + 1) * 128]
            return inner

        lax.fori_loop(0, windows, window, 0)

        for i, b in enumerate(bs):
            z, q = b // 4, b % 4
            x8 = pl.multiple_of(q * 8, 8)
            summed = deposit[i, 0:48, :] + (deposit[i, 48:96, :] + deposit[i, 96:144, :])
            for c in range(3):
                left, right = summed[c * 16 : c * 16 + 8], summed[c * 16 + 8 : c * 16 + 16]
                sum_ref[z, c, pl.ds(x8, 8), :] = jnp.concatenate([left, right], axis=1)
        return carry

    lax.fori_loop(0, 32 // group, blocks, 0)


def viscous_kernel(bricks_ref, rest_ref, below_ref, above_ref, sum_ref, net_ref, padded):
    for c in range(4):
        own = slice(c * 32, (c + 1) * 32)
        for z in range(8):
            padded[z + 1, c, 8:40, :] = rest_ref[z, 0:32, :] if c == 3 else bricks_ref[z, own, :]
            padded[z + 1, c, 7:8, :] = rest_ref[z, 32 + c : 33 + c, :]
            padded[z + 1, c, 40:41, :] = rest_ref[z, 36 + c : 37 + c, :]
        padded[0, c, 8:40, :] = below_ref[own, :]
        padded[9, c, 8:40, :] = above_ref[own, :]
    y_iota = lax.broadcasted_iota(I32, (8, 512), 1)

    def plane(z, carry):
        for x8 in range(0, 32, 8):
            tall = [padded[z + 1, c, x8 : x8 + 24, :] for c in range(4)]
            below = [padded[z, c, x8 + 8 : x8 + 16, :] for c in range(4)]
            above = [padded[z + 2, c, x8 + 8 : x8 + 16, :] for c in range(4)]
            centre = [t[8:16] for t in tall]
            sides = [above, below, [t[9:17] for t in tall], [t[7:15] for t in tall]]
            sides.append([jnp.where(y_iota == 511, 0.0, pltpu.roll(t, 511, 1)) for t in centre])
            sides.append([jnp.where(y_iota == 0, 0.0, pltpu.roll(t, 1, 1)) for t in centre])
            total = [jnp.zeros((8, 512), F32) for _ in range(3)]
            for side in sides:
                weight = 0.5 * (centre[3] + side[3])
                for c in range(3):
                    total[c] = total[c] + weight * (side[c] - centre[c])
            for c in range(3):
                net_ref[z, c, x8 : x8 + 8, :] = total[c] - sum_ref[z, c, x8 : x8 + 8, :]
        return carry

    lax.fori_loop(0, 8, plane, 0)


def per_device(
    fluid_velocity, porosity, particle_velocity, drag_coef, send_rows, counts, recv_cell
):
    n_slab = lax.axis_size("slab")
    n_brick = lax.axis_size("brick")
    devices = n_slab * n_brick
    cap = send_rows.shape[0] // devices
    vmem = pl.BlockSpec(memory_space=pltpu.VMEM)
    smem = pl.BlockSpec(memory_space=pltpu.SMEM)
    params = pltpu.CompilerParams(vmem_limit_bytes=32 << 20)
    square = jax.ShapeDtypeStruct((256, 128), F32)
    hbm = pl.BlockSpec(memory_space=pl.ANY)
    staged, others, starts, key, p0, p1, p2, drag = pl.pallas_call(
        functools.partial(exchange_kernel, cap=cap, group=8),
        out_shape=(
            jax.ShapeDtypeStruct((8, 96, 512), F32),
            jax.ShapeDtypeStruct((8, 40, 512), F32),
            jax.ShapeDtypeStruct((33,), I32),
            jax.ShapeDtypeStruct((256, 128), I32),
            square, square, square, square,
        ),
        in_specs=[smem] + [hbm] * 6,
        out_specs=(hbm, vmem, smem) + (vmem,) * 5,
        scratch_shapes=[
            pltpu.VMEM((3, 16384), F32),
            pltpu.VMEM((128, 128), F32),
            pltpu.VMEM((256, 128), I32),
            pltpu.VMEM((3, 256, 512), F32),
            pltpu.VMEM((256, 512), F32),
            pltpu.VMEM((256, 128), I32),
            pltpu.VMEM((3, 128, 128), F32),
            pltpu.VMEM((8, 136, 512), F32),
            pltpu.VMEM((768, 256), BF16),
            pltpu.VMEM((devices, 8, 128), F32),
            pltpu.VMEM((devices, 8, 128), F32),
            pltpu.SemaphoreType.DMA((6,)),
            pltpu.SemaphoreType.DMA,
            pltpu.SemaphoreType.DMA,
            pltpu.SemaphoreType.DMA,
            pltpu.SemaphoreType.DMA((8,)),
            pltpu.SemaphoreType.DMA((8,)),
        ],
        compiler_params=pltpu.CompilerParams(
            vmem_limit_bytes=60 << 20, collective_id=0, has_side_effects=True
        ),
        name="exchange",
    )(
        counts,
        particle_velocity,
        drag_coef.reshape(128, 128),
        send_rows.reshape(256, 128),
        fluid_velocity.reshape(3, 256, 512),
        porosity.reshape(256, 512),
        recv_cell.reshape(256, 128),
    )

    bricks = lax.all_to_all(staged, "brick", split_axis=0, concat_axis=0, tiled=True)
    ordered = lax.sort(
        [part.reshape(-1) for part in (key, drag, p0, p1, p2)], num_keys=1, is_stable=False
    )
    top, bottom = [jnp.concatenate([bricks[z], others[z, :32]]) for z in (7, 0)]
    below = lax.ppermute(top, "slab", [(i, i + 1) for i in range(n_slab - 1)])
    above = lax.ppermute(bottom, "slab", [(i + 1, i) for i in range(n_slab - 1)])
    f0, f1, f2, slot, summed = pl.pallas_call(
        functools.partial(brick_kernel, width=256, group=8),
        out_shape=(
            square, square, square,
            jax.ShapeDtypeStruct((256, 128), I32),
            jax.ShapeDtypeStruct((8, 3, 32, 512), F32),
        ),
        in_specs=[smem] + [vmem] * 7,
        out_specs=(vmem,) * 5,
        scratch_shapes=[pltpu.VMEM((8, 192, 256), BF16), pltpu.VMEM((8, 144, 256), F32)],
        compiler_params=params,
        cost_estimate=pl.CostEstimate(flops=30_000_000_000, bytes_accessed=6_000_000, transcendentals=0),
        name="brick_forces",
    )(starts, *[part.reshape(256, 128) for part in ordered], bricks, others)
    net = pl.pallas_call(
        viscous_kernel,
        out_shape=jax.ShapeDtypeStruct((8, 3, 32, 512), F32),
        in_specs=[vmem] * 5,
        out_specs=vmem,
        scratch_shapes=[pltpu.VMEM((10, 4, 48, 512), F32)],
        compiler_params=params,
        name="viscous",
    )(bricks, others, below, above, summed)

    slot, f0, f1, f2, net = lax.optimization_barrier((slot, f0, f1, f2, net))
    returned = lax.all_to_all(net, "brick", split_axis=0, concat_axis=0, tiled=True)
    back = lax.sort([part.reshape(-1) for part in (slot, f0, f1, f2)], num_keys=1, is_stable=False)
    slot_force = jnp.stack(back[1:])
    returned = jnp.swapaxes(returned, 0, 1).reshape(fluid_velocity.shape)
    new_velocity = fluid_velocity + time_step * returned / porosity
    return (new_velocity, slot_force)


def solution(mesh):
    placed = (
        P(None, ("slab", "brick"), None, None),
        P(("slab", "brick"), None, None),
        P(None, ("slab", "brick")),
        P(("slab", "brick")),
        P(("slab", "brick")),
        P(("slab", "brick")),
        P(("slab", "brick")),
    )
    return jax.shard_map(
        per_device,
        mesh=mesh,
        in_specs=placed,
        out_specs=(P(None, ("slab", "brick"), None, None), P(None, ("slab", "brick"))),
        check_vma=False,
    )
```

```python
import functools

import jax
import jax.numpy as jnp
from jax import lax
from jax.experimental import pallas as pl
from jax.experimental.pallas import tpu as pltpu
from jax.sharding import PartitionSpec as P

time_step = 0.05
F32, BF16, I32 = jnp.float32, jnp.bfloat16, jnp.int32
LAST = 2**31 - 1


def split3(x):
    high = x.astype(BF16)
    rest = x - high.astype(F32)
    mid = rest.astype(BF16)
    low = (rest - mid.astype(F32)).astype(BF16)
    return high, mid, low


def exchange_kernel(
    counts_ref, pv_hbm, coef_hbm, rows_hbm, u_hbm, frac_hbm, cell_hbm,
    stage_hbm, rest_ref, starts_ref, key_ref, p0_ref, p1_ref, p2_ref, drag_ref,
    pv_ref, coef_ref, rows_ref, u_ref, frac_ref, cell_ref, particles,
    stage, table, packed, arrived_ref, load_sem, stage_sem, part_send, part_recv, rest_send, rest_recv,
    *, cap, group,
):
    pairs = (
        (u_hbm, u_ref), (frac_hbm, frac_ref), (pv_hbm, pv_ref), (coef_hbm, coef_ref), (rows_hbm, rows_ref),
        (cell_hbm, cell_ref),
    )
    loads = [pltpu.make_async_copy(source, target, load_sem.at[i]) for i, (source, target) in enumerate(pairs)]
    for load in loads:
        load.start()
    n_slab, n_brick = lax.axis_size("slab"), lax.axis_size("brick")
    devices = n_slab * n_brick
    slab, brick = lax.axis_index("slab"), lax.axis_index("brick")
    me = slab * n_brick + brick
    mesh_id = pl.DeviceIdType.MESH

    def coords(d):
        return (d // n_brick, d % n_brick)

    barrier = pltpu.get_barrier_semaphore()

    def greet(j, carry):
        pl.semaphore_signal(barrier, inc=1, device_id=coords((me + j) % devices), device_id_type=mesh_id)
        return carry

    lax.fori_loop(1, devices, greet, 0)

    loads[0].wait()
    loads[1].wait()
    for c in range(4):
        for b in range(8):
            field = frac_ref[b * 32 : (b + 1) * 32, :] if c == 3 else u_ref[c, b * 32 : (b + 1) * 32, :]
            stage[b, c * 32 : (c + 1) * 32, :] = field
            if b < 7:
                stage[b + 1, 128 + c : 129 + c, :] = field[31:32]
            if b > 0:
                stage[b - 1, 132 + c : 133 + c, :] = field[0:1]
        stage[0, 128 + c : 129 + c, :] = jnp.zeros((1, 512), F32)
        stage[7, 132 + c : 133 + c, :] = jnp.zeros((1, 512), F32)
    saved = pltpu.make_async_copy(stage.at[:, pl.ds(0, 96)], stage_hbm, stage_sem)
    saved.start()
    for load in loads[2:]:
        load.wait()
    for l in range(128):
        part = pv_ref[:, l * 128 : (l + 1) * 128]
        for c in range(3):
            particles[c, l : l + 1, :] = part[c : c + 1]
    for c in range(4):
        whole = coef_ref[...] if c == 3 else particles[c]
        halves = jnp.concatenate([whole[:64], whole[64:]], axis=1)
        for p, piece in enumerate(split3(halves)):
            table[p * 256 + c * 64 : p * 256 + (c + 1) * 64, :] = piece

    r_iota = lax.broadcasted_iota(I32, (256, cap), 0).astype(F32).astype(BF16)
    one, zero = jnp.ones((), BF16), jnp.zeros((), BF16)
    l_iota = lax.broadcasted_iota(I32, (64, cap), 0)
    k_iota = lax.broadcasted_iota(I32, (1, cap), 1)

    def pick(to):
        onehots, planes, gots, picked = [], [], [], []
        for t in to:
            row = jnp.concatenate([rows_ref[pl.ds(2 * t, 1), :], rows_ref[pl.ds(2 * t + 1, 1), :]], axis=1)
            r = (row & 127) + ((row >> 13) << 7)
            onehots.append(jnp.where(r_iota == r.astype(F32).astype(BF16), one, zero))
            planes.append((row >> 7) & 63)
        for onehot in onehots:
            gots.append(jnp.dot(table[...], onehot, preferred_element_type=F32))
        slot = (me * cap + k_iota).astype(F32)
        for t, got, l in zip(to, gots, planes):
            got = got[:256] + (got[256:512] + got[512:])
            mask = l_iota == l
            live = k_iota < counts_ref[t]
            values = []
            for c in range(4):
                value = jnp.sum(jnp.where(mask, got[c * 64 : (c + 1) * 64], 0.0), axis=0, keepdims=True)
                if c == 0:
                    value = jnp.where(live, value, slot)
                if c == 3:
                    value = jnp.where(live, value, 0.0)
                values += [value[:, :128], value[:, 128:]]
            picked.append(jnp.concatenate(values, axis=0))
        return picked

    def parcel(t):
        return pltpu.make_async_remote_copy(
            src_ref=packed.at[t], dst_ref=arrived_ref.at[me], send_sem=part_send, recv_sem=part_recv,
            device_id=coords(t), device_id_type=mesh_id,
        )

    def other(j):
        to = (brick + j) % n_brick
        return pltpu.make_async_remote_copy(
            src_ref=stage.at[to, pl.ds(96, 40)], dst_ref=rest_ref.at[brick], send_sem=rest_send.at[to],
            recv_sem=rest_recv.at[brick], device_id=(slab, to), device_id_type=mesh_id,
        )

    def fill(i, carry):
        to = [(me + 1 + i * group + j) % devices for j in range(group)]
        for t, value in zip(to, pick(to)):
            packed[t] = value
        return carry

    def send(i, carry):
        for j in range(group):
            parcel((me + 1 + i * group + j) % devices).start()
        return carry

    def some(i, carry):
        return send(i, fill(i, carry))

    rest_ref[brick] = stage[brick, 96:136]
    fill(0, 0)
    pl.semaphore_wait(barrier, devices - 1)
    for j in range(1, 8):
        other(j).start()
    send(0, 0)
    lax.fori_loop(1, devices // group - 1, some, 0)
    to = [(me + 1 + devices - group + j) % devices for j in range(group)]
    picked = pick(to)
    for t, value in zip(to[:-1], picked):
        packed[t] = value
    arrived_ref[me] = picked[-1]
    for t in to[:-1]:
        parcel(t).start()

    tiles = cell_ref.shape[0] // 8
    place = lax.broadcasted_iota(I32, (8, 128), 0) * 128 + lax.broadcasted_iota(I32, (8, 128), 1)

    def early(j, carry):
        rows = pl.ds(pl.multiple_of(8 * j, 8), 8)
        cell = cell_ref[rows, :]
        key_ref[rows, :] = (((cell >> 12) - 16) << 27) + ((j * 1024 + place) << 12) + (cell & 4095)
        return carry

    lax.fori_loop(0, tiles, early, 0, unroll=4)
    rest = pltpu.make_async_remote_copy(
        src_ref=packed.at[pl.ds(0, devices - 1)], dst_ref=arrived_ref.at[pl.ds(0, devices - 1)],
        send_sem=part_send, recv_sem=part_recv, device_id=coords((me + 1) % devices), device_id_type=mesh_id,
    )
    rest.wait_send()
    rest.wait_recv()
    saved.wait()
    for j in range(1, 8):
        other(j).wait_send()
        source = (brick + j) % n_brick
        pltpu.make_async_remote_copy(
            src_ref=stage.at[source, pl.ds(96, 40)], dst_ref=rest_ref.at[source], send_sem=rest_send.at[source],
            recv_sem=rest_recv.at[source], device_id=(slab, source), device_id_type=mesh_id,
        ).wait_recv()

    def keys(j, sums):
        parts = [arrived_ref[4 * j + i] for i in range(4)]
        rows = pl.ds(pl.multiple_of(8 * j, 8), 8)
        for c, ref in enumerate((p0_ref, p1_ref, p2_ref, drag_ref)):
            value = jnp.concatenate([part[2 * c : 2 * c + 2] for part in parts], axis=0)
            ref[rows, :] = value
        live = value != 0.0
        key = key_ref[rows, :]
        key_ref[rows, :] = jnp.where(live, key, LAST)
        block = jnp.where(live, (key >> 27) + 16, 32)
        return tuple(s + jnp.where(block < b + 1, 1, 0) for b, s in enumerate(sums))

    sums = lax.fori_loop(0, tiles, keys, tuple(jnp.zeros((8, 128), I32) for _ in range(32)))
    tail = (cell_ref[tiles * 8 - 8 :, :] == 131071) & (drag_ref[tiles * 8 - 8 :, :] != 0.0) & (place == 1023)
    starts_ref[0] = 0
    for b in range(32):
        starts_ref[b + 1] = jnp.sum(sums[b])
    starts_ref[32] = jnp.where(jnp.sum(jnp.where(tail, 1, 0)) > 0, tiles * 1024, starts_ref[32])


def brick_kernel(
    starts_ref, key_ref, coef_ref, p0_ref, p1_ref, p2_ref, bricks_ref, rest_ref,
    f0_ref, f1_ref, f2_ref, slot_ref, sum_ref, table, deposit, *, width, group,
):
    rows = key_ref.shape[0]
    n = width // 128
    force_refs = (f0_ref, f1_ref, f2_ref)
    for ref in force_refs:
        ref[...] = jnp.zeros_like(ref)
    slot_ref[...] = jnp.where(coef_ref[...] != 0.0, (key_ref[...] >> 12) & 32767, p0_ref[...].astype(I32))

    r_iota = lax.broadcasted_iota(I32, (256, width), 0)
    l_iota = lax.broadcasted_iota(I32, (16, width), 0)
    r_iota = r_iota.astype(F32).astype(BF16)
    l_bf = l_iota.astype(F32).astype(BF16)
    p_iota = lax.broadcasted_iota(I32, (1, width), 1)
    one, zero = jnp.ones((), BF16), jnp.zeros((), BF16)

    def blocks(g, carry):
        bs = [g * group + i for i in range(group)]
        row0s, counts = [], []
        for i, b in enumerate(bs):
            z, q = b // 4, b % 4
            x8 = pl.multiple_of(q * 8, 8)
            for c in range(4):
                ref, at = (rest_ref, x8) if c == 3 else (bricks_ref, pl.multiple_of(c * 32 + x8, 8))
                centre = ref[z, pl.ds(at, 8), :]
                for p, piece in enumerate(split3(centre)):
                    at = p * 64 + c * 16
                    table[i, at : at + 16, :] = jnp.concatenate([piece[:, :256], piece[:, 256:]], axis=0)
            deposit[i] = jnp.zeros(deposit.shape[1:], F32)
            first, end = starts_ref[b], starts_ref[b + 1]
            row0 = first // 128
            row0s.append(row0)
            counts.append(jnp.where(end > first, (end - row0 * 128 + width - 1) // width, 0))
        windows = counts[0]
        for c in counts[1:]:
            windows = jnp.maximum(windows, c)

        def window(w, inner):
            ats, oh, valids, ls, gots = [], [], [], [], []

            def line(ref, at):
                return jnp.concatenate([ref[pl.ds(at + k, 1), :] for k in range(n)], axis=1)

            for i, b in enumerate(bs):
                row = row0s[i] + w * n
                at = jnp.minimum(row, rows - n)
                key = line(key_ref, at)
                valid = ((key >> 27) + 16 == b) & (p_iota >= (row - at) * 128)
                r = jnp.where(valid, key & 255, -1)
                l = ((key >> 9) & 7) + ((key >> 8) & 1) * 8
                ats.append(at)
                oh.append(jnp.where(r_iota == r.astype(F32).astype(BF16), one, zero))
                valids.append(valid)
                ls.append(l)
            for i in range(group):
                gots.append(jnp.dot(table[i], oh[i], preferred_element_type=F32))
            spreads = []
            forces = []
            for i in range(group):
                got = gots[i]
                got = got[:64] + (got[64:128] + got[128:])
                mask = l_iota == ls[i]
                u = [
                    jnp.sum(jnp.where(mask, got[c * 16 : (c + 1) * 16], 0.0), axis=0, keepdims=True) for c in range(4)
                ]
                frac = jnp.where(valids[i], u[3], 1.0)
                beta = line(coef_ref, ats[i]) * (1.0 - frac) / (frac * frac)
                fs = [
                    jnp.where(valids[i], beta * (u[c] - line(ref, ats[i])), 0.0)
                    for c, ref in enumerate((p0_ref, p1_ref, p2_ref))
                ]
                forces.append(fs)
                split = [split3(f) for f in fs]
                low_mask = l_bf == ls[i].astype(F32).astype(BF16)
                spreads.append(
                    jnp.concatenate(
                        [jnp.where(low_mask, split[c][p], zero) for p in range(3) for c in range(3)], axis=0
                    )
                )
            for i in range(group):
                deposit[i] += lax.dot_general(
                    spreads[i], oh[i], (((1,), (1,)), ((), ())), preferred_element_type=F32
                )
            for i in range(group):
                for c in range(3):
                    for k in range(n):
                        force_refs[c][pl.ds(ats[i] + k, 1), :] += forces[i][c][:, k * 128 : (k + 1) * 128]
            return inner

        lax.fori_loop(0, windows, window, 0)

        for i, b in enumerate(bs):
            z, q = b // 4, b % 4
            x8 = pl.multiple_of(q * 8, 8)
            summed = deposit[i, 0:48, :] + (deposit[i, 48:96, :] + deposit[i, 96:144, :])
            for c in range(3):
                left, right = summed[c * 16 : c * 16 + 8], summed[c * 16 + 8 : c * 16 + 16]
                sum_ref[z, c, pl.ds(x8, 8), :] = jnp.concatenate([left, right], axis=1)
        return carry

    lax.fori_loop(0, 32 // group, blocks, 0)


def viscous_kernel(bricks_ref, rest_ref, below_ref, above_ref, sum_ref, net_hbm, net_ref, padded, net_sem):
    for c in range(4):
        own = slice(c * 32, (c + 1) * 32)
        for z in range(8):
            padded[z + 1, c, 8:40, :] = rest_ref[z, 0:32, :] if c == 3 else bricks_ref[z, own, :]
            padded[z + 1, c, 7:8, :] = rest_ref[z, 32 + c : 33 + c, :]
            padded[z + 1, c, 40:41, :] = rest_ref[z, 36 + c : 37 + c, :]
        padded[0, c, 8:40, :] = below_ref[own, :]
        padded[9, c, 8:40, :] = above_ref[own, :]
    y_iota = lax.broadcasted_iota(I32, (8, 512), 1)

    def plane(z, carry):
        for x8 in range(0, 32, 8):
            tall = [padded[z + 1, c, x8 : x8 + 24, :] for c in range(4)]
            below = [padded[z, c, x8 + 8 : x8 + 16, :] for c in range(4)]
            above = [padded[z + 2, c, x8 + 8 : x8 + 16, :] for c in range(4)]
            centre = [t[8:16] for t in tall]
            sides = [above, below, [t[9:17] for t in tall], [t[7:15] for t in tall]]
            sides.append([jnp.where(y_iota == 511, 0.0, pltpu.roll(t, 511, 1)) for t in centre])
            sides.append([jnp.where(y_iota == 0, 0.0, pltpu.roll(t, 1, 1)) for t in centre])
            total = [jnp.zeros((8, 512), F32) for _ in range(3)]
            for side in sides:
                weight = 0.5 * (centre[3] + side[3])
                for c in range(3):
                    total[c] = total[c] + weight * (side[c] - centre[c])
            for c in range(3):
                net_ref[z, c, x8 : x8 + 8, :] = total[c] - sum_ref[z, c, x8 : x8 + 8, :]
        pltpu.make_async_copy(net_ref.at[z], net_hbm.at[z], net_sem.at[z]).start()
        return carry

    lax.fori_loop(0, 8, plane, 0)
    for z in range(8):
        pltpu.make_async_copy(net_ref.at[z], net_hbm.at[z], net_sem.at[z]).wait()


def per_device(
    fluid_velocity, porosity, particle_velocity, drag_coef, send_rows, counts, recv_cell
):
    n_slab = lax.axis_size("slab")
    n_brick = lax.axis_size("brick")
    devices = n_slab * n_brick
    cap = send_rows.shape[0] // devices
    vmem = pl.BlockSpec(memory_space=pltpu.VMEM)
    smem = pl.BlockSpec(memory_space=pltpu.SMEM)
    params = pltpu.CompilerParams(vmem_limit_bytes=32 << 20)
    square = jax.ShapeDtypeStruct((256, 128), F32)
    hbm = pl.BlockSpec(memory_space=pl.ANY)
    staged, others, starts, key, p0, p1, p2, drag = pl.pallas_call(
        functools.partial(exchange_kernel, cap=cap, group=16),
        out_shape=(
            jax.ShapeDtypeStruct((8, 96, 512), F32),
            jax.ShapeDtypeStruct((8, 40, 512), F32),
            jax.ShapeDtypeStruct((33,), I32),
            jax.ShapeDtypeStruct((256, 128), I32),
            square, square, square, square,
        ),
        in_specs=[smem] + [hbm] * 6,
        out_specs=(hbm, vmem, smem) + (vmem,) * 5,
        scratch_shapes=[
            pltpu.VMEM((3, 16384), F32),
            pltpu.VMEM((128, 128), F32),
            pltpu.VMEM((256, 128), I32),
            pltpu.VMEM((3, 256, 512), F32),
            pltpu.VMEM((256, 512), F32),
            pltpu.VMEM((256, 128), I32),
            pltpu.VMEM((3, 128, 128), F32),
            pltpu.VMEM((8, 136, 512), F32),
            pltpu.VMEM((768, 256), BF16),
            pltpu.VMEM((devices, 8, 128), F32),
            pltpu.VMEM((devices, 8, 128), F32),
            pltpu.SemaphoreType.DMA((6,)),
            pltpu.SemaphoreType.DMA,
            pltpu.SemaphoreType.DMA,
            pltpu.SemaphoreType.DMA,
            pltpu.SemaphoreType.DMA((8,)),
            pltpu.SemaphoreType.DMA((8,)),
        ],
        compiler_params=pltpu.CompilerParams(
            vmem_limit_bytes=60 << 20, collective_id=0, has_side_effects=True
        ),
        name="exchange",
    )(
        counts,
        particle_velocity,
        drag_coef.reshape(128, 128),
        send_rows.reshape(256, 128),
        fluid_velocity.reshape(3, 256, 512),
        porosity.reshape(256, 512),
        recv_cell.reshape(256, 128),
    )

    bricks = lax.all_to_all(staged, "brick", split_axis=0, concat_axis=0, tiled=True)
    ordered = lax.sort(
        [part.reshape(-1) for part in (key, drag, p0, p1, p2)], num_keys=1, is_stable=False
    )
    top, bottom = [jnp.concatenate([bricks[z], others[z, :32]]) for z in (7, 0)]
    below = lax.ppermute(top, "slab", [(i, i + 1) for i in range(n_slab - 1)])
    above = lax.ppermute(bottom, "slab", [(i + 1, i) for i in range(n_slab - 1)])
    f0, f1, f2, slot, summed = pl.pallas_call(
        functools.partial(brick_kernel, width=256, group=16),
        out_shape=(
            square, square, square,
            jax.ShapeDtypeStruct((256, 128), I32),
            jax.ShapeDtypeStruct((8, 3, 32, 512), F32),
        ),
        in_specs=[smem] + [vmem] * 7,
        out_specs=(vmem,) * 5,
        scratch_shapes=[pltpu.VMEM((16, 192, 256), BF16), pltpu.VMEM((16, 144, 256), F32)],
        compiler_params=params,
        cost_estimate=pl.CostEstimate(flops=30_000_000_000, bytes_accessed=6_000_000, transcendentals=0),
        name="brick_forces",
    )(starts, *[part.reshape(256, 128) for part in ordered], bricks, others)
    net = pl.pallas_call(
        viscous_kernel,
        out_shape=jax.ShapeDtypeStruct((8, 3, 32, 512), F32),
        in_specs=[vmem] * 5,
        out_specs=hbm,
        scratch_shapes=[
            pltpu.VMEM((8, 3, 32, 512), F32),
            pltpu.VMEM((10, 4, 48, 512), F32),
            pltpu.SemaphoreType.DMA((8,)),
        ],
        compiler_params=params,
        name="viscous",
    )(bricks, others, below, above, summed)

    slot, f0, f1, f2, net = lax.optimization_barrier((slot, f0, f1, f2, net))
    returned = lax.all_to_all(net, "brick", split_axis=0, concat_axis=0, tiled=True)
    back = lax.sort([part.reshape(-1) for part in (slot, f0, f1, f2)], num_keys=1, is_stable=False)
    slot_force = jnp.stack(back[1:])
    returned = jnp.swapaxes(returned, 0, 1).reshape(fluid_velocity.shape)
    new_velocity = fluid_velocity + time_step * returned / porosity
    return (new_velocity, slot_force)


def solution(mesh):
    placed = (
        P(None, ("slab", "brick"), None, None),
        P(("slab", "brick"), None, None),
        P(None, ("slab", "brick")),
        P(("slab", "brick")),
        P(("slab", "brick")),
        P(("slab", "brick")),
        P(("slab", "brick")),
    )
    return jax.shard_map(
        per_device,
        mesh=mesh,
        in_specs=placed,
        out_specs=(P(None, ("slab", "brick"), None, None), P(None, ("slab", "brick"))),
        check_vma=False,
    )
```

```python
import functools

import jax
import jax.numpy as jnp
from jax import lax
from jax.experimental import pallas as pl
from jax.experimental.pallas import tpu as pltpu
from jax.sharding import PartitionSpec as P

time_step = 0.05
F32, BF16, I32 = jnp.float32, jnp.bfloat16, jnp.int32
LAST = 2**31 - 1


def split3(x):
    high = x.astype(BF16)
    rest = x - high.astype(F32)
    mid = rest.astype(BF16)
    low = (rest - mid.astype(F32)).astype(BF16)
    return high, mid, low


def exchange_kernel(
    counts_ref, pv_hbm, coef_hbm, rows_hbm, u_hbm, frac_hbm, cell_hbm,
    stage_hbm, rest_ref, starts_ref, key_ref, p0_ref, p1_ref, p2_ref, drag_ref,
    pv_ref, coef_ref, rows_ref, u_ref, frac_ref, cell_ref, particles,
    stage, table, packed, arrived_ref, load_sem, stage_sem, part_send, part_recv, rest_send, rest_recv,
    *, cap, group,
):
    pairs = (
        (pv_hbm, pv_ref), (coef_hbm, coef_ref), (rows_hbm, rows_ref), (u_hbm, u_ref), (frac_hbm, frac_ref),
        (cell_hbm, cell_ref),
    )
    loads = [pltpu.make_async_copy(source, target, load_sem.at[i]) for i, (source, target) in enumerate(pairs)]
    for load in loads:
        load.start()
    n_slab, n_brick = lax.axis_size("slab"), lax.axis_size("brick")
    devices = n_slab * n_brick
    slab, brick = lax.axis_index("slab"), lax.axis_index("brick")
    me = slab * n_brick + brick
    mesh_id = pl.DeviceIdType.MESH

    def coords(d):
        return (d // n_brick, d % n_brick)

    barrier = pltpu.get_barrier_semaphore()

    def greet(j):
        pl.semaphore_signal(barrier, inc=1, device_id=coords((me + j) % devices), device_id_type=mesh_id)

    def greet_some(i, carry):
        for j in range(6):
            greet(6 * i + j + 1)
        return carry

    lax.fori_loop(0, 21, greet_some, 0)
    greet(127)

    for load in loads[:3]:
        load.wait()
    for l in range(128):
        part = pv_ref[:, l * 128 : (l + 1) * 128]
        for c in range(3):
            particles[c, l : l + 1, :] = part[c : c + 1]
    for c in range(4):
        whole = coef_ref[...] if c == 3 else particles[c]
        halves = jnp.concatenate([whole[:64], whole[64:]], axis=1)
        for p, piece in enumerate(split3(halves)):
            table[p * 256 + c * 64 : p * 256 + (c + 1) * 64, :] = piece

    r_iota = lax.broadcasted_iota(I32, (256, cap), 0).astype(F32).astype(BF16)
    one, zero = jnp.ones((), BF16), jnp.zeros((), BF16)
    l_iota = lax.broadcasted_iota(I32, (64, cap), 0)
    k_iota = lax.broadcasted_iota(I32, (1, cap), 1)

    def pick(to):
        onehots, planes, gots, picked = [], [], [], []
        for t in to:
            row = jnp.concatenate([rows_ref[pl.ds(2 * t, 1), :], rows_ref[pl.ds(2 * t + 1, 1), :]], axis=1)
            r = (row & 127) + ((row >> 13) << 7)
            onehots.append(jnp.where(r_iota == r.astype(F32).astype(BF16), one, zero))
            planes.append((row >> 7) & 63)
        for onehot in onehots:
            gots.append(jnp.dot(table[...], onehot, preferred_element_type=F32))
        slot = (me * cap + k_iota).astype(F32)
        for t, got, l in zip(to, gots, planes):
            got = got[:256] + (got[256:512] + got[512:])
            mask = l_iota == l
            live = k_iota < counts_ref[t]
            values = []
            for c in range(4):
                value = jnp.sum(jnp.where(mask, got[c * 64 : (c + 1) * 64], 0.0), axis=0, keepdims=True)
                if c == 0:
                    value = jnp.where(live, value, slot)
                if c == 3:
                    value = jnp.where(live, value, 0.0)
                values += [value[:, :128], value[:, 128:]]
            picked.append(jnp.concatenate(values, axis=0))
        return picked

    def parcel(t):
        return pltpu.make_async_remote_copy(
            src_ref=packed.at[t], dst_ref=arrived_ref.at[me], send_sem=part_send, recv_sem=part_recv,
            device_id=coords(t), device_id_type=mesh_id,
        )

    def other(j):
        to = (brick + j) % n_brick
        return pltpu.make_async_remote_copy(
            src_ref=stage.at[to, pl.ds(96, 40)], dst_ref=rest_ref.at[brick], send_sem=rest_send.at[to],
            recv_sem=rest_recv.at[brick], device_id=(slab, to), device_id_type=mesh_id,
        )

    def fill(i, carry):
        to = [(me + 1 + i * group + j) % devices for j in range(group)]
        for t, value in zip(to, pick(to)):
            packed[t] = value
        return carry

    def send(i, carry):
        for j in range(group):
            parcel((me + 1 + i * group + j) % devices).start()
        return carry

    def some(i, carry):
        return send(i, fill(i, carry))

    fill(0, 0)
    for load in loads[3:]:
        load.wait()
    for c in range(4):
        for b in range(8):
            field = frac_ref[b * 32 : (b + 1) * 32, :] if c == 3 else u_ref[c, b * 32 : (b + 1) * 32, :]
            stage[b, c * 32 : (c + 1) * 32, :] = field
            if b < 7:
                stage[b + 1, 128 + c : 129 + c, :] = field[31:32]
            if b > 0:
                stage[b - 1, 132 + c : 133 + c, :] = field[0:1]
        stage[0, 128 + c : 129 + c, :] = jnp.zeros((1, 512), F32)
        stage[7, 132 + c : 133 + c, :] = jnp.zeros((1, 512), F32)
    saved = pltpu.make_async_copy(stage.at[:, pl.ds(0, 96)], stage_hbm, stage_sem)
    saved.start()
    rest_ref[brick] = stage[brick, 96:136]
    pl.semaphore_wait(barrier, devices - 1)
    for j in range(1, 8):
        other(j).start()
    send(0, 0)
    lax.fori_loop(1, devices // group - 1, some, 0)
    to = [(me + 1 + devices - group + j) % devices for j in range(group)]
    picked = pick(to)
    for t, value in zip(to[:-1], picked):
        packed[t] = value
    arrived_ref[me] = picked[-1]
    for t in to[:-1]:
        parcel(t).start()

    tiles = cell_ref.shape[0] // 8
    place = lax.broadcasted_iota(I32, (8, 128), 0) * 128 + lax.broadcasted_iota(I32, (8, 128), 1)

    def early(j, carry):
        rows = pl.ds(pl.multiple_of(8 * j, 8), 8)
        cell = cell_ref[rows, :]
        key_ref[rows, :] = (((cell >> 12) - 16) << 27) + ((j * 1024 + place) << 12) + (cell & 4095)
        return carry

    lax.fori_loop(0, tiles, early, 0, unroll=4)
    rest = pltpu.make_async_remote_copy(
        src_ref=packed.at[pl.ds(0, devices - 1)], dst_ref=arrived_ref.at[pl.ds(0, devices - 1)],
        send_sem=part_send, recv_sem=part_recv, device_id=coords((me + 1) % devices), device_id_type=mesh_id,
    )
    rest.wait_send()
    rest.wait_recv()
    saved.wait()
    for j in range(1, 8):
        other(j).wait_send()
        source = (brick + j) % n_brick
        pltpu.make_async_remote_copy(
            src_ref=stage.at[source, pl.ds(96, 40)], dst_ref=rest_ref.at[source], send_sem=rest_send.at[source],
            recv_sem=rest_recv.at[source], device_id=(slab, source), device_id_type=mesh_id,
        ).wait_recv()

    def keys(j, sums):
        parts = [arrived_ref[4 * j + i] for i in range(4)]
        rows = pl.ds(pl.multiple_of(8 * j, 8), 8)
        for c, ref in enumerate((p0_ref, p1_ref, p2_ref, drag_ref)):
            value = jnp.concatenate([part[2 * c : 2 * c + 2] for part in parts], axis=0)
            ref[rows, :] = value
        live = value != 0.0
        key = key_ref[rows, :]
        key_ref[rows, :] = jnp.where(live, key, LAST)
        block = jnp.where(live, (key >> 27) + 16, 32)
        return tuple(s + jnp.where(block < b + 1, 1, 0) for b, s in enumerate(sums))

    sums = lax.fori_loop(0, tiles, keys, tuple(jnp.zeros((8, 128), I32) for _ in range(32)))
    tail = (cell_ref[tiles * 8 - 8 :, :] == 131071) & (drag_ref[tiles * 8 - 8 :, :] != 0.0) & (place == 1023)
    starts_ref[0] = 0
    for b in range(32):
        starts_ref[b + 1] = jnp.sum(sums[b])
    starts_ref[32] = jnp.where(jnp.sum(jnp.where(tail, 1, 0)) > 0, tiles * 1024, starts_ref[32])


def brick_kernel(
    starts_ref, key_ref, coef_ref, p0_ref, p1_ref, p2_ref, bricks_ref, rest_ref,
    f0_ref, f1_ref, f2_ref, slot_ref, sum_ref, table, deposit, *, width, group,
):
    rows = key_ref.shape[0]
    n = width // 128
    force_refs = (f0_ref, f1_ref, f2_ref)
    for ref in force_refs:
        ref[...] = jnp.zeros_like(ref)
    slot_ref[...] = jnp.where(coef_ref[...] != 0.0, (key_ref[...] >> 12) & 32767, p0_ref[...].astype(I32))

    r_iota = lax.broadcasted_iota(I32, (256, width), 0)
    l_iota = lax.broadcasted_iota(I32, (16, width), 0)
    r_iota = r_iota.astype(F32).astype(BF16)
    l_bf = l_iota.astype(F32).astype(BF16)
    p_iota = lax.broadcasted_iota(I32, (1, width), 1)
    one, zero = jnp.ones((), BF16), jnp.zeros((), BF16)

    def blocks(g, carry):
        bs = [g * group + i for i in range(group)]
        row0s, counts = [], []
        for i, b in enumerate(bs):
            z, q = b // 4, b % 4
            x8 = pl.multiple_of(q * 8, 8)
            for c in range(4):
                ref, at = (rest_ref, x8) if c == 3 else (bricks_ref, pl.multiple_of(c * 32 + x8, 8))
                centre = ref[z, pl.ds(at, 8), :]
                for p, piece in enumerate(split3(centre)):
                    at = p * 64 + c * 16
                    table[i, at : at + 16, :] = jnp.concatenate([piece[:, :256], piece[:, 256:]], axis=0)
            deposit[i] = jnp.zeros(deposit.shape[1:], F32)
            first, end = starts_ref[b], starts_ref[b + 1]
            row0 = first // 128
            row0s.append(row0)
            counts.append(jnp.where(end > first, (end - row0 * 128 + width - 1) // width, 0))
        windows = counts[0]
        for c in counts[1:]:
            windows = jnp.maximum(windows, c)

        def window(w, inner):
            ats, oh, valids, ls, gots = [], [], [], [], []

            def line(ref, at):
                return jnp.concatenate([ref[pl.ds(at + k, 1), :] for k in range(n)], axis=1)

            for i, b in enumerate(bs):
                row = row0s[i] + w * n
                at = jnp.minimum(row, rows - n)
                key = line(key_ref, at)
                valid = ((key >> 27) + 16 == b) & (p_iota >= (row - at) * 128)
                r = jnp.where(valid, key & 255, -1)
                l = ((key >> 9) & 7) + ((key >> 8) & 1) * 8
                ats.append(at)
                oh.append(jnp.where(r_iota == r.astype(F32).astype(BF16), one, zero))
                valids.append(valid)
                ls.append(l)
            for i in range(group):
                gots.append(jnp.dot(table[i], oh[i], preferred_element_type=F32))
            spreads = []
            forces = []
            for i in range(group):
                got = gots[i]
                got = got[:64] + (got[64:128] + got[128:])
                mask = l_iota == ls[i]
                u = [
                    jnp.sum(jnp.where(mask, got[c * 16 : (c + 1) * 16], 0.0), axis=0, keepdims=True) for c in range(4)
                ]
                frac = jnp.where(valids[i], u[3], 1.0)
                beta = line(coef_ref, ats[i]) * (1.0 - frac) / (frac * frac)
                fs = [
                    jnp.where(valids[i], beta * (u[c] - line(ref, ats[i])), 0.0)
                    for c, ref in enumerate((p0_ref, p1_ref, p2_ref))
                ]
                forces.append(fs)
                split = [split3(f) for f in fs]
                low_mask = l_bf == ls[i].astype(F32).astype(BF16)
                spreads.append(
                    jnp.concatenate(
                        [jnp.where(low_mask, split[c][p], zero) for p in range(3) for c in range(3)], axis=0
                    )
                )
            for i in range(group):
                deposit[i] += lax.dot_general(
                    spreads[i], oh[i], (((1,), (1,)), ((), ())), preferred_element_type=F32
                )
            for i in range(group):
                for c in range(3):
                    for k in range(n):
                        force_refs[c][pl.ds(ats[i] + k, 1), :] += forces[i][c][:, k * 128 : (k + 1) * 128]
            return inner

        lax.fori_loop(0, windows, window, 0)

        for i, b in enumerate(bs):
            z, q = b // 4, b % 4
            x8 = pl.multiple_of(q * 8, 8)
            summed = deposit[i, 0:48, :] + (deposit[i, 48:96, :] + deposit[i, 96:144, :])
            for c in range(3):
                left, right = summed[c * 16 : c * 16 + 8], summed[c * 16 + 8 : c * 16 + 16]
                sum_ref[z, c, pl.ds(x8, 8), :] = jnp.concatenate([left, right], axis=1)
        return carry

    lax.fori_loop(0, 32 // group, blocks, 0)


def viscous_kernel(bricks_ref, rest_ref, below_ref, above_ref, sum_ref, net_hbm, net_ref, padded, net_sem):
    for c in range(4):
        own = slice(c * 32, (c + 1) * 32)
        for z in range(8):
            padded[z + 1, c, 8:40, :] = rest_ref[z, 0:32, :] if c == 3 else bricks_ref[z, own, :]
            padded[z + 1, c, 7:8, :] = rest_ref[z, 32 + c : 33 + c, :]
            padded[z + 1, c, 40:41, :] = rest_ref[z, 36 + c : 37 + c, :]
        padded[0, c, 8:40, :] = below_ref[own, :]
        padded[9, c, 8:40, :] = above_ref[own, :]
    y_iota = lax.broadcasted_iota(I32, (8, 512), 1)

    def plane(z, carry):
        for x8 in range(0, 32, 8):
            tall = [padded[z + 1, c, x8 : x8 + 24, :] for c in range(4)]
            below = [padded[z, c, x8 + 8 : x8 + 16, :] for c in range(4)]
            above = [padded[z + 2, c, x8 + 8 : x8 + 16, :] for c in range(4)]
            centre = [t[8:16] for t in tall]
            sides = [above, below, [t[9:17] for t in tall], [t[7:15] for t in tall]]
            sides.append([jnp.where(y_iota == 511, 0.0, pltpu.roll(t, 511, 1)) for t in centre])
            sides.append([jnp.where(y_iota == 0, 0.0, pltpu.roll(t, 1, 1)) for t in centre])
            total = [jnp.zeros((8, 512), F32) for _ in range(3)]
            for side in sides:
                weight = 0.5 * (centre[3] + side[3])
                for c in range(3):
                    total[c] = total[c] + weight * (side[c] - centre[c])
            for c in range(3):
                net_ref[z, c, x8 : x8 + 8, :] = total[c] - sum_ref[z, c, x8 : x8 + 8, :]
        pltpu.make_async_copy(net_ref.at[z], net_hbm.at[z], net_sem.at[z]).start()
        return carry

    lax.fori_loop(0, 8, plane, 0)
    for z in range(8):
        pltpu.make_async_copy(net_ref.at[z], net_hbm.at[z], net_sem.at[z]).wait()


def step_kernel(u_ref, frac_ref, net_ref, out_hbm, out_ref, save_sem):
    def save(k):
        x = pl.ds(k * 64, 64)
        return pltpu.make_async_copy(out_ref.at[:, x], out_hbm.at[:, x], save_sem.at[k])

    for k in range(4):
        for b in range(2 * k, 2 * k + 2):
            x = slice(b * 32, (b + 1) * 32)
            for c in range(3):
                out_ref[c, x, :] = u_ref[c, x, :] + time_step * net_ref[b, c] / frac_ref[x, :]
        save(k).start()
    for k in range(4):
        save(k).wait()


def per_device(
    fluid_velocity, porosity, particle_velocity, drag_coef, send_rows, counts, recv_cell
):
    n_slab = lax.axis_size("slab")
    n_brick = lax.axis_size("brick")
    devices = n_slab * n_brick
    cap = send_rows.shape[0] // devices
    vmem = pl.BlockSpec(memory_space=pltpu.VMEM)
    smem = pl.BlockSpec(memory_space=pltpu.SMEM)
    params = pltpu.CompilerParams(vmem_limit_bytes=32 << 20)
    square = jax.ShapeDtypeStruct((256, 128), F32)
    hbm = pl.BlockSpec(memory_space=pl.ANY)
    staged, others, starts, key, p0, p1, p2, drag = pl.pallas_call(
        functools.partial(exchange_kernel, cap=cap, group=16),
        out_shape=(
            jax.ShapeDtypeStruct((8, 96, 512), F32),
            jax.ShapeDtypeStruct((8, 40, 512), F32),
            jax.ShapeDtypeStruct((33,), I32),
            jax.ShapeDtypeStruct((256, 128), I32),
            square, square, square, square,
        ),
        in_specs=[smem] + [hbm] * 6,
        out_specs=(hbm, vmem, smem) + (vmem,) * 5,
        scratch_shapes=[
            pltpu.VMEM((3, 16384), F32),
            pltpu.VMEM((128, 128), F32),
            pltpu.VMEM((256, 128), I32),
            pltpu.VMEM((3, 256, 512), F32),
            pltpu.VMEM((256, 512), F32),
            pltpu.VMEM((256, 128), I32),
            pltpu.VMEM((3, 128, 128), F32),
            pltpu.VMEM((8, 136, 512), F32),
            pltpu.VMEM((768, 256), BF16),
            pltpu.VMEM((devices, 8, 128), F32),
            pltpu.VMEM((devices, 8, 128), F32),
            pltpu.SemaphoreType.DMA((6,)),
            pltpu.SemaphoreType.DMA,
            pltpu.SemaphoreType.DMA,
            pltpu.SemaphoreType.DMA,
            pltpu.SemaphoreType.DMA((8,)),
            pltpu.SemaphoreType.DMA((8,)),
        ],
        compiler_params=pltpu.CompilerParams(
            vmem_limit_bytes=60 << 20, collective_id=0, has_side_effects=True
        ),
        name="exchange",
    )(
        counts,
        particle_velocity,
        drag_coef.reshape(128, 128),
        send_rows.reshape(256, 128),
        fluid_velocity.reshape(3, 256, 512),
        porosity.reshape(256, 512),
        recv_cell.reshape(256, 128),
    )

    bricks = lax.all_to_all(staged, "brick", split_axis=0, concat_axis=0, tiled=True)
    ordered = lax.sort(
        [part.reshape(-1) for part in (key, drag, p0, p1, p2)], num_keys=1, is_stable=False
    )
    top, bottom = [jnp.concatenate([bricks[z], others[z, :32]]) for z in (7, 0)]
    below = lax.ppermute(top, "slab", [(i, i + 1) for i in range(n_slab - 1)])
    above = lax.ppermute(bottom, "slab", [(i + 1, i) for i in range(n_slab - 1)])
    f0, f1, f2, slot, summed = pl.pallas_call(
        functools.partial(brick_kernel, width=256, group=16),
        out_shape=(
            square, square, square,
            jax.ShapeDtypeStruct((256, 128), I32),
            jax.ShapeDtypeStruct((8, 3, 32, 512), F32),
        ),
        in_specs=[smem] + [vmem] * 7,
        out_specs=(vmem,) * 5,
        scratch_shapes=[pltpu.VMEM((16, 192, 256), BF16), pltpu.VMEM((16, 144, 256), F32)],
        compiler_params=params,
        cost_estimate=pl.CostEstimate(flops=30_000_000_000, bytes_accessed=6_000_000, transcendentals=0),
        name="brick_forces",
    )(starts, *[part.reshape(256, 128) for part in ordered], bricks, others)
    net = pl.pallas_call(
        viscous_kernel,
        out_shape=jax.ShapeDtypeStruct((8, 3, 32, 512), F32),
        in_specs=[vmem] * 5,
        out_specs=hbm,
        scratch_shapes=[
            pltpu.VMEM((8, 3, 32, 512), F32),
            pltpu.VMEM((10, 4, 48, 512), F32),
            pltpu.SemaphoreType.DMA((8,)),
        ],
        compiler_params=params,
        name="viscous",
    )(bricks, others, below, above, summed)

    slot, f0, f1, f2, net = lax.optimization_barrier((slot, f0, f1, f2, net))
    returned = lax.all_to_all(net, "brick", split_axis=0, concat_axis=0, tiled=True)
    back = lax.sort([part.reshape(-1) for part in (slot, f0, f1, f2)], num_keys=1, is_stable=False)
    slot_force = jnp.stack(back[1:])
    new_velocity = pl.pallas_call(
        step_kernel,
        out_shape=jax.ShapeDtypeStruct((3, 256, 512), F32),
        in_specs=[vmem] * 3,
        out_specs=hbm,
        scratch_shapes=[
            pltpu.VMEM((3, 256, 512), F32),
            pltpu.SemaphoreType.DMA((4,)),
        ],
        compiler_params=pltpu.CompilerParams(vmem_limit_bytes=12 << 20),
        name="velocity_step",
    )(fluid_velocity.reshape(3, 256, 512), porosity.reshape(256, 512), returned)
    new_velocity = new_velocity.reshape(fluid_velocity.shape)
    return (new_velocity, slot_force)


def solution(mesh):
    placed = (
        P(None, ("slab", "brick"), None, None),
        P(("slab", "brick"), None, None),
        P(None, ("slab", "brick")),
        P(("slab", "brick")),
        P(("slab", "brick")),
        P(("slab", "brick")),
        P(("slab", "brick")),
    )
    return jax.shard_map(
        per_device,
        mesh=mesh,
        in_specs=placed,
        out_specs=(P(None, ("slab", "brick"), None, None), P(None, ("slab", "brick"))),
        check_vma=False,
    )
```

```python
import functools

import jax
import jax.numpy as jnp
from jax import lax
from jax.experimental import pallas as pl
from jax.experimental.pallas import tpu as pltpu
from jax.sharding import PartitionSpec as P

time_step = 0.05
F32, BF16, I32 = jnp.float32, jnp.bfloat16, jnp.int32
LAST = 2**31 - 1


def split3(x):
    high = x.astype(BF16)
    rest = x - high.astype(F32)
    mid = rest.astype(BF16)
    low = (rest - mid.astype(F32)).astype(BF16)
    return high, mid, low


def exchange_kernel(
    counts_ref, pv_hbm, coef_hbm, rows_hbm, u_hbm, frac_hbm, cell_hbm,
    stage_hbm, rest_ref, starts_ref, key_ref, p0_ref, p1_ref, p2_ref, drag_ref,
    pv_ref, coef_ref, rows_ref, u_ref, frac_ref, cell_ref, particles,
    stage, table, packed, arrived_ref, load_sem, stage_sem, part_send, part_recv, rest_send, rest_recv,
    *, cap, group,
):
    pairs = (
        (pv_hbm, pv_ref), (coef_hbm, coef_ref), (rows_hbm, rows_ref), (u_hbm, u_ref), (frac_hbm, frac_ref),
        (cell_hbm, cell_ref),
    )
    loads = [pltpu.make_async_copy(source, target, load_sem.at[i]) for i, (source, target) in enumerate(pairs)]
    for load in loads:
        load.start()
    n_slab, n_brick = lax.axis_size("slab"), lax.axis_size("brick")
    devices = n_slab * n_brick
    slab, brick = lax.axis_index("slab"), lax.axis_index("brick")
    me = slab * n_brick + brick
    mesh_id = pl.DeviceIdType.MESH

    def coords(d):
        return (d // n_brick, d % n_brick)

    barrier = pltpu.get_barrier_semaphore()

    def greet(j):
        pl.semaphore_signal(barrier, inc=1, device_id=coords((me + j) % devices), device_id_type=mesh_id)

    def greet_some(i, carry):
        for j in range(6):
            greet(6 * i + j + 1)
        return carry

    lax.fori_loop(0, 21, greet_some, 0)
    greet(127)

    for load in loads[:3]:
        load.wait()
    for l in range(128):
        part = pv_ref[:, l * 128 : (l + 1) * 128]
        for c in range(3):
            particles[c, l : l + 1, :] = part[c : c + 1]
    for c in range(4):
        whole = coef_ref[...] if c == 3 else particles[c]
        halves = jnp.concatenate([whole[:64], whole[64:]], axis=1)
        for p, piece in enumerate(split3(halves)):
            table[p * 256 + c * 64 : p * 256 + (c + 1) * 64, :] = piece

    r_iota = lax.broadcasted_iota(I32, (256, cap), 0).astype(F32).astype(BF16)
    one, zero = jnp.ones((), BF16), jnp.zeros((), BF16)
    l_iota = lax.broadcasted_iota(I32, (64, cap), 0)
    k_iota = lax.broadcasted_iota(I32, (1, cap), 1)

    def pick(to):
        onehots, planes, gots, picked = [], [], [], []
        for t in to:
            row = jnp.concatenate([rows_ref[pl.ds(2 * t, 1), :], rows_ref[pl.ds(2 * t + 1, 1), :]], axis=1)
            r = (row & 127) + ((row >> 13) << 7)
            onehots.append(jnp.where(r_iota == r.astype(F32).astype(BF16), one, zero))
            planes.append((row >> 7) & 63)
        for onehot in onehots:
            gots.append(jnp.dot(table[...], onehot, preferred_element_type=F32))
        slot = (me * cap + k_iota).astype(F32)
        for t, got, l in zip(to, gots, planes):
            got = got[:256] + (got[256:512] + got[512:])
            mask = l_iota == l
            live = k_iota < counts_ref[t]
            values = []
            for c in range(4):
                value = jnp.sum(jnp.where(mask, got[c * 64 : (c + 1) * 64], 0.0), axis=0, keepdims=True)
                if c == 0:
                    value = jnp.where(live, value, slot)
                if c == 3:
                    value = jnp.where(live, value, 0.0)
                values += [value[:, :128], value[:, 128:]]
            picked.append(jnp.concatenate(values, axis=0))
        return picked

    def parcel(t):
        return pltpu.make_async_remote_copy(
            src_ref=packed.at[t], dst_ref=arrived_ref.at[me], send_sem=part_send, recv_sem=part_recv,
            device_id=coords(t), device_id_type=mesh_id,
        )

    def other(j):
        to = (brick + j) % n_brick
        return pltpu.make_async_remote_copy(
            src_ref=stage.at[to, pl.ds(96, 40)], dst_ref=rest_ref.at[brick], send_sem=rest_send.at[to],
            recv_sem=rest_recv.at[brick], device_id=(slab, to), device_id_type=mesh_id,
        )

    def fill(i, carry):
        to = [(me + 1 + i * group + j) % devices for j in range(group)]
        for t, value in zip(to, pick(to)):
            packed[t] = value
        return carry

    def send(i, carry):
        for j in range(group):
            parcel((me + 1 + i * group + j) % devices).start()
        return carry

    def some(i, carry):
        return send(i, fill(i, carry))

    fill(0, 0)
    for load in loads[3:]:
        load.wait()
    for c in range(4):
        for b in range(8):
            field = frac_ref[b * 32 : (b + 1) * 32, :] if c == 3 else u_ref[c, b * 32 : (b + 1) * 32, :]
            stage[b, c * 32 : (c + 1) * 32, :] = field
            if b < 7:
                stage[b + 1, 128 + c : 129 + c, :] = field[31:32]
            if b > 0:
                stage[b - 1, 132 + c : 133 + c, :] = field[0:1]
        stage[0, 128 + c : 129 + c, :] = jnp.zeros((1, 512), F32)
        stage[7, 132 + c : 133 + c, :] = jnp.zeros((1, 512), F32)
    saved = pltpu.make_async_copy(stage.at[:, pl.ds(0, 96)], stage_hbm, stage_sem)
    saved.start()
    rest_ref[brick] = stage[brick, 96:136]
    pl.semaphore_wait(barrier, devices - 1)
    for j in range(1, 8):
        other(j).start()
    send(0, 0)
    lax.fori_loop(1, devices // group - 1, some, 0)
    to = [(me + 1 + devices - group + j) % devices for j in range(group)]
    picked = pick(to)
    for t, value in zip(to[:-1], picked):
        packed[t] = value
    arrived_ref[me] = picked[-1]
    for t in to[:-1]:
        parcel(t).start()

    tiles = cell_ref.shape[0] // 8
    place = lax.broadcasted_iota(I32, (8, 128), 0) * 128 + lax.broadcasted_iota(I32, (8, 128), 1)

    def early(j, carry):
        rows = pl.ds(pl.multiple_of(8 * j, 8), 8)
        cell = cell_ref[rows, :]
        key_ref[rows, :] = (((cell >> 12) - 16) << 27) + ((j * 1024 + place) << 12) + (cell & 4095)
        return carry

    lax.fori_loop(0, tiles, early, 0, unroll=4)
    rest = pltpu.make_async_remote_copy(
        src_ref=packed.at[pl.ds(0, devices - 1)], dst_ref=arrived_ref.at[pl.ds(0, devices - 1)],
        send_sem=part_send, recv_sem=part_recv, device_id=coords((me + 1) % devices), device_id_type=mesh_id,
    )
    rest.wait_send()
    rest.wait_recv()
    saved.wait()
    for j in range(1, 8):
        other(j).wait_send()
        source = (brick + j) % n_brick
        pltpu.make_async_remote_copy(
            src_ref=stage.at[source, pl.ds(96, 40)], dst_ref=rest_ref.at[source], send_sem=rest_send.at[source],
            recv_sem=rest_recv.at[source], device_id=(slab, source), device_id_type=mesh_id,
        ).wait_recv()

    def keys(j, sums):
        parts = [arrived_ref[4 * j + i] for i in range(4)]
        rows = pl.ds(pl.multiple_of(8 * j, 8), 8)
        for c, ref in enumerate((p0_ref, p1_ref, p2_ref, drag_ref)):
            value = jnp.concatenate([part[2 * c : 2 * c + 2] for part in parts], axis=0)
            ref[rows, :] = value
        live = value != 0.0
        key = key_ref[rows, :]
        key_ref[rows, :] = jnp.where(live, key, LAST)
        block = jnp.where(live, (key >> 27) + 16, 32)
        return tuple(s + jnp.where(block < b + 1, 1, 0) for b, s in enumerate(sums))

    sums = lax.fori_loop(0, tiles, keys, tuple(jnp.zeros((8, 128), I32) for _ in range(32)))
    tail = (cell_ref[tiles * 8 - 8 :, :] == 131071) & (drag_ref[tiles * 8 - 8 :, :] != 0.0) & (place == 1023)
    starts_ref[0] = 0
    for b in range(32):
        starts_ref[b + 1] = jnp.sum(sums[b])
    starts_ref[32] = jnp.where(jnp.sum(jnp.where(tail, 1, 0)) > 0, tiles * 1024, starts_ref[32])


def brick_kernel(
    starts_ref, key_ref, coef_ref, p0_ref, p1_ref, p2_ref, bricks_ref, rest_ref,
    f0_ref, f1_ref, f2_ref, slot_ref, sum_ref, table, deposit, *, width, group,
):
    rows = key_ref.shape[0]
    n = width // 128
    force_refs = (f0_ref, f1_ref, f2_ref)
    for ref in force_refs:
        ref[...] = jnp.zeros_like(ref)
    slot_ref[...] = jnp.where(coef_ref[...] != 0.0, (key_ref[...] >> 12) & 32767, p0_ref[...].astype(I32))

    r_iota = lax.broadcasted_iota(I32, (256, width), 0)
    l_iota = lax.broadcasted_iota(I32, (16, width), 0)
    r_iota = r_iota.astype(F32).astype(BF16)
    l_bf = l_iota.astype(F32).astype(BF16)
    p_iota = lax.broadcasted_iota(I32, (1, width), 1)
    one, zero = jnp.ones((), BF16), jnp.zeros((), BF16)

    def blocks(g, carry):
        bs = [g * group + i for i in range(group)]
        row0s, counts = [], []
        for i, b in enumerate(bs):
            z, q = b // 4, b % 4
            x8 = pl.multiple_of(q * 8, 8)
            for c in range(4):
                ref, at = (rest_ref, x8) if c == 3 else (bricks_ref, pl.multiple_of(c * 32 + x8, 8))
                centre = ref[z, pl.ds(at, 8), :]
                for p, piece in enumerate(split3(centre)):
                    at = p * 64 + c * 16
                    table[i, at : at + 16, :] = jnp.concatenate([piece[:, :256], piece[:, 256:]], axis=0)
            deposit[i] = jnp.zeros(deposit.shape[1:], F32)
            first, end = starts_ref[b], starts_ref[b + 1]
            row0 = first // 128
            row0s.append(row0)
            counts.append(jnp.where(end > first, (end - row0 * 128 + width - 1) // width, 0))
        windows = counts[0]
        for c in counts[1:]:
            windows = jnp.maximum(windows, c)

        def window(w, inner):
            ats, oh, valids, ls, gots = [], [], [], [], []

            def line(ref, at):
                return jnp.concatenate([ref[pl.ds(at + k, 1), :] for k in range(n)], axis=1)

            for i, b in enumerate(bs):
                row = row0s[i] + w * n
                at = jnp.minimum(row, rows - n)
                key = line(key_ref, at)
                valid = ((key >> 27) + 16 == b) & (p_iota >= (row - at) * 128)
                r = jnp.where(valid, key & 255, -1)
                l = ((key >> 9) & 7) + ((key >> 8) & 1) * 8
                ats.append(at)
                oh.append(jnp.where(r_iota == r.astype(F32).astype(BF16), one, zero))
                valids.append(valid)
                ls.append(l)
            for i in range(group):
                gots.append(jnp.dot(table[i], oh[i], preferred_element_type=F32))
            spreads = []
            forces = []
            for i in range(group):
                got = gots[i]
                got = got[:64] + (got[64:128] + got[128:])
                mask = l_iota == ls[i]
                u = [
                    jnp.sum(jnp.where(mask, got[c * 16 : (c + 1) * 16], 0.0), axis=0, keepdims=True) for c in range(4)
                ]
                frac = jnp.where(valids[i], u[3], 1.0)
                beta = line(coef_ref, ats[i]) * (1.0 - frac) / (frac * frac)
                fs = [
                    jnp.where(valids[i], beta * (u[c] - line(ref, ats[i])), 0.0)
                    for c, ref in enumerate((p0_ref, p1_ref, p2_ref))
                ]
                forces.append(fs)
                split = [split3(f) for f in fs]
                low_mask = l_bf == ls[i].astype(F32).astype(BF16)
                spreads.append(
                    jnp.concatenate(
                        [jnp.where(low_mask, split[c][p], zero) for p in range(3) for c in range(3)], axis=0
                    )
                )
            for i in range(group):
                deposit[i] += lax.dot_general(
                    spreads[i], oh[i], (((1,), (1,)), ((), ())), preferred_element_type=F32
                )
            for i in range(group):
                for c in range(3):
                    for k in range(n):
                        force_refs[c][pl.ds(ats[i] + k, 1), :] += forces[i][c][:, k * 128 : (k + 1) * 128]
            return inner

        lax.fori_loop(0, windows, window, 0)

        for i, b in enumerate(bs):
            z, q = b // 4, b % 4
            x8 = pl.multiple_of(q * 8, 8)
            summed = deposit[i, 0:48, :] + (deposit[i, 48:96, :] + deposit[i, 96:144, :])
            for c in range(3):
                left, right = summed[c * 16 : c * 16 + 8], summed[c * 16 + 8 : c * 16 + 16]
                sum_ref[z, c, pl.ds(x8, 8), :] = jnp.concatenate([left, right], axis=1)
        return carry

    lax.fori_loop(0, 32 // group, blocks, 0)


def viscous_kernel(bricks_ref, rest_ref, below_ref, above_ref, sum_ref, net_hbm, net_ref, padded, net_sem):
    for c in range(4):
        own = slice(c * 32, (c + 1) * 32)
        for z in range(8):
            padded[z + 1, c, 8:40, :] = rest_ref[z, 0:32, :] if c == 3 else bricks_ref[z, own, :]
            padded[z + 1, c, 7:8, :] = rest_ref[z, 32 + c : 33 + c, :]
            padded[z + 1, c, 40:41, :] = rest_ref[z, 36 + c : 37 + c, :]
        padded[0, c, 8:40, :] = below_ref[own, :]
        padded[9, c, 8:40, :] = above_ref[own, :]
    y_iota = lax.broadcasted_iota(I32, (8, 512), 1)

    def plane(z, carry):
        for x8 in range(0, 32, 8):
            tall = [padded[z + 1, c, x8 : x8 + 24, :] for c in range(4)]
            below = [padded[z, c, x8 + 8 : x8 + 16, :] for c in range(4)]
            above = [padded[z + 2, c, x8 + 8 : x8 + 16, :] for c in range(4)]
            centre = [t[8:16] for t in tall]
            sides = [above, below, [t[9:17] for t in tall], [t[7:15] for t in tall]]
            sides.append([jnp.where(y_iota == 511, 0.0, pltpu.roll(t, 511, 1)) for t in centre])
            sides.append([jnp.where(y_iota == 0, 0.0, pltpu.roll(t, 1, 1)) for t in centre])
            total = [jnp.zeros((8, 512), F32) for _ in range(3)]
            for side in sides:
                weight = 0.5 * (centre[3] + side[3])
                for c in range(3):
                    total[c] = total[c] + weight * (side[c] - centre[c])
            for c in range(3):
                net_ref[z, c, x8 : x8 + 8, :] = total[c] - sum_ref[z, c, x8 : x8 + 8, :]
        pltpu.make_async_copy(net_ref.at[z], net_hbm.at[z], net_sem.at[z]).start()
        return carry

    lax.fori_loop(0, 8, plane, 0)
    for z in range(8):
        pltpu.make_async_copy(net_ref.at[z], net_hbm.at[z], net_sem.at[z]).wait()


def per_device(
    fluid_velocity, porosity, particle_velocity, drag_coef, send_rows, counts, recv_cell
):
    n_slab = lax.axis_size("slab")
    n_brick = lax.axis_size("brick")
    devices = n_slab * n_brick
    cap = send_rows.shape[0] // devices
    vmem = pl.BlockSpec(memory_space=pltpu.VMEM)
    smem = pl.BlockSpec(memory_space=pltpu.SMEM)
    params = pltpu.CompilerParams(vmem_limit_bytes=32 << 20)
    square = jax.ShapeDtypeStruct((256, 128), F32)
    hbm = pl.BlockSpec(memory_space=pl.ANY)
    staged, others, starts, key, p0, p1, p2, drag = pl.pallas_call(
        functools.partial(exchange_kernel, cap=cap, group=16),
        out_shape=(
            jax.ShapeDtypeStruct((8, 96, 512), F32),
            jax.ShapeDtypeStruct((8, 40, 512), F32),
            jax.ShapeDtypeStruct((33,), I32),
            jax.ShapeDtypeStruct((256, 128), I32),
            square, square, square, square,
        ),
        in_specs=[smem] + [hbm] * 6,
        out_specs=(hbm, vmem, smem) + (vmem,) * 5,
        scratch_shapes=[
            pltpu.VMEM((3, 16384), F32),
            pltpu.VMEM((128, 128), F32),
            pltpu.VMEM((256, 128), I32),
            pltpu.VMEM((3, 256, 512), F32),
            pltpu.VMEM((256, 512), F32),
            pltpu.VMEM((256, 128), I32),
            pltpu.VMEM((3, 128, 128), F32),
            pltpu.VMEM((8, 136, 512), F32),
            pltpu.VMEM((768, 256), BF16),
            pltpu.VMEM((devices, 8, 128), F32),
            pltpu.VMEM((devices, 8, 128), F32),
            pltpu.SemaphoreType.DMA((6,)),
            pltpu.SemaphoreType.DMA,
            pltpu.SemaphoreType.DMA,
            pltpu.SemaphoreType.DMA,
            pltpu.SemaphoreType.DMA((8,)),
            pltpu.SemaphoreType.DMA((8,)),
        ],
        compiler_params=pltpu.CompilerParams(
            vmem_limit_bytes=60 << 20, collective_id=0, has_side_effects=True
        ),
        name="exchange",
    )(
        counts,
        particle_velocity,
        drag_coef.reshape(128, 128),
        send_rows.reshape(256, 128),
        fluid_velocity.reshape(3, 256, 512),
        porosity.reshape(256, 512),
        recv_cell.reshape(256, 128),
    )

    bricks = lax.all_to_all(staged, "brick", split_axis=0, concat_axis=0, tiled=True)
    ordered = lax.sort(
        [part.reshape(-1) for part in (key, drag, p0, p1, p2)], num_keys=1, is_stable=False
    )
    top, bottom = [jnp.concatenate([bricks[z], others[z, :32]]) for z in (7, 0)]
    below = lax.ppermute(top, "slab", [(i, i + 1) for i in range(n_slab - 1)])
    above = lax.ppermute(bottom, "slab", [(i + 1, i) for i in range(n_slab - 1)])
    f0, f1, f2, slot, summed = pl.pallas_call(
        functools.partial(brick_kernel, width=256, group=32),
        out_shape=(
            square, square, square,
            jax.ShapeDtypeStruct((256, 128), I32),
            jax.ShapeDtypeStruct((8, 3, 32, 512), F32),
        ),
        in_specs=[smem] + [vmem] * 7,
        out_specs=(vmem,) * 5,
        scratch_shapes=[pltpu.VMEM((32, 192, 256), BF16), pltpu.VMEM((32, 144, 256), F32)],
        compiler_params=params,
        cost_estimate=pl.CostEstimate(flops=30_000_000_000, bytes_accessed=6_000_000, transcendentals=0),
        name="brick_forces",
    )(starts, *[part.reshape(256, 128) for part in ordered], bricks, others)
    net = pl.pallas_call(
        viscous_kernel,
        out_shape=jax.ShapeDtypeStruct((8, 3, 32, 512), F32),
        in_specs=[vmem] * 5,
        out_specs=hbm,
        scratch_shapes=[
            pltpu.VMEM((8, 3, 32, 512), F32),
            pltpu.VMEM((10, 4, 48, 512), F32),
            pltpu.SemaphoreType.DMA((8,)),
        ],
        compiler_params=params,
        name="viscous",
    )(bricks, others, below, above, summed)

    slot, f0, f1, f2, net = lax.optimization_barrier((slot, f0, f1, f2, net))
    returned = lax.all_to_all(net, "brick", split_axis=0, concat_axis=0, tiled=True)
    back = lax.sort([part.reshape(-1) for part in (slot, f0, f1, f2)], num_keys=1, is_stable=False)
    slot_force = jnp.stack(back[1:])
    returned = jnp.swapaxes(returned, 0, 1).reshape(fluid_velocity.shape)
    new_velocity = fluid_velocity + time_step * returned / porosity
    return (new_velocity, slot_force)


def solution(mesh):
    placed = (
        P(None, ("slab", "brick"), None, None),
        P(("slab", "brick"), None, None),
        P(None, ("slab", "brick")),
        P(("slab", "brick")),
        P(("slab", "brick")),
        P(("slab", "brick")),
        P(("slab", "brick")),
    )
    return jax.shard_map(
        per_device,
        mesh=mesh,
        in_specs=placed,
        out_specs=(P(None, ("slab", "brick"), None, None), P(None, ("slab", "brick"))),
        check_vma=False,
    )
```

```python
import functools

import jax
import jax.numpy as jnp
from jax import lax
from jax.experimental import pallas as pl
from jax.experimental.pallas import tpu as pltpu
from jax.sharding import PartitionSpec as P

time_step = 0.05
F32, BF16, I32 = jnp.float32, jnp.bfloat16, jnp.int32
LAST = 2**31 - 1


def split3(x):
    high = x.astype(BF16)
    rest = x - high.astype(F32)
    mid = rest.astype(BF16)
    low = (rest - mid.astype(F32)).astype(BF16)
    return high, mid, low


def exchange_kernel(
    counts_ref, pv_hbm, coef_hbm, rows_hbm, u_hbm, frac_hbm, cell_hbm,
    stage_hbm, rest_ref, starts_ref, key_ref, p0_ref, p1_ref, p2_ref, drag_ref,
    pv_ref, coef_ref, rows_ref, u_ref, frac_ref, cell_ref, particles,
    stage, table, packed, arrived_ref, load_sem, stage_sem, part_send, part_recv, rest_send, rest_recv,
    *, cap, group,
):
    pairs = (
        (pv_hbm, pv_ref), (coef_hbm, coef_ref), (rows_hbm, rows_ref), (u_hbm, u_ref), (frac_hbm, frac_ref),
        (cell_hbm, cell_ref),
    )
    loads = [pltpu.make_async_copy(source, target, load_sem.at[i]) for i, (source, target) in enumerate(pairs)]
    for load in loads:
        load.start()
    n_slab, n_brick = lax.axis_size("slab"), lax.axis_size("brick")
    devices = n_slab * n_brick
    slab, brick = lax.axis_index("slab"), lax.axis_index("brick")
    me = slab * n_brick + brick
    mesh_id = pl.DeviceIdType.MESH

    def coords(d):
        return (d // n_brick, d % n_brick)

    barrier = pltpu.get_barrier_semaphore()

    def greet(j):
        pl.semaphore_signal(barrier, inc=1, device_id=coords((me + j) % devices), device_id_type=mesh_id)

    def greet_some(i, carry):
        for j in range(6):
            greet(6 * i + j + 1)
        return carry

    lax.fori_loop(0, 21, greet_some, 0)
    greet(127)

    for load in loads[:3]:
        load.wait()
    for l in range(128):
        part = pv_ref[:, l * 128 : (l + 1) * 128]
        for c in range(3):
            particles[c, l : l + 1, :] = part[c : c + 1]
    for c in range(4):
        whole = coef_ref[...] if c == 3 else particles[c]
        halves = jnp.concatenate([whole[:64], whole[64:]], axis=1)
        for p, piece in enumerate(split3(halves)):
            table[p * 256 + c * 64 : p * 256 + (c + 1) * 64, :] = piece

    r_iota = lax.broadcasted_iota(I32, (256, cap), 0).astype(F32).astype(BF16)
    one, zero = jnp.ones((), BF16), jnp.zeros((), BF16)
    l_iota = lax.broadcasted_iota(I32, (64, cap), 0)
    k_iota = lax.broadcasted_iota(I32, (1, cap), 1)

    def pick(to):
        onehots, planes, gots, picked = [], [], [], []
        for t in to:
            row = jnp.concatenate([rows_ref[pl.ds(2 * t, 1), :], rows_ref[pl.ds(2 * t + 1, 1), :]], axis=1)
            r = (row & 127) + ((row >> 13) << 7)
            onehots.append(jnp.where(r_iota == r.astype(F32).astype(BF16), one, zero))
            planes.append((row >> 7) & 63)
        for onehot in onehots:
            gots.append(jnp.dot(table[...], onehot, preferred_element_type=F32))
        slot = (me * cap + k_iota).astype(F32)
        for t, got, l in zip(to, gots, planes):
            got = got[:256] + (got[256:512] + got[512:])
            mask = l_iota == l
            live = k_iota < counts_ref[t]
            values = []
            for c in range(4):
                value = jnp.sum(jnp.where(mask, got[c * 64 : (c + 1) * 64], 0.0), axis=0, keepdims=True)
                if c == 0:
                    value = jnp.where(live, value, slot)
                if c == 3:
                    value = jnp.where(live, value, 0.0)
                values += [value[:, :128], value[:, 128:]]
            picked.append(jnp.concatenate(values, axis=0))
        return picked

    def parcel(t):
        return pltpu.make_async_remote_copy(
            src_ref=packed.at[t], dst_ref=arrived_ref.at[me], send_sem=part_send, recv_sem=part_recv,
            device_id=coords(t), device_id_type=mesh_id,
        )

    def other(j):
        to = (brick + j) % n_brick
        return pltpu.make_async_remote_copy(
            src_ref=stage.at[to, pl.ds(96, 40)], dst_ref=rest_ref.at[brick], send_sem=rest_send.at[to],
            recv_sem=rest_recv.at[brick], device_id=(slab, to), device_id_type=mesh_id,
        )

    def fill(i, carry):
        to = [(me + 1 + i * group + j) % devices for j in range(group)]
        for t, value in zip(to, pick(to)):
            packed[t] = value
        return carry

    def send(i, carry):
        for j in range(group):
            parcel((me + 1 + i * group + j) % devices).start()
        return carry

    def some(i, carry):
        return send(i, fill(i, carry))

    fill(0, 0)
    for load in loads[3:]:
        load.wait()
    for c in range(4):
        for b in range(8):
            field = frac_ref[b * 32 : (b + 1) * 32, :] if c == 3 else u_ref[c, b * 32 : (b + 1) * 32, :]
            stage[b, c * 32 : (c + 1) * 32, :] = field
            if b < 7:
                stage[b + 1, 128 + c : 129 + c, :] = field[31:32]
            if b > 0:
                stage[b - 1, 132 + c : 133 + c, :] = field[0:1]
        stage[0, 128 + c : 129 + c, :] = jnp.zeros((1, 512), F32)
        stage[7, 132 + c : 133 + c, :] = jnp.zeros((1, 512), F32)
    saved = pltpu.make_async_copy(stage.at[:, pl.ds(0, 96)], stage_hbm, stage_sem)
    saved.start()
    rest_ref[brick] = stage[brick, 96:136]
    pl.semaphore_wait(barrier, devices - 1)
    for j in range(1, 8):
        other(j).start()
    send(0, 0)
    lax.fori_loop(1, devices // group - 1, some, 0)
    to = [(me + 1 + devices - group + j) % devices for j in range(group)]
    picked = pick(to)
    for t, value in zip(to[:-1], picked):
        packed[t] = value
    arrived_ref[me] = picked[-1]
    for t in to[:-1]:
        parcel(t).start()

    tiles = cell_ref.shape[0] // 8
    place = lax.broadcasted_iota(I32, (8, 128), 0) * 128 + lax.broadcasted_iota(I32, (8, 128), 1)

    def early(j, carry):
        rows = pl.ds(pl.multiple_of(8 * j, 8), 8)
        cell = cell_ref[rows, :]
        key_ref[rows, :] = (((cell >> 12) - 16) << 27) + ((j * 1024 + place) << 12) + (cell & 4095)
        return carry

    lax.fori_loop(0, tiles, early, 0, unroll=4)
    rest = pltpu.make_async_remote_copy(
        src_ref=packed.at[pl.ds(0, devices - 1)], dst_ref=arrived_ref.at[pl.ds(0, devices - 1)],
        send_sem=part_send, recv_sem=part_recv, device_id=coords((me + 1) % devices), device_id_type=mesh_id,
    )
    rest.wait_send()
    rest.wait_recv()
    saved.wait()
    for j in range(1, 8):
        other(j).wait_send()
        source = (brick + j) % n_brick
        pltpu.make_async_remote_copy(
            src_ref=stage.at[source, pl.ds(96, 40)], dst_ref=rest_ref.at[source], send_sem=rest_send.at[source],
            recv_sem=rest_recv.at[source], device_id=(slab, source), device_id_type=mesh_id,
        ).wait_recv()

    def keys(j, sums):
        parts = [arrived_ref[4 * j + i] for i in range(4)]
        rows = pl.ds(pl.multiple_of(8 * j, 8), 8)
        for c, ref in enumerate((p0_ref, p1_ref, p2_ref, drag_ref)):
            value = jnp.concatenate([part[2 * c : 2 * c + 2] for part in parts], axis=0)
            ref[rows, :] = value
        live = value != 0.0
        key = key_ref[rows, :]
        key_ref[rows, :] = jnp.where(live, key, LAST)
        block = jnp.where(live, (key >> 27) + 16, 32)
        return tuple(s + jnp.where(block < b + 1, 1, 0) for b, s in enumerate(sums))

    sums = lax.fori_loop(0, tiles, keys, tuple(jnp.zeros((8, 128), I32) for _ in range(32)))
    tail = (cell_ref[tiles * 8 - 8 :, :] == 131071) & (drag_ref[tiles * 8 - 8 :, :] != 0.0) & (place == 1023)
    starts_ref[0] = 0
    for b in range(32):
        starts_ref[b + 1] = jnp.sum(sums[b])
    starts_ref[32] = jnp.where(jnp.sum(jnp.where(tail, 1, 0)) > 0, tiles * 1024, starts_ref[32])


def brick_kernel(
    starts_ref, key_ref, coef_ref, p0_ref, p1_ref, p2_ref, bricks_ref, rest_ref,
    f0_ref, f1_ref, f2_ref, slot_ref, sum_ref, table, deposit, *, width, group,
):
    rows = key_ref.shape[0]
    n = width // 128
    force_refs = (f0_ref, f1_ref, f2_ref)
    for ref in force_refs:
        ref[...] = jnp.zeros_like(ref)
    slot_ref[...] = jnp.where(coef_ref[...] != 0.0, (key_ref[...] >> 12) & 32767, p0_ref[...].astype(I32))

    r_iota = lax.broadcasted_iota(I32, (256, width), 0)
    l_iota = lax.broadcasted_iota(I32, (16, width), 0)
    r_iota = r_iota.astype(F32).astype(BF16)
    l_bf = l_iota.astype(F32).astype(BF16)
    p_iota = lax.broadcasted_iota(I32, (1, width), 1)
    one, zero = jnp.ones((), BF16), jnp.zeros((), BF16)

    def blocks(g, carry):
        bs = [g * group + i for i in range(group)]
        row0s, counts = [], []
        for i, b in enumerate(bs):
            z, q = b // 4, b % 4
            x8 = pl.multiple_of(q * 8, 8)
            for c in range(4):
                ref, at = (rest_ref, x8) if c == 3 else (bricks_ref, pl.multiple_of(c * 32 + x8, 8))
                centre = ref[z, pl.ds(at, 8), :]
                for p, piece in enumerate(split3(centre)):
                    at = p * 64 + c * 16
                    table[i, at : at + 16, :] = jnp.concatenate([piece[:, :256], piece[:, 256:]], axis=0)
            deposit[i] = jnp.zeros(deposit.shape[1:], F32)
            first, end = starts_ref[b], starts_ref[b + 1]
            row0 = first // 128
            row0s.append(row0)
            counts.append(jnp.where(end > first, (end - row0 * 128 + width - 1) // width, 0))
        windows = counts[0]
        for c in counts[1:]:
            windows = jnp.maximum(windows, c)

        def window(w, inner):
            ats, oh, valids, ls, gots = [], [], [], [], []

            def line(ref, at):
                return jnp.concatenate([ref[pl.ds(at + k, 1), :] for k in range(n)], axis=1)

            for i, b in enumerate(bs):
                row = row0s[i] + w * n
                at = jnp.minimum(row, rows - n)
                key = line(key_ref, at)
                valid = ((key >> 27) + 16 == b) & (p_iota >= (row - at) * 128)
                r = jnp.where(valid, key & 255, -1)
                l = ((key >> 9) & 7) + ((key >> 8) & 1) * 8
                ats.append(at)
                oh.append(jnp.where(r_iota == r.astype(F32).astype(BF16), one, zero))
                valids.append(valid)
                ls.append(l)
            for i in range(group):
                gots.append(jnp.dot(table[i], oh[i], preferred_element_type=F32))
            spreads = []
            forces = []
            for i in range(group):
                got = gots[i]
                got = got[:64] + (got[64:128] + got[128:])
                mask = l_iota == ls[i]
                u = [
                    jnp.sum(jnp.where(mask, got[c * 16 : (c + 1) * 16], 0.0), axis=0, keepdims=True) for c in range(4)
                ]
                frac = jnp.where(valids[i], u[3], 1.0)
                beta = line(coef_ref, ats[i]) * (1.0 - frac) / (frac * frac)
                fs = [
                    jnp.where(valids[i], beta * (u[c] - line(ref, ats[i])), 0.0)
                    for c, ref in enumerate((p0_ref, p1_ref, p2_ref))
                ]
                forces.append(fs)
                split = [split3(f) for f in fs]
                low_mask = l_bf == ls[i].astype(F32).astype(BF16)
                spreads.append(
                    jnp.concatenate(
                        [jnp.where(low_mask, split[c][p], zero) for p in range(3) for c in range(3)], axis=0
                    )
                )
            for i in range(group):
                deposit[i] += lax.dot_general(
                    spreads[i], oh[i], (((1,), (1,)), ((), ())), preferred_element_type=F32
                )
            for i in range(group):
                for c in range(3):
                    for k in range(n):
                        force_refs[c][pl.ds(ats[i] + k, 1), :] += forces[i][c][:, k * 128 : (k + 1) * 128]
            return inner

        lax.fori_loop(0, windows, window, 0)

        for i, b in enumerate(bs):
            z, q = b // 4, b % 4
            x8 = pl.multiple_of(q * 8, 8)
            summed = deposit[i, 0:48, :] + (deposit[i, 48:96, :] + deposit[i, 96:144, :])
            for c in range(3):
                left, right = summed[c * 16 : c * 16 + 8], summed[c * 16 + 8 : c * 16 + 16]
                sum_ref[z, c, pl.ds(x8, 8), :] = jnp.concatenate([left, right], axis=1)
        return carry

    lax.fori_loop(0, 32 // group, blocks, 0)


def viscous_kernel(bricks_ref, rest_ref, below_ref, above_ref, sum_ref, net_hbm, net_ref, padded, net_sem):
    for c in range(4):
        own = slice(c * 32, (c + 1) * 32)
        for z in range(8):
            padded[z + 1, c, 8:40, :] = rest_ref[z, 0:32, :] if c == 3 else bricks_ref[z, own, :]
            padded[z + 1, c, 7:8, :] = rest_ref[z, 32 + c : 33 + c, :]
            padded[z + 1, c, 40:41, :] = rest_ref[z, 36 + c : 37 + c, :]
        padded[0, c, 8:40, :] = below_ref[own, :]
        padded[9, c, 8:40, :] = above_ref[own, :]
    y_iota = lax.broadcasted_iota(I32, (8, 512), 1)

    def plane(z, carry):
        for x8 in range(0, 32, 8):
            tall = [padded[z + 1, c, x8 : x8 + 24, :] for c in range(4)]
            below = [padded[z, c, x8 + 8 : x8 + 16, :] for c in range(4)]
            above = [padded[z + 2, c, x8 + 8 : x8 + 16, :] for c in range(4)]
            centre = [t[8:16] for t in tall]
            sides = [above, below, [t[9:17] for t in tall], [t[7:15] for t in tall]]
            sides.append([jnp.where(y_iota == 511, 0.0, pltpu.roll(t, 511, 1)) for t in centre])
            sides.append([jnp.where(y_iota == 0, 0.0, pltpu.roll(t, 1, 1)) for t in centre])
            total = [jnp.zeros((8, 512), F32) for _ in range(3)]
            for side in sides:
                weight = 0.5 * (centre[3] + side[3])
                for c in range(3):
                    total[c] = total[c] + weight * (side[c] - centre[c])
            for c in range(3):
                net_ref[z, c, x8 : x8 + 8, :] = total[c] - sum_ref[z, c, x8 : x8 + 8, :]
        pltpu.make_async_copy(net_ref.at[z], net_hbm.at[z], net_sem.at[z]).start()
        return carry

    lax.fori_loop(0, 8, plane, 0)
    for z in range(8):
        pltpu.make_async_copy(net_ref.at[z], net_hbm.at[z], net_sem.at[z]).wait()


def per_device(
    fluid_velocity, porosity, particle_velocity, drag_coef, send_rows, counts, recv_cell
):
    n_slab = lax.axis_size("slab")
    n_brick = lax.axis_size("brick")
    devices = n_slab * n_brick
    cap = send_rows.shape[0] // devices
    vmem = pl.BlockSpec(memory_space=pltpu.VMEM)
    smem = pl.BlockSpec(memory_space=pltpu.SMEM)
    params = pltpu.CompilerParams(vmem_limit_bytes=32 << 20)
    square = jax.ShapeDtypeStruct((256, 128), F32)
    hbm = pl.BlockSpec(memory_space=pl.ANY)
    staged, others, starts, key, p0, p1, p2, drag = pl.pallas_call(
        functools.partial(exchange_kernel, cap=cap, group=32),
        out_shape=(
            jax.ShapeDtypeStruct((8, 96, 512), F32),
            jax.ShapeDtypeStruct((8, 40, 512), F32),
            jax.ShapeDtypeStruct((33,), I32),
            jax.ShapeDtypeStruct((256, 128), I32),
            square, square, square, square,
        ),
        in_specs=[smem] + [hbm] * 6,
        out_specs=(hbm, vmem, smem) + (vmem,) * 5,
        scratch_shapes=[
            pltpu.VMEM((3, 16384), F32),
            pltpu.VMEM((128, 128), F32),
            pltpu.VMEM((256, 128), I32),
            pltpu.VMEM((3, 256, 512), F32),
            pltpu.VMEM((256, 512), F32),
            pltpu.VMEM((256, 128), I32),
            pltpu.VMEM((3, 128, 128), F32),
            pltpu.VMEM((8, 136, 512), F32),
            pltpu.VMEM((768, 256), BF16),
            pltpu.VMEM((devices, 8, 128), F32),
            pltpu.VMEM((devices, 8, 128), F32),
            pltpu.SemaphoreType.DMA((6,)),
            pltpu.SemaphoreType.DMA,
            pltpu.SemaphoreType.DMA,
            pltpu.SemaphoreType.DMA,
            pltpu.SemaphoreType.DMA((8,)),
            pltpu.SemaphoreType.DMA((8,)),
        ],
        compiler_params=pltpu.CompilerParams(
            vmem_limit_bytes=60 << 20, collective_id=0, has_side_effects=True
        ),
        name="exchange",
    )(
        counts,
        particle_velocity,
        drag_coef.reshape(128, 128),
        send_rows.reshape(256, 128),
        fluid_velocity.reshape(3, 256, 512),
        porosity.reshape(256, 512),
        recv_cell.reshape(256, 128),
    )

    bricks = lax.all_to_all(staged, "brick", split_axis=0, concat_axis=0, tiled=True)
    ordered = lax.sort(
        [part.reshape(-1) for part in (key, drag, p0, p1, p2)], num_keys=1, is_stable=False
    )
    top, bottom = [jnp.concatenate([bricks[z], others[z, :32]]) for z in (7, 0)]
    below = lax.ppermute(top, "slab", [(i, i + 1) for i in range(n_slab - 1)])
    above = lax.ppermute(bottom, "slab", [(i + 1, i) for i in range(n_slab - 1)])
    f0, f1, f2, slot, summed = pl.pallas_call(
        functools.partial(brick_kernel, width=256, group=32),
        out_shape=(
            square, square, square,
            jax.ShapeDtypeStruct((256, 128), I32),
            jax.ShapeDtypeStruct((8, 3, 32, 512), F32),
        ),
        in_specs=[smem] + [vmem] * 7,
        out_specs=(vmem,) * 5,
        scratch_shapes=[pltpu.VMEM((32, 192, 256), BF16), pltpu.VMEM((32, 144, 256), F32)],
        compiler_params=params,
        cost_estimate=pl.CostEstimate(flops=30_000_000_000, bytes_accessed=6_000_000, transcendentals=0),
        name="brick_forces",
    )(starts, *[part.reshape(256, 128) for part in ordered], bricks, others)
    net = pl.pallas_call(
        viscous_kernel,
        out_shape=jax.ShapeDtypeStruct((8, 3, 32, 512), F32),
        in_specs=[vmem] * 5,
        out_specs=hbm,
        scratch_shapes=[
            pltpu.VMEM((8, 3, 32, 512), F32),
            pltpu.VMEM((10, 4, 48, 512), F32),
            pltpu.SemaphoreType.DMA((8,)),
        ],
        compiler_params=params,
        name="viscous",
    )(bricks, others, below, above, summed)

    slot, f0, f1, f2, net = lax.optimization_barrier((slot, f0, f1, f2, net))
    returned = lax.all_to_all(net, "brick", split_axis=0, concat_axis=0, tiled=True)
    back = lax.sort([part.reshape(-1) for part in (slot, f0, f1, f2)], num_keys=1, is_stable=False)
    slot_force = jnp.stack(back[1:])
    returned = jnp.swapaxes(returned, 0, 1).reshape(fluid_velocity.shape)
    new_velocity = fluid_velocity + time_step * returned / porosity
    return (new_velocity, slot_force)


def solution(mesh):
    placed = (
        P(None, ("slab", "brick"), None, None),
        P(("slab", "brick"), None, None),
        P(None, ("slab", "brick")),
        P(("slab", "brick")),
        P(("slab", "brick")),
        P(("slab", "brick")),
        P(("slab", "brick")),
    )
    return jax.shard_map(
        per_device,
        mesh=mesh,
        in_specs=placed,
        out_specs=(P(None, ("slab", "brick"), None, None), P(None, ("slab", "brick"))),
        check_vma=False,
    )
```
